32 devices in a mesh: batch: 8 (over y, x, core), frame: 4 (over z).
Axes of the slice: x: 2, y: 2, z: 4, core: 2. Of those that a mesh axis runs over, the one named last changes fastest.
Arguments:
- tokens: bfloat16 [4, 6304, 768], P('frame', 'batch'), may hold values from -6 to 6
- size_tag: int32 [8], P('batch'), may hold values from 196 to 784, as said below
- cotangent: bfloat16 [4, 6304, 768], P('frame', 'batch'), may hold values from -6 to 6
- time_project: bfloat16 [768, 2304], P('batch'), may hold values from -0.21875 to 0.21875
- time_output: bfloat16 [768, 768], P('batch'), may hold values from -0.4375 to 0.4375
- time_vector: bfloat16 [5, 768], P(None, 'batch'), may hold values from -1.25 to 1.4
- space_project: bfloat16 [768, 2304], P('batch'), may hold values from -0.21875 to 0.21875
- space_output: bfloat16 [768, 768], P('batch'), may hold values from -1.25 to 1.25
- space_vector: bfloat16 [5, 768], P(None, 'batch'), may hold values from -1.25 to 1.4
- feed_inner: bfloat16 [768, 3072], P('batch'), may hold values from -0.21875 to 0.21875
- feed_bias: bfloat16 [3072], P('batch'), may hold values from -1.796875 to 1.796875
- feed_outer: bfloat16 [3072, 768], P('batch'), may hold values from -0.109375 to 0.109375
- feed_vector: bfloat16 [3, 768], P(None, 'batch'), may hold values from -1.25 to 1.4
Outputs:
- block_out: bfloat16 [4, 6304, 768], P('frame', 'batch')
- grad_tokens: float32 [4, 6304, 768], P('frame', 'batch')
- grad_time_project: float32 [768, 2304], replicated
- grad_time_output: float32 [768, 768], replicated
- grad_time_vector: float32 [5, 768], replicated
- grad_space_project: float32 [768, 2304], replicated
- grad_space_output: float32 [768, 768], replicated
- grad_space_vector: float32 [5, 768], replicated
- grad_feed_inner: float32 [768, 3072], replicated
- grad_feed_bias: float32 [3072], replicated
- grad_feed_outer: float32 [3072, 768], replicated
- grad_feed_vector: float32 [3, 768], replicated
The draws below stay inside these ranges and needn't reach their ends.
Inputs may be any that keep to these rules, and one draw needn't show every extreme that they name: `size_tag`: A batch index with tag 196 holds 4 clips of 196 patches a frame, one with tag 4 * 196 holds 1 clips of 784; both tags occur in every draw.
All inputs are finite; a program needn't handle non-finite values.
Results may differ from the reference program's by a relative error of at most 0.019.
Values may be sent and summed in bfloat16 or wider, within the bound.
No kernel may reach another device: no remote copies, remote signals or barrier semaphores. Data moves between devices by JAX's collectives and lax.ppermute only.
A program may use at most 384 MiB of HBM per device.

```python
from functools import partial
import jax
import jax.numpy as jnp
from jax import lax

D = 768
HEADS = 12
FF = 3072
PATCH = 196
UNITS = 4
HEAD_DIM = 64
FRAMES = 4
PATCHES = 784
ROWS_DEV = 788
ROWS = 6304
N_BATCH = 8


def vector_rows(key, row_count):
    gain_key, other_key = jax.random.split(key)
    gains = jax.random.uniform(gain_key, (1, D), jnp.float32, 0.6, 1.4)
    others = 0.4 * jnp.clip(jax.random.normal(other_key, (row_count - 1, D), jnp.float32), -3.0, 3.0)
    return jnp.concatenate([gains, others], axis=0).astype(jnp.bfloat16)


def draw_time_vector(key, part):
    key = jax.random.fold_in(key, 11)
    return vector_rows(key, 5)


def draw_space_vector(key, part):
    key = jax.random.fold_in(key, 23)
    return vector_rows(key, 5)


def draw_feed_vector(key, part):
    key = jax.random.fold_in(key, 37)
    return vector_rows(key, 3)


def draw_size_tag(key, part):
    key = jax.random.fold_in(key, 53)
    count_key, order_key = jax.random.split(key)
    large_count = jax.random.randint(count_key, (), 1, N_BATCH)
    order = jax.random.permutation(order_key, N_BATCH)
    return jnp.where(order < large_count, 4 * PATCH, PATCH).astype(jnp.int32)


def shard_levels(rng, extent, cuts, smallest, largest):
    gain, own = 1.0, jax.random.fold_in(rng, 6)
    for dim, parts in cuts:
        heights = jnp.exp(jax.random.uniform(jax.random.fold_in(own, dim), (parts,), jnp.float32, smallest / len(cuts), largest / len(cuts)))
        gain = gain * jnp.repeat(heights, extent[dim] // parts).reshape([-1 if axis == dim else 1 for axis in range(len(extent))])
    return gain


def normal_values(key, dims, width, reach, cuts=(), kind=jnp.bfloat16):
    values = width * jax.random.normal(key, dims, jnp.float32)
    if cuts:
        values = values * shard_levels(key, dims, cuts, -0.22, 0.18)
    return jnp.clip(values, -reach, reach).astype(kind)


def setup_inputs(seed: int = 0) -> dict:
    streams_of = jax.random.split(jax.random.key(seed), 14)
    return {
        "tokens": normal_values(streams_of[0], (FRAMES, ROWS, D), 1.0, 6.0, ((0, 4), (1, 8))),
        "size_tag": draw_size_tag(jax.random.fold_in(streams_of[13], 71), 0),
        "cotangent": normal_values(streams_of[2], (FRAMES, ROWS, D), 1.0, 6.0, ((0, 4), (1, 8))),
        "time_project": normal_values(streams_of[3], (D, 3 * D), D ** -0.5, 0.21875, ((0, 8),)),
        "time_output": normal_values(streams_of[4], (D, D), (D // 4) ** -0.5, 0.4375, ((0, 8),)),
        "time_vector": draw_time_vector(jax.random.fold_in(streams_of[13], 71), 0),
        "space_project": normal_values(streams_of[6], (D, 3 * D), D ** -0.5, 0.21875, ((0, 8),)),
        "space_output": normal_values(streams_of[7], (D, D), (D // 32) ** -0.5, 1.25, ((0, 8),)),
        "space_vector": draw_space_vector(jax.random.fold_in(streams_of[13], 71), 0),
        "feed_inner": normal_values(streams_of[9], (D, FF), D ** -0.5, 0.21875, ((0, 8),)),
        "feed_bias": normal_values(streams_of[10], (FF,), 0.3, 1.796875, ((0, 8),)),
        "feed_outer": normal_values(streams_of[11], (FF, D), FF ** -0.5, 0.109375, ((0, 8),)),
        "feed_vector": draw_feed_vector(jax.random.fold_in(streams_of[13], 71), 0),
    }


@jax.custom_vjp
def low(v):
    return lax.optimization_barrier(v.astype(jnp.bfloat16)).astype(jnp.float32)

@jax.custom_vjp
def low_back(v):
    return v

def low_keep(v):
    return (low(v), None)

def low_pass(kept, grad):
    return (grad,)

def back_keep(v):
    return (v, None)

def back_low(kept, grad):
    return (low(grad),)
low.defvjp(low_keep, low_pass)
low_back.defvjp(back_keep, back_low)

def both_round(values):
    return low_back(low(values))

def norm_rows(values, norm_gain, norm_shift):
    average = lax.optimization_barrier(jnp.mean(values, axis=-1, keepdims=True))
    centered = values - average
    variance = lax.optimization_barrier(jnp.mean(centered * centered, axis=-1, keepdims=True))
    return centered * lax.rsqrt(variance + 1e-06) * norm_gain + norm_shift

def product(operand, partner):
    return jnp.dot(operand, partner, precision=lax.Precision.HIGHEST, preferred_element_type=jnp.float32)

def projections(normed, weight, vector):
    joined = product(low(normed), weight)
    queries = both_round(joined[..., :D] + vector[2])
    key_rows = both_round(joined[..., D:2 * D])
    values = both_round(joined[..., 2 * D:] + vector[3])
    return (queries, key_rows, values)

def split_heads(array):
    return array.reshape(array.shape[:-1] + (HEADS, HEAD_DIM))

def group_forward(params, group_tokens, clip_tag):
    time_project, time_output, time_vector, space_project, space_output, space_vector, feed_inner, feed_bias, feed_outer, feed_vector = params
    highest = lax.Precision.HIGHEST
    scaling = HEAD_DIM ** (-0.5)
    patches = group_tokens[:, :PATCHES]
    normed = norm_rows(patches, time_vector[0], time_vector[1])
    queries, key_rows, values = projections(normed, time_project, time_vector)
    scores = jnp.einsum('fphd,gphd->phfg', split_heads(queries), split_heads(key_rows), precision=highest) * scaling
    attention = low(jax.nn.softmax(low_back(scores), axis=-1))
    mixture = jnp.einsum('phfg,gphd->fphd', attention, split_heads(values), precision=highest)
    mixture = mixture.reshape(FRAMES, PATCHES, D)
    branch = low_back(product(both_round(mixture), time_output) + time_vector[4])
    after_time = jnp.concatenate([patches + branch, group_tokens[:, PATCHES:]], axis=1)
    normed = norm_rows(after_time, space_vector[0], space_vector[1])
    queries, key_rows, values = projections(normed, space_project, space_vector)
    clip_number = jnp.concatenate([jnp.arange(PATCHES, dtype=jnp.int32) // clip_tag, jnp.arange(UNITS, dtype=jnp.int32)])
    linked = clip_number[:, None] == clip_number[None, :]
    scores = jnp.einsum('fqhd,fkhd->fhqk', split_heads(queries), split_heads(key_rows), precision=highest) * scaling
    scores = jnp.where(linked, low_back(scores), -1e+30)
    attention = low(jax.nn.softmax(scores, axis=-1))
    mixture = jnp.einsum('fhqk,fkhd->fqhd', attention, split_heads(values), precision=highest)
    mixture = mixture.reshape(FRAMES, ROWS_DEV, D)
    after_space = after_time + low_back(product(both_round(mixture), space_output) + space_vector[4])
    normed = norm_rows(after_space, feed_vector[0], feed_vector[1])
    hidden = low_back(product(low(normed), feed_inner) + feed_bias)
    active = low(jax.nn.gelu(hidden, approximate=False))
    return after_space + low_back(product(active, feed_outer) + feed_vector[2])

def forward(params, tokens, size_tag):
    grouped = tokens.reshape(FRAMES, N_BATCH, ROWS_DEV, D).transpose(1, 0, 2, 3)
    grouped_step = jax.checkpoint(partial(group_forward, params))

    def apply_group(paired):
        return grouped_step(paired[0], paired[1])
    result = lax.map(apply_group, (grouped, size_tag))
    return result.transpose(1, 0, 2, 3).reshape(FRAMES, ROWS, D)

def reference(tokens, size_tag, cotangent, time_project, time_output, time_vector, space_project, space_output, space_vector, feed_inner, feed_bias, feed_outer, feed_vector):
    params = (time_project.astype(jnp.float32), time_output.astype(jnp.float32), time_vector.astype(jnp.float32), space_project.astype(jnp.float32), space_output.astype(jnp.float32), space_vector.astype(jnp.float32), feed_inner.astype(jnp.float32), feed_bias.astype(jnp.float32), feed_outer.astype(jnp.float32), feed_vector.astype(jnp.float32))

    def whole_forward(token_rows, *weights):
        return forward(weights, token_rows, size_tag)
    output, pullback = jax.vjp(whole_forward, tokens.astype(jnp.float32), *params)
    gradients = pullback(cotangent.astype(jnp.float32))
    return (output.astype(jnp.bfloat16), gradients[0], gradients[1], gradients[2], gradients[3], gradients[4], gradients[5], gradients[6], gradients[7], gradients[8], gradients[9], gradients[10])
```

```python
import jax
import jax.numpy as jnp
from jax import lax
from jax.sharding import PartitionSpec as P

HEADS = 12
UNITS = 4
PATCHES = 784


def norm_rows(values, norm_gain, norm_shift):
    average = jnp.mean(values, axis=-1, keepdims=True)
    centered = values - average
    variance = jnp.mean(centered * centered, axis=-1, keepdims=True)
    return centered * lax.rsqrt(variance + 1e-06) * norm_gain + norm_shift


def gelu_exact(hidden):
    return jax.nn.gelu(hidden, approximate=False)


def forward_dot(operand, partner):
    return jnp.dot(operand, partner, preferred_element_type=jnp.float32)


def inner_rows(operand, partner):
    return lax.dot_general(
        operand, partner, (((0,), (0,)), ((), ())), preferred_element_type=jnp.float32
    )


def times_back(operand, partner):
    return lax.dot_general(
        operand, partner, (((1,), (1,)), ((), ())), preferred_element_type=jnp.float32
    )


def split_frames(array):
    frame_count, row_count, feature_count = array.shape
    return array.reshape(frame_count, row_count, HEADS, feature_count // HEADS)


def frame_scores(queries, key_rows):
    head_size = queries.shape[2] // HEADS
    scores = jnp.einsum(
        "frhd,grhd->rhfg",
        split_frames(queries),
        split_frames(key_rows),
        preferred_element_type=jnp.float32,
    )
    return scores * head_size ** (-0.5)


def frame_forward(queries, key_rows, values):
    scores = frame_scores(queries, key_rows)
    log_total = jax.nn.logsumexp(scores, axis=-1)
    rounded = jnp.exp(scores - log_total[..., None]).astype(jnp.bfloat16)
    mixture = jnp.einsum(
        "rhfg,grhd->frhd", rounded, split_frames(values), preferred_element_type=jnp.float32
    )
    return (mixture.reshape(queries.shape).astype(jnp.bfloat16), log_total)


def frame_backward(queries, key_rows, values, log_total, grad_mixture):
    head_size = queries.shape[2] // HEADS
    scores = frame_scores(queries, key_rows)
    probability = jnp.exp(scores - log_total[..., None])
    rounded = probability.astype(jnp.bfloat16)
    grad_split = split_frames(grad_mixture)
    grad_weights = jnp.einsum(
        "frhd,grhd->rhfg", grad_split, split_frames(values), preferred_element_type=jnp.float32
    )
    grad_scores = probability * (
        grad_weights - jnp.sum(grad_weights * probability, axis=-1, keepdims=True)
    )
    grad_scores = grad_scores.astype(jnp.bfloat16)
    scaling = head_size ** (-0.5)
    grad_query = (
        jnp.einsum(
            "rhfg,grhd->frhd",
            grad_scores,
            split_frames(key_rows),
            preferred_element_type=jnp.float32,
        )
        * scaling
    )
    grad_keys = (
        jnp.einsum(
            "rhfg,frhd->grhd",
            grad_scores,
            split_frames(queries),
            preferred_element_type=jnp.float32,
        )
        * scaling
    )
    grad_values = jnp.einsum(
        "rhfg,frhd->grhd", rounded, grad_split, preferred_element_type=jnp.float32
    )
    return (
        grad_query.reshape(queries.shape),
        grad_keys.reshape(key_rows.shape),
        grad_values.reshape(values.shape),
    )


def round_up(count, step):
    return -(-count // step) * step


def shift_frames(block, frame_count, shift):
    if shift % frame_count == 0:
        return block
    pairs = [(index, (index + shift) % frame_count) for index in range(frame_count)]
    return lax.ppermute(block, "frame", pairs)


def rows_to_frames(rows, frame_count, frame_index):
    part = rows.shape[0] // frame_count
    slots = []
    for shift in range(frame_count):
        owner = (frame_index + shift) % frame_count
        block = lax.dynamic_slice_in_dim(rows, owner * part, part, 0)
        slots.append(shift_frames(block, frame_count, shift))
    return slots


def frames_to_rows(slots, frame_count, frame_index):
    part = slots[0].shape[0]
    rows = jnp.zeros((part * frame_count, slots[0].shape[1]), slots[0].dtype)
    for shift in range(frame_count):
        owner = (frame_index + shift) % frame_count
        block = shift_frames(slots[shift], frame_count, -shift)
        rows = lax.dynamic_update_slice_in_dim(rows, block, owner * part, 0)
    return rows


def swap_bit(block, axis, size, bit):
    pairs = [(index, index ^ (1 << bit)) for index in range(size)]
    return lax.ppermute(block, axis, pairs)


def halve_sum(block, axis, size, bit, index):
    half = block.shape[0] // 2
    own = (index >> bit) & 1
    sent = lax.dynamic_slice_in_dim(block, (1 - own) * half, half, 0)
    kept = lax.dynamic_slice_in_dim(block, own * half, half, 0)
    arrived = swap_bit(sent, axis, size, bit)
    return (kept.astype(jnp.float32) + arrived.astype(jnp.float32)).astype(jnp.bfloat16)


def double_rows(block, axis, size, bit, index):
    arrived = swap_bit(block, axis, size, bit)
    own = ((index >> bit) & 1) == 1
    return jnp.concatenate(
        [jnp.where(own, arrived, block), jnp.where(own, block, arrived)], axis=0
    )


def sum_everywhere(blocks, sizes, indices):
    batch_size, frame_size = sizes
    batch_index, frame_index = indices
    batch_bits = batch_size.bit_length() - 1
    frame_bits = frame_size.bit_length() - 1
    results = []
    for order, block in enumerate(blocks):
        wide = list(range(1, batch_bits))
        if order % 2:
            wide = wide[::-1]
        stages = [("batch", batch_size, bit, batch_index) for bit in [0] + wide]
        stages += [("frame", frame_size, bit, frame_index) for bit in range(frame_bits)]
        for stage in stages:
            block = halve_sum(block, *stage)
        for stage in stages[::-1]:
            block = double_rows(block, *stage)
        results.append(block)
    return results

def space_scores(queries, key_rows, linked):
    row_count, feature_count = queries.shape
    head_size = feature_count // HEADS
    query_split = queries.reshape(row_count, HEADS, head_size)
    key_split = key_rows.reshape(row_count, HEADS, head_size)
    scores = jnp.einsum(
        "qhd,khd->hqk", query_split, key_split, preferred_element_type=jnp.float32
    ) * head_size ** (-0.5)
    return jnp.where(linked[None], scores, -1e30)


def body(
    tokens,
    size_tag,
    cotangent,
    time_project,
    time_output,
    time_vector,
    space_project,
    space_output,
    space_vector,
    feed_inner,
    feed_bias,
    feed_outer,
    feed_vector,
):
    frame_count = lax.axis_size("frame")
    batch_count = lax.axis_size("batch")
    frame_index = lax.axis_index("frame")
    batch_index = lax.axis_index("batch")
    feature_count = tokens.shape[2]
    row_count = tokens.shape[1]
    head_size = feature_count // HEADS
    part = round_up(-(-PATCHES // frame_count), 16)
    padded = part * frame_count
    token_rows = jnp.pad(tokens[0], ((0, padded - row_count), (0, 0)))
    grad_result = jnp.pad(cotangent[0], ((0, padded - row_count), (0, 0)))
    row_number = jnp.arange(padded, dtype=jnp.int32)[:, None]
    is_patch = row_number < PATCHES

    vectors = jnp.concatenate(
        [time_vector, space_vector, feed_vector, feed_bias.reshape(-1, time_vector.shape[1])], axis=0
    )
    vectors = lax.all_gather(vectors, "batch", axis=0)
    vectors_full = vectors[:, :13].transpose(1, 0, 2).reshape(13, feature_count)
    feed_bias_full = vectors[:, 13:].reshape(-1)
    time_rows = vectors_full[0:5].astype(jnp.float32)
    space_rows = vectors_full[5:10].astype(jnp.float32)
    feed_rows = vectors_full[10:13].astype(jnp.float32)
    time_packed = lax.all_gather(
        jnp.concatenate([time_project, time_output], axis=1), "batch", axis=0, tiled=True
    )
    space_packed = lax.all_gather(
        jnp.concatenate([space_project, space_output], axis=1), "batch", axis=0, tiled=True
    )
    feed_inner_full = lax.all_gather(feed_inner, "batch", axis=0, tiled=True)
    feed_outer_full = lax.all_gather(feed_outer, "batch", axis=0, tiled=True)
    time_project_full = time_packed[:, : 3 * feature_count]
    time_output_full = time_packed[:, 3 * feature_count :]
    space_project_full = space_packed[:, : 3 * feature_count]
    space_output_full = space_packed[:, 3 * feature_count :]

    inputs = token_rows.astype(jnp.float32)
    patches = jnp.concatenate(rows_to_frames(token_rows, frame_count, frame_index), axis=0).astype(
        jnp.float32
    )
    normed_time, time_norm_back = jax.vjp(norm_rows, patches, time_rows[0], time_rows[1])
    first_input = normed_time.astype(jnp.bfloat16)
    joined = forward_dot(first_input, time_project_full)
    query_time = (joined[:, :feature_count] + time_rows[2]).astype(jnp.bfloat16)
    key_time = joined[:, feature_count : 2 * feature_count].astype(jnp.bfloat16)
    value_time = (joined[:, 2 * feature_count :] + time_rows[3]).astype(jnp.bfloat16)
    query_time, key_time, value_time = (
        array.reshape(frame_count, part, feature_count)
        for array in (query_time, key_time, value_time)
    )
    mixture, time_total = frame_forward(query_time, key_time, value_time)
    mixture_time = frames_to_rows(list(mixture), frame_count, frame_index)
    after_time = inputs + jnp.where(
        is_patch, forward_dot(mixture_time, time_output_full) + time_rows[4], 0.0
    )
    normed_space, space_norm_back = jax.vjp(norm_rows, after_time, space_rows[0], space_rows[1])
    second_input = normed_space.astype(jnp.bfloat16)
    joined = forward_dot(second_input, space_project_full)
    query_space = (joined[:, :feature_count] + space_rows[2]).astype(jnp.bfloat16)
    key_space = joined[:, feature_count : 2 * feature_count].astype(jnp.bfloat16)
    value_space = (joined[:, 2 * feature_count :] + space_rows[3]).astype(jnp.bfloat16)
    clip_tag = size_tag[0]
    clip_number = jnp.concatenate(
        [
            jnp.arange(PATCHES, dtype=jnp.int32) // clip_tag,
            jnp.arange(UNITS, dtype=jnp.int32),
            jnp.full((padded - PATCHES - UNITS,), -1, jnp.int32),
        ]
    )
    linked = clip_number[:, None] == clip_number[None, :]
    scores = space_scores(query_space, key_space, linked)
    space_total = jax.nn.logsumexp(scores, axis=-1)
    rounded = jnp.exp(scores - space_total[..., None]).astype(jnp.bfloat16)
    value_split = value_space.reshape(padded, HEADS, head_size)
    mixture_space = jnp.einsum(
        "hqk,khd->qhd", rounded, value_split, preferred_element_type=jnp.float32
    )
    mixture_space = mixture_space.reshape(padded, feature_count).astype(jnp.bfloat16)
    after_space = after_time + forward_dot(mixture_space, space_output_full) + space_rows[4]
    normed_feed, feed_norm_back = jax.vjp(norm_rows, after_space, feed_rows[0], feed_rows[1])
    third_input = normed_feed.astype(jnp.bfloat16)
    hidden = forward_dot(third_input, feed_inner_full) + feed_bias_full.astype(jnp.float32)
    active_float, gelu_back = jax.vjp(gelu_exact, hidden)
    active = active_float.astype(jnp.bfloat16)
    block_out = (after_space + forward_dot(active, feed_outer_full) + feed_rows[2]).astype(
        jnp.bfloat16
    )
    grad_top = grad_result.astype(jnp.float32)
    grad_feed_outer = inner_rows(active, grad_result)
    feed_out_sum = jnp.sum(grad_top, axis=0)
    (grad_hidden,) = gelu_back(times_back(grad_result, feed_outer_full))
    grad_hidden = grad_hidden.astype(jnp.bfloat16)
    grad_feed_inner = inner_rows(third_input, grad_hidden)
    grad_feed_bias = jnp.sum(grad_hidden.astype(jnp.float32), axis=0)
    grad_second, feed_gain, feed_shift = feed_norm_back(times_back(grad_hidden, feed_inner_full))
    grad_second = grad_second + grad_top
    grad_feed_vector = jnp.stack([feed_gain, feed_shift, feed_out_sum])
    grad_branch = grad_second.astype(jnp.bfloat16)
    grad_space_output = inner_rows(mixture_space, grad_branch)
    space_out_sum = jnp.sum(grad_branch.astype(jnp.float32), axis=0)
    grad_mixture = times_back(grad_branch, space_output_full).astype(jnp.bfloat16)
    scores = space_scores(query_space, key_space, linked)
    probability = jnp.exp(scores - space_total[..., None])
    grad_split = grad_mixture.reshape(padded, HEADS, head_size)
    grad_weights = jnp.einsum(
        "qhd,khd->hqk", grad_split, value_split, preferred_element_type=jnp.float32
    )
    grad_scores = probability * (
        grad_weights - jnp.sum(grad_weights * probability, axis=-1, keepdims=True)
    )
    grad_scores = grad_scores.astype(jnp.bfloat16)
    scaling = head_size ** (-0.5)
    query_split = query_space.reshape(padded, HEADS, head_size)
    key_split = key_space.reshape(padded, HEADS, head_size)
    grad_query = (
        jnp.einsum("hqk,khd->qhd", grad_scores, key_split, preferred_element_type=jnp.float32)
        * scaling
    )
    grad_keys = (
        jnp.einsum("hqk,qhd->khd", grad_scores, query_split, preferred_element_type=jnp.float32)
        * scaling
    )
    grad_values = jnp.einsum(
        "hqk,qhd->khd",
        probability.astype(jnp.bfloat16),
        grad_split,
        preferred_element_type=jnp.float32,
    )
    grad_query = grad_query.reshape(padded, feature_count).astype(jnp.bfloat16)
    grad_keys = grad_keys.reshape(padded, feature_count).astype(jnp.bfloat16)
    grad_values = grad_values.reshape(padded, feature_count).astype(jnp.bfloat16)
    grad_joined = jnp.concatenate([grad_query, grad_keys, grad_values], axis=1)
    grad_space_project = inner_rows(second_input, grad_joined)
    grad_first, space_gain, space_shift = space_norm_back(
        times_back(grad_joined, space_project_full)
    )
    grad_first = grad_first + grad_second
    grad_space_vector = jnp.stack(
        [
            space_gain,
            space_shift,
            jnp.sum(grad_query.astype(jnp.float32), axis=0),
            jnp.sum(grad_values.astype(jnp.float32), axis=0),
            space_out_sum,
        ]
    )
    grad_patch = jnp.where(is_patch, grad_first, 0.0).astype(jnp.bfloat16)
    grad_time_output = inner_rows(mixture_time, grad_patch)
    time_out_sum = jnp.sum(grad_patch.astype(jnp.float32), axis=0)
    grad_mixture_time = times_back(grad_patch, time_output_full).astype(jnp.bfloat16)
    grad_mixture_slots = rows_to_frames(grad_mixture_time, frame_count, frame_index)
    grads_time = frame_backward(
        query_time, key_time, value_time, time_total, jnp.stack(grad_mixture_slots)
    )
    grad_query_time, grad_key_time, grad_value_time = (
        array.reshape(padded, feature_count).astype(jnp.bfloat16) for array in grads_time
    )
    grad_joined_time = jnp.concatenate([grad_query_time, grad_key_time, grad_value_time], axis=1)
    grad_time_project = inner_rows(first_input, grad_joined_time)
    grad_patches, time_gain, time_shift = time_norm_back(
        times_back(grad_joined_time, time_project_full)
    )
    grad_slots = list(grad_patches.astype(jnp.bfloat16).reshape(frame_count, part, feature_count))
    grad_tokens = grad_first + frames_to_rows(grad_slots, frame_count, frame_index).astype(
        jnp.float32
    )
    grad_time_vector = jnp.stack(
        [
            time_gain,
            time_shift,
            jnp.sum(grad_query_time.astype(jnp.float32), axis=0),
            jnp.sum(grad_value_time.astype(jnp.float32), axis=0),
            time_out_sum,
        ]
    )
    sizes = (batch_count, frame_count)
    indices = (batch_index, frame_index)
    low = jnp.bfloat16
    vector_grads = jnp.concatenate(
        [grad_time_vector, grad_space_vector, grad_feed_vector, grad_feed_bias.reshape(-1, feature_count)]
    )
    vector_grads = lax.psum(vector_grads, ("batch", "frame"))
    grad_feed_inner, grad_feed_outer = lax.psum(
        (grad_feed_inner.astype(low), grad_feed_outer.astype(low)), ("batch", "frame")
    )
    (space_sum,) = sum_everywhere(
        [jnp.concatenate([grad_space_project.astype(low), grad_space_output.astype(low)], axis=1)],
        sizes,
        indices,
    )
    (time_sum,) = sum_everywhere(
        [jnp.concatenate([grad_time_project.astype(low), grad_time_output.astype(low)], axis=1)],
        sizes,
        indices,
    )
    space_sum = space_sum.astype(jnp.float32)
    time_sum = time_sum.astype(jnp.float32)
    return (
        block_out[None, :row_count],
        grad_tokens[None, :row_count],
        time_sum[:, : 3 * feature_count],
        time_sum[:, 3 * feature_count :],
        vector_grads[0:5],
        space_sum[:, : 3 * feature_count],
        space_sum[:, 3 * feature_count :],
        vector_grads[5:10],
        grad_feed_inner.astype(jnp.float32),
        vector_grads[13:].reshape(-1),
        grad_feed_outer.astype(jnp.float32),
        vector_grads[10:13],
    )


def solution(mesh):
    placed = (
        P("frame", "batch", None),
        P("batch"),
        P("frame", "batch", None),
        P("batch", None),
        P("batch", None),
        P(None, "batch"),
        P("batch", None),
        P("batch", None),
        P(None, "batch"),
        P("batch", None),
        P("batch"),
        P("batch", None),
        P(None, "batch"),
    )
    return jax.shard_map(
        body,
        mesh=mesh,
        in_specs=placed,
        out_specs=(
            P("frame", "batch", None),
            P("frame", "batch", None),
            P(),
            P(),
            P(),
            P(),
            P(),
            P(),
            P(),
            P(),
            P(),
            P(),
        ),
        check_vma=False,
    )
```

```python
import functools
import math

import jax
import jax.numpy as jnp
from jax import lax
from jax.experimental import pallas as pl
from jax.experimental.pallas import tpu as pltpu
from jax.sharding import PartitionSpec as P

HEADS = 12
UNITS = 4
PATCHES = 784
LOG2E = 1.4426950408889634

def round_up(count, step):
    return -(-count // step) * step


def shift_frames(block, frame_count, shift):
    if shift % frame_count == 0:
        return block
    pairs = [(index, (index + shift) % frame_count) for index in range(frame_count)]
    return lax.ppermute(block, "frame", pairs)


def rows_to_frames(rows, frame_count, frame_index):
    part = rows.shape[0] // frame_count
    slots = []
    for shift in range(frame_count):
        owner = (frame_index + shift) % frame_count
        block = lax.dynamic_slice_in_dim(rows, owner * part, part, 0)
        slots.append(shift_frames(block, frame_count, shift))
    return slots


def frames_to_rows(slots, frame_count, frame_index):
    part = slots[0].shape[0]
    rows = jnp.zeros((part * frame_count, slots[0].shape[1]), slots[0].dtype)
    for shift in range(frame_count):
        owner = (frame_index + shift) % frame_count
        block = shift_frames(slots[shift], frame_count, -shift)
        rows = lax.dynamic_update_slice_in_dim(rows, block, owner * part, 0)
    return rows


def swap_bit(block, axis, size, bit):
    pairs = [(index, index ^ (1 << bit)) for index in range(size)]
    return lax.ppermute(block, axis, pairs)


def halve_sum(block, axis, size, bit, index):
    half = block.shape[0] // 2
    own = (index >> bit) & 1
    sent = lax.dynamic_slice_in_dim(block, (1 - own) * half, half, 0)
    kept = lax.dynamic_slice_in_dim(block, own * half, half, 0)
    arrived = swap_bit(sent, axis, size, bit)
    return (kept.astype(jnp.float32) + arrived.astype(jnp.float32)).astype(jnp.bfloat16)


def double_rows(block, axis, size, bit, index):
    arrived = swap_bit(block, axis, size, bit)
    own = ((index >> bit) & 1) == 1
    return jnp.concatenate(
        [jnp.where(own, arrived, block), jnp.where(own, block, arrived)], axis=0
    )


def sum_everywhere(blocks, sizes, indices):
    batch_size, frame_size = sizes
    batch_index, frame_index = indices
    batch_bits = batch_size.bit_length() - 1
    frame_bits = frame_size.bit_length() - 1
    results = []
    for order, block in enumerate(blocks):
        wide = list(range(1, batch_bits))
        if order % 2:
            wide = wide[::-1]
        stages = [("batch", batch_size, bit, batch_index) for bit in [0] + wide]
        stages += [("frame", frame_size, bit, frame_index) for bit in range(frame_bits)]
        for stage in stages:
            block = halve_sum(block, *stage)
        for stage in stages[::-1]:
            block = double_rows(block, *stage)
        results.append(block)
    return results

def contract(x,y,dims):
    return lax.dot_general(x,y,((dims[0:1],dims[1:2]),((),())),preferred_element_type=jnp.float32)

def widen_rows(values, wide):
    rows, width = values.shape
    if wide == rows:
        return values
    return jnp.concatenate([values, jnp.zeros((wide - rows, width), values.dtype)])


def head_halves(width):
    lane = lax.broadcasted_iota(jnp.int32, (1, width), 1)
    return [lane < width // 2, lane >= width // 2]

def space_forward_kernel(scale, tile, column_ref, row_ref, q_ref, k_ref, v_ref, mixture_ref, total_ref, bias_ref, k_wide, v_wide):
    rows, width = q_ref.shape
    wide = k_wide.shape[0]
    @pl.when(pl.program_id(0) == 0)
    def _():
        bias_ref[...] = jnp.where(column_ref[...] == row_ref[...], 0.0, -1e30)
        if wide > rows:
            k_wide[rows:] = jnp.zeros((wide - rows, width), k_wide.dtype)
            v_wide[rows:] = jnp.zeros((wide - rows, width), v_wide.dtype)
    k_wide[:rows] = k_ref[...]
    v_wide[:rows] = v_ref[...]
    halves = head_halves(width)
    zero, one = jnp.zeros((), q_ref.dtype), jnp.ones((), q_ref.dtype)
    filled = [jnp.where(half, v_wide[...], one) for half in halves]
    for start in range(0, rows, tile):
        span = slice(start, start + tile)
        outs, tops = [], []
        for half, values in zip(halves, filled):
            queries = jnp.where(half, q_ref[span], zero)
            scores = contract(queries, k_wide[...], (1, 1)) * (scale * LOG2E) + bias_ref[span]
            top = jnp.max(scores, axis=1, keepdims=True)
            weights = jnp.exp2(scores - top)
            outs.append(contract(weights.astype(jnp.bfloat16), values, (1, 0)))
            tops.append(top)
        mass = pltpu.roll(jnp.where(halves[0], outs[1], outs[0]), width // 2, 1)
        mixture = jnp.where(halves[0], outs[0], outs[1]) / mass
        mixture_ref[span] = mixture.astype(mixture_ref.dtype)
        total_ref[span] = jnp.where(halves[0], tops[0], tops[1]) + jnp.log2(mass)


def space_forward(qkv, clip, features):
    rows = qkv.shape[0]
    pairs = HEADS // 2
    width = features // pairs
    wide = round_up(rows, 128)
    scale = (features // HEADS) ** -0.5
    tile = rows
    column = clip[:, None]
    row = jnp.pad(clip, (0, wide - rows), constant_values=-2)[None]
    blocks = [pl.BlockSpec((rows, width), lambda i, o=o: (0, o + i)) for o in (0, pairs, 2 * pairs)]
    out = pl.BlockSpec((rows, width), lambda i: (0, i))
    return pl.pallas_call(
        functools.partial(space_forward_kernel, scale, tile),
        grid=(pairs,),
        in_specs=[pl.BlockSpec((rows, 1), lambda i: (0, 0)), pl.BlockSpec((1, wide), lambda i: (0, 0))] + blocks,
        out_specs=[out, out],
        out_shape=[jax.ShapeDtypeStruct((rows, features), jnp.bfloat16), jax.ShapeDtypeStruct((rows, features), jnp.float32)],
        scratch_shapes=[pltpu.VMEM((rows, wide), jnp.float32), pltpu.VMEM((wide, width), jnp.bfloat16), pltpu.VMEM((wide, width), jnp.bfloat16)],
        compiler_params=pltpu.CompilerParams(vmem_limit_bytes=48 << 20),
    )(column, row, qkv, qkv, qkv)

def space_backward_kernel(scale, tile, column_ref, row_ref, q_ref, k_ref, v_ref, mixture_ref, total_ref, grad_ref, dq_ref, dk_ref, dv_ref, bias_ref, q_wide, g_wide, dq_wide):
    rows, width = q_ref.shape
    wide = q_wide.shape[0]
    @pl.when(pl.program_id(0) == 0)
    def _():
        bias_ref[...] = jnp.where(column_ref[...] == row_ref[...], 0.0, -1e30)
        if wide > rows:
            q_wide[rows:] = jnp.zeros((wide - rows, width), q_wide.dtype)
            g_wide[rows:] = jnp.zeros((wide - rows, width), g_wide.dtype)
    q_wide[:rows] = q_ref[...]
    g_wide[:rows] = grad_ref[...]
    halves = head_halves(width)
    zero = jnp.zeros((), q_ref.dtype)
    product = grad_ref[...].astype(jnp.float32) * mixture_ref[...].astype(jnp.float32)
    sums = [jnp.sum(jnp.where(half, product, 0.0), axis=1, keepdims=True) for half in halves]
    delta = widen_rows(jnp.where(halves[0], sums[0], sums[1]), wide).T
    total = widen_rows(total_ref[...], wide).T
    dq_parts = [None, None]
    for start in range(0, rows, tile):
        span = slice(start, start + tile)
        dk, dv = [], []
        for index, half in enumerate(halves):
            at = index * (width // 2)
            keys = jnp.where(half, k_ref[span], zero)
            values = jnp.where(half, v_ref[span], zero)
            scores = contract(keys, q_wide[...], (1, 1)) * (scale * LOG2E)
            weights = jnp.exp2(scores + (bias_ref[span] - total[at:at + 1]))
            slopes = contract(values, g_wide[...], (1, 1))
            slopes = (weights * (slopes - delta[at:at + 1])).astype(jnp.bfloat16)
            dv.append(contract(weights.astype(jnp.bfloat16), g_wide[...], (1, 0)))
            dk.append(contract(slopes, q_wide[...], (1, 0)))
            part = contract(slopes, keys, (0, 0))
            dq_parts[index] = part if start == 0 else dq_parts[index] + part
        dk_ref[span] = (jnp.where(halves[0], dk[0], dk[1]) * scale).astype(dk_ref.dtype)
        dv_ref[span] = jnp.where(halves[0], dv[0], dv[1]).astype(dv_ref.dtype)
    dq_ref[...] = ((dq_parts[0] + dq_parts[1])[:rows] * scale).astype(dq_ref.dtype)

def space_backward(qkv, mixture, total, grad, clip, features):
    rows = qkv.shape[0]
    pairs = HEADS // 2
    width = features // pairs
    wide = round_up(rows, 128)
    scale = (features // HEADS) ** -0.5
    tile = rows
    column = clip[:, None]
    row = jnp.pad(clip, (0, wide - rows), constant_values=-2)[None]
    blocks = [pl.BlockSpec((rows, width), lambda i, o=o: (0, o + i)) for o in (0, pairs, 2 * pairs)]
    out = pl.BlockSpec((rows, width), lambda i: (0, i))
    shape = jax.ShapeDtypeStruct((rows, features), jnp.bfloat16)
    return pl.pallas_call(
        functools.partial(space_backward_kernel, scale, tile),
        grid=(pairs,),
        in_specs=[pl.BlockSpec((rows, 1), lambda i: (0, 0)), pl.BlockSpec((1, wide), lambda i: (0, 0))] + blocks + [out, out, out],
        out_specs=[out, out, out],
        out_shape=[shape, shape, shape],
        scratch_shapes=[pltpu.VMEM((rows, wide), jnp.float32), pltpu.VMEM((wide, width), jnp.bfloat16), pltpu.VMEM((wide, width), jnp.bfloat16), pltpu.VMEM((wide, width), jnp.float32)],
        compiler_params=pltpu.CompilerParams(vmem_limit_bytes=48 << 20),
    )(column, row, qkv, qkv, qkv, mixture, total, grad)

def norm_parts(values):
    average = jnp.mean(values, axis=1, keepdims=True)
    centered = values - average
    spread = lax.rsqrt(jnp.mean(centered * centered, axis=1, keepdims=True) + 1e-06)
    return centered * spread, spread
def norm_back(grad, normed, spread, gain):
    scaled = grad * gain
    return spread * (scaled - jnp.mean(scaled, axis=1, keepdims=True) - normed * jnp.mean(scaled * normed, axis=1, keepdims=True))
def column_sum(values):
    return jnp.sum(values, axis=0, keepdims=True)

def feed_kernel(chunks, x1_ref, mixture_ref, dz_ref, so_ref, fi_ref, fo_ref, fb_ref, vec_ref,
                out_ref, dx2_ref, dys_ref, dos_ref, gfi_ref, gfo_ref, gfb_ref, gso_ref, gvec_ref,
                x2_s, a3_s, a3t_s, acc_s, da_s, g_s, dh_s):
    step = pl.program_id(0)
    rows = x1_ref.shape[0]
    @pl.when(step == 0)
    def _():
        x2 = x1_ref[...] + contract(mixture_ref[...], so_ref[...], (1, 0)) + vec_ref[9:10]
        x2_s[...] = x2
        normed, _ = norm_parts(x2)
        a3 = (normed * vec_ref[10:11] + vec_ref[11:12]).astype(jnp.bfloat16)
        a3_s[...] = a3
        a3t_s[...] = a3.T
        acc_s[...] = x2 + vec_ref[12:13]
        da_s[...] = jnp.zeros_like(da_s)
    part = rows // chunks
    for chunk in range(chunks):
        span = slice(chunk * part, (chunk + 1) * part)
        hidden = contract(a3_s[span], fi_ref[...], (1, 0)) + fb_ref[...]
        cdf = 0.5 + 0.5 * lax.erf(hidden * math.sqrt(0.5))
        slope = cdf + hidden * jnp.exp(hidden * hidden * -0.5) * (1.0 / math.sqrt(2.0 * math.pi))
        active = (hidden * cdf).astype(jnp.bfloat16)
        g_s[span] = active
        dh = (contract(dz_ref[span], fo_ref[...], (1, 1)) * slope).astype(jnp.bfloat16)
        dh_s[span] = dh
        acc_s[span] += contract(active, fo_ref[...], (1, 0))
        da_s[span] += contract(dh, fi_ref[...], (1, 1))
    gfo_ref[...] = contract(g_s[...], dz_ref[...], (0, 0)).astype(gfo_ref.dtype)
    gfi_ref[...] = contract(a3t_s[...], dh_s[...], (1, 0)).astype(gfi_ref.dtype)
    gfb_ref[...] = column_sum(dh_s[...].astype(jnp.float32))
    @pl.when(step == pl.num_programs(0) - 1)
    def _():
        out_ref[...] = acc_s[...].astype(out_ref.dtype)
        normed, spread = norm_parts(x2_s[...])
        grad = da_s[...]
        dz = dz_ref[...].astype(jnp.float32)
        dx2 = dz + norm_back(grad, normed, spread, vec_ref[10:11])
        dx2_ref[...] = dx2
        dys = dx2.astype(jnp.bfloat16)
        dys_ref[...] = dys
        dos_ref[...] = contract(dys, so_ref[...], (1, 1)).astype(dos_ref.dtype)
        gso_ref[...] = contract(mixture_ref[...], dys, (0, 0)).astype(gso_ref.dtype)
        gvec_ref[0:1] = column_sum(grad * normed)
        gvec_ref[1:2] = column_sum(grad)
        gvec_ref[2:3] = column_sum(dz)
        gvec_ref[3:4] = column_sum(dys.astype(jnp.float32))
        gvec_ref[4:8] = jnp.zeros((4, gvec_ref.shape[1]), jnp.float32)

def feed_block(x1, mixture, dz, space_packed, fi, fo, fb, vec, tile, chunks):
    rows, features = x1.shape
    hidden = fi.shape[1]
    whole = pl.BlockSpec((rows, features), lambda j: (0, 0))
    square = pl.BlockSpec((features, features), lambda j: (0, 0))
    fi_spec = pl.BlockSpec((features, tile), lambda j: (0, j))
    fo_spec = pl.BlockSpec((tile, features), lambda j: (j, 0))
    fb_spec = pl.BlockSpec((1, tile), lambda j: (0, j))
    vec_spec = pl.BlockSpec(vec.shape, lambda j: (0, 0))
    sum_spec = pl.BlockSpec((8, features), lambda j: (0, 0))
    low, full = jnp.bfloat16, jnp.float32
    shape = jax.ShapeDtypeStruct
    return pl.pallas_call(
        functools.partial(feed_kernel, chunks),
        grid=(hidden // tile,),
        in_specs=[whole, whole, whole, pl.BlockSpec((features, features), lambda j: (0, space_packed.shape[1] // features - 1)), fi_spec, fo_spec, fb_spec, vec_spec],
        out_specs=[whole, whole, whole, whole, fi_spec, fo_spec, fb_spec, square, sum_spec],
        out_shape=[shape((rows, features), low), shape((rows, features), full), shape((rows, features), low), shape((rows, features), low),
                   shape(fi.shape, low), shape(fo.shape, low), shape((1, hidden), full), shape((features, features), low), shape((8, features), full)],
        scratch_shapes=[pltpu.VMEM((rows, features), full), pltpu.VMEM((rows, features), low), pltpu.VMEM((features, rows), low),
                        pltpu.VMEM((rows, features), full), pltpu.VMEM((rows, features), full), pltpu.VMEM((rows, tile), low), pltpu.VMEM((rows, tile), low)],
        compiler_params=pltpu.CompilerParams(vmem_limit_bytes=56 << 20),
    )(x1, mixture, dz, space_packed, fi, fo, fb, vec)

def middle_kernel(token_ref, mixture_ref, to_ref, sp_ref, vec_ref, x1_ref, a2_ref, qkv_ref):
    rows, features = token_ref.shape
    number = lax.broadcasted_iota(jnp.int32, (rows, 1), 0)
    branch = contract(mixture_ref[...], to_ref[...], (1, 0)) + vec_ref[4:5]
    x1 = token_ref[...].astype(jnp.float32) + jnp.where(number < PATCHES, branch, 0.0)
    x1_ref[...] = x1
    normed, _ = norm_parts(x1)
    a2 = (normed * vec_ref[5:6] + vec_ref[6:7]).astype(jnp.bfloat16)
    a2_ref[...] = a2
    for third in range(3):
        span = slice(third * features, (third + 1) * features)
        joined = contract(a2, sp_ref[:, span], (1, 0))
        if third != 1:
            joined = joined + vec_ref[7 + third // 2 : 8 + third // 2]
        qkv_ref[:, span] = joined.astype(jnp.bfloat16)


def middle_forward(tokens, mixture, time_packed, space_packed, vec):
    rows, features = tokens.shape
    whole = pl.BlockSpec((rows, features), lambda i: (0, 0))
    shape = jax.ShapeDtypeStruct
    return pl.pallas_call(
        middle_kernel,
        grid=(1,),
        in_specs=[
            whole,
            whole,
            pl.BlockSpec((features, features), lambda i: (0, 3)),
            pl.BlockSpec((features, 3 * features), lambda i: (0, 0)),
            pl.BlockSpec(vec.shape, lambda i: (0, 0)),
        ],
        out_specs=[whole, whole, pl.BlockSpec((rows, 3 * features), lambda i: (0, 0))],
        out_shape=[
            shape((rows, features), jnp.float32),
            shape((rows, features), jnp.bfloat16),
            shape((rows, 3 * features), jnp.bfloat16),
        ],
        compiler_params=pltpu.CompilerParams(vmem_limit_bytes=56 << 20),
    )(tokens, mixture, time_packed, space_packed, vec)


def middle_back_kernel(dq_ref, dk_ref, dv_ref, x1_ref, dx2_ref, to_ref, sp_ref, vec_ref, dx1_ref, dyt_ref, dot_ref, sums_ref):
    rows, features = x1_ref.shape
    grad = 0.0
    for third, piece in enumerate((dq_ref, dk_ref, dv_ref)):
        span = slice(third * features, (third + 1) * features)
        grad = grad + contract(piece[...], sp_ref[:, span], (1, 1))
    normed, spread = norm_parts(x1_ref[...])
    dx1 = dx2_ref[...] + norm_back(grad, normed, spread, vec_ref[5:6])
    dx1_ref[...] = dx1
    number = lax.broadcasted_iota(jnp.int32, (rows, 1), 0)
    dyt = jnp.where(number < PATCHES, dx1, 0.0).astype(jnp.bfloat16)
    dyt_ref[...] = dyt
    dot_ref[...] = contract(dyt, to_ref[...], (1, 1)).astype(dot_ref.dtype)
    sums_ref[0:1] = column_sum(grad * normed)
    sums_ref[1:2] = column_sum(grad)
    sums_ref[2:3] = column_sum(dq_ref[...].astype(jnp.float32))
    sums_ref[3:4] = column_sum(dv_ref[...].astype(jnp.float32))
    sums_ref[4:5] = column_sum(dyt.astype(jnp.float32))
    sums_ref[5:8] = jnp.zeros((3, features), jnp.float32)


def middle_backward(dq, dk, dv, x1, dx2, time_packed, space_packed, vec):
    rows, features = x1.shape
    whole = pl.BlockSpec((rows, features), lambda i: (0, 0))
    shape = jax.ShapeDtypeStruct
    return pl.pallas_call(
        middle_back_kernel,
        grid=(1,),
        in_specs=[whole] * 5
        + [
            pl.BlockSpec((features, features), lambda i: (0, 3)),
            pl.BlockSpec((features, 3 * features), lambda i: (0, 0)),
            pl.BlockSpec(vec.shape, lambda i: (0, 0)),
        ],
        out_specs=[whole, whole, whole, pl.BlockSpec((8, features), lambda i: (0, 0))],
        out_shape=[
            shape((rows, features), jnp.float32),
            shape((rows, features), jnp.bfloat16),
            shape((rows, features), jnp.bfloat16),
            shape((8, features), jnp.float32),
        ],
        compiler_params=pltpu.CompilerParams(vmem_limit_bytes=56 << 20),
    )(dq, dk, dv, x1, dx2, time_packed, space_packed, vec)


def middle_weights_kernel(a2_ref, dq_ref, dk_ref, dv_ref, mixture_ref, dyt_ref, gsp_ref, gto_ref):
    features = a2_ref.shape[1]
    turned = a2_ref[...].T
    for third, piece in enumerate((dq_ref, dk_ref, dv_ref)):
        span = slice(third * features, (third + 1) * features)
        gsp_ref[:, span] = contract(turned, piece[...], (1, 0)).astype(gsp_ref.dtype)
    gto_ref[...] = contract(mixture_ref[...], dyt_ref[...], (0, 0)).astype(gto_ref.dtype)


def middle_weights(a2, dq, dk, dv, mixture, dyt):
    features = a2.shape[1]
    vmem = pl.BlockSpec(memory_space=pltpu.VMEM)
    shape = jax.ShapeDtypeStruct
    return pl.pallas_call(
        middle_weights_kernel,
        in_specs=[vmem] * 6,
        out_specs=[vmem] * 2,
        out_shape=[
            shape((features, 3 * features), jnp.bfloat16),
            shape((features, features), jnp.bfloat16),
        ],
        compiler_params=pltpu.CompilerParams(vmem_limit_bytes=56 << 20),
    )(a2, dq, dk, dv, mixture, dyt)

CHUNK=16
def head_map(features, lanes=128):
    head = jnp.arange(features, dtype=jnp.int32) // (features // HEADS)
    return (head[:, None] == jnp.arange(lanes, dtype=jnp.int32)[None]).astype(jnp.bfloat16)

def pair_sums(left, right, gather_ref, pair_s):
    count = len(left)
    for f in range(count):
        for g in range(count):
            at = (f * count + g) * CHUNK
            pair_s[at:at + CHUNK] = (left[f] * right[g]).astype(jnp.bfloat16)
    return contract(pair_s[...], gather_ref[...], (1, 0))

def time_forward_kernel(count, scale, *refs):
    slots, (tp_ref, vec_ref, gather_ref, spread_ref) = refs[:count], refs[count:count + 4]
    outs, (qkv_ref, prob_ref, a1_ref) = refs[count + 4:2 * count + 4], refs[2 * count + 4:2 * count + 7]
    pair_s, weight_s = refs[2 * count + 7:]
    part, features = slots[0].shape
    for s in range(count):
        normed, _ = norm_parts(slots[s][...].astype(jnp.float32))
        a1_ref[s * part:(s + 1) * part] = (normed * vec_ref[0:1] + vec_ref[1:2]).astype(jnp.bfloat16)
    for third in range(3):
        span = slice(third * features, (third + 1) * features)
        joined = contract(a1_ref[...], tp_ref[:, span], (1, 0))
        if third != 1:
            joined = joined + vec_ref[2 + third // 2:3 + third // 2]
        qkv_ref[:, span] = joined.astype(jnp.bfloat16)

    def chunk_step(index, carry):
        def rows_of(s, third):
            start = pl.multiple_of(s * part + index * CHUNK, CHUNK)
            return qkv_ref[pl.ds(start, CHUNK), third * features:(third + 1) * features].astype(jnp.float32)
        queries, keys, values = ([rows_of(s, third) for s in range(count)] for third in range(3))
        scores = pair_sums(queries, keys, gather_ref, pair_s) * (scale * LOG2E)
        place = pl.ds(pl.multiple_of(index * CHUNK, CHUNK), CHUNK)
        for f in range(count):
            row = [scores[(f * count + g) * CHUNK:(f * count + g + 1) * CHUNK] for g in range(count)]
            top = functools.reduce(jnp.maximum, row)
            raised = [jnp.exp2(item - top) for item in row]
            mass = functools.reduce(jnp.add, raised)
            for g in range(count):
                weight = raised[g] / mass
                prob_ref[f * count + g, place] = weight
                at = (f * count + g) * CHUNK
                weight_s[at:at + CHUNK] = weight.astype(jnp.bfloat16)
        wide = contract(weight_s[...], spread_ref[...], (1, 0))
        for f in range(count):
            total = 0.0
            for g in range(count):
                at = (f * count + g) * CHUNK
                total = total + wide[at:at + CHUNK] * values[g]
            outs[f][place] = total.astype(jnp.bfloat16)
        return carry
    lax.fori_loop(0, part // CHUNK, chunk_step, 0)

def time_forward(slots, time_packed, vec):
    count = len(slots)
    part, features = slots[0].shape
    gather = head_map(features)
    low, full = jnp.bfloat16, jnp.float32
    shape = jax.ShapeDtypeStruct
    vmem = pl.BlockSpec(memory_space=pltpu.VMEM)
    results = pl.pallas_call(
        functools.partial(time_forward_kernel, count, (features // HEADS) ** -0.5),
        grid=(1,),
        in_specs=[pl.BlockSpec((part, features), lambda i: (0, 0))] * count + [pl.BlockSpec((features, 3 * features), lambda i: (0, 0)), vmem, vmem, vmem],
        out_specs=[vmem] * (count + 3),
        out_shape=[shape((part, features), low)] * count + [shape((count * part, 3 * features), low), shape((count * count, part, 128), full), shape((count * part, features), low)],
        scratch_shapes=[pltpu.VMEM((count * count * CHUNK, features), low), pltpu.VMEM((count * count * CHUNK, 128), low)],
        compiler_params=pltpu.CompilerParams(vmem_limit_bytes=56 << 20),
    )(*slots, time_packed, vec, gather, gather.T)
    return results[:count], results[count], results[count + 1], results[count + 2]

def time_backward_kernel(count, scale, *refs):
    grads, (qkv_ref, prob_ref, a1_ref, gather_ref, spread_ref) = refs[:count], refs[count:count + 5]
    dqkv_ref, gtp_ref, sums_ref, pair_s, weight_s = refs[count + 5:]
    part, features = grads[0].shape
    def chunk_step(index, carry):
        place = pl.ds(pl.multiple_of(index * CHUNK, CHUNK), CHUNK)
        def rows_of(s, third):
            start = pl.multiple_of(s * part + index * CHUNK, CHUNK)
            return qkv_ref[pl.ds(start, CHUNK), third * features:(third + 1) * features].astype(jnp.float32)
        queries, keys, values = ([rows_of(s, third) for s in range(count)] for third in range(3))
        outer = [grads[s][place].astype(jnp.float32) for s in range(count)]
        slopes = pair_sums(outer, values, gather_ref, pair_s)
        size = count * count * CHUNK
        for f in range(count):
            row = [slopes[(f * count + g) * CHUNK:(f * count + g + 1) * CHUNK] for g in range(count)]
            weights = [prob_ref[f * count + g, place] for g in range(count)]
            delta = functools.reduce(jnp.add, [w * s for w, s in zip(weights, row)])
            for g in range(count):
                at = (f * count + g) * CHUNK
                weight_s[at:at + CHUNK] = weights[g].astype(jnp.bfloat16)
                weight_s[size + at:size + at + CHUNK] = (weights[g] * (row[g] - delta)).astype(jnp.bfloat16)
        wide = contract(weight_s[...], spread_ref[...], (1, 0))
        for s in range(count):
            dq, dk, dv = 0.0, 0.0, 0.0
            for t in range(count):
                forth, back = (s * count + t) * CHUNK, (t * count + s) * CHUNK
                dq = dq + wide[size + forth:size + forth + CHUNK] * keys[t]
                dk = dk + wide[size + back:size + back + CHUNK] * queries[t]
                dv = dv + wide[back:back + CHUNK] * outer[t]
            start = pl.ds(pl.multiple_of(s * part + index * CHUNK, CHUNK), CHUNK)
            for third, value in enumerate((dq * scale, dk * scale, dv)):
                dqkv_ref[start, third * features:(third + 1) * features] = value.astype(jnp.bfloat16)
        return carry
    lax.fori_loop(0, part // CHUNK, chunk_step, 0)
    a1t = a1_ref[...].T
    for third in range(3):
        span = slice(third * features, (third + 1) * features)
        gtp_ref[:, span] = contract(a1t, dqkv_ref[:, span], (1, 0)).astype(gtp_ref.dtype)
    sums_ref[0:1] = column_sum(dqkv_ref[:, :features].astype(jnp.float32))
    sums_ref[1:2] = column_sum(dqkv_ref[:, 2 * features:].astype(jnp.float32))
    sums_ref[2:8] = jnp.zeros((6, features), jnp.float32)

def time_backward(grads, qkv, prob, a1):
    count = len(grads)
    part, features = grads[0].shape
    gather = head_map(features)
    shape = jax.ShapeDtypeStruct
    vmem = pl.BlockSpec(memory_space=pltpu.VMEM)
    return pl.pallas_call(
        functools.partial(time_backward_kernel, count, (features // HEADS) ** -0.5),
        in_specs=[vmem] * (count + 5),
        out_specs=[vmem] * 3,
        out_shape=[shape(qkv.shape, jnp.bfloat16), shape((features, 3 * features), jnp.bfloat16), shape((8, features), jnp.float32)],
        scratch_shapes=[pltpu.VMEM((count * count * CHUNK, features), jnp.bfloat16), pltpu.VMEM((2 * count * count * CHUNK, 128), jnp.bfloat16)],
        compiler_params=pltpu.CompilerParams(vmem_limit_bytes=56 << 20),
    )(*grads, qkv, prob, a1, gather, gather.T)

def time_input_kernel(count, *refs):
    slots, (dqkv_ref, tp_ref, vec_ref) = refs[:count], refs[count:count + 3]
    outs, sums_ref = refs[count + 3:2 * count + 3], refs[2 * count + 3]
    part, features = slots[0].shape
    grad = contract(dqkv_ref[...], tp_ref[...], (1, 1))
    gain, shift = 0.0, 0.0
    for s in range(count):
        piece = grad[s * part:(s + 1) * part]
        normed, spread = norm_parts(slots[s][...].astype(jnp.float32))
        outs[s][...] = norm_back(piece, normed, spread, vec_ref[0:1]).astype(jnp.bfloat16)
        gain = gain + column_sum(piece * normed)
        shift = shift + column_sum(piece)
    sums_ref[0:1] = gain
    sums_ref[1:2] = shift
    sums_ref[2:8] = jnp.zeros((6, features), jnp.float32)

def time_input(slots, dqkv, time_packed, vec):
    count = len(slots)
    part, features = slots[0].shape
    shape = jax.ShapeDtypeStruct
    vmem = pl.BlockSpec(memory_space=pltpu.VMEM)
    results = pl.pallas_call(
        functools.partial(time_input_kernel, count),
        grid=(1,),
        in_specs=[pl.BlockSpec((part, features), lambda i: (0, 0))] * count + [vmem, pl.BlockSpec((features, 3 * features), lambda i: (0, 0)), vmem],
        out_specs=[vmem] * (count + 1),
        out_shape=[shape((part, features), jnp.bfloat16)] * count + [shape((8, features), jnp.float32)],
        compiler_params=pltpu.CompilerParams(vmem_limit_bytes=56 << 20),
    )(*slots, dqkv, time_packed, vec)
    return results[:count], results[count]

def body(
    tokens,
    size_tag,
    cotangent,
    time_project,
    time_output,
    time_vector,
    space_project,
    space_output,
    space_vector,
    feed_inner,
    feed_bias,
    feed_outer,
    feed_vector,
):
    frame_count = lax.axis_size("frame")
    batch_count = lax.axis_size("batch")
    frame_index = lax.axis_index("frame")
    batch_index = lax.axis_index("batch")
    features = tokens.shape[2]
    row_count = tokens.shape[1]
    part = round_up(-(-PATCHES // frame_count), 16)
    padded = part * frame_count
    token_rows = jnp.pad(tokens[0], ((0, padded - row_count), (0, 0)))
    grad_result = jnp.pad(cotangent[0], ((0, padded - row_count), (0, 0)))

    vectors = jnp.concatenate(
        [time_vector, space_vector, feed_vector, feed_bias.reshape(-1, time_vector.shape[1])], axis=0
    )
    vectors = lax.all_gather(vectors, "batch", axis=0)
    vec = vectors[:, :13].transpose(1, 0, 2).reshape(13, features).astype(jnp.float32)
    vec = jnp.pad(vec, ((0, 3), (0, 0)))
    feed_bias_row = vectors[:, 13:].reshape(1, -1).astype(jnp.float32)
    time_packed = lax.all_gather(
        jnp.concatenate([time_project, time_output], axis=1), "batch", axis=0, tiled=True
    )
    space_packed = lax.all_gather(
        jnp.concatenate([space_project, space_output], axis=1), "batch", axis=0, tiled=True
    )
    feed_inner_full = lax.all_gather(feed_inner, "batch", axis=0, tiled=True)
    feed_outer_full = lax.all_gather(feed_outer, "batch", axis=0, tiled=True)

    slots = rows_to_frames(token_rows, frame_count, frame_index)
    mixture_slots, qkv_time, prob_time, first_input = time_forward(slots, time_packed, vec)
    mixture_time = frames_to_rows(mixture_slots, frame_count, frame_index)
    after_time, second_input, qkv_space = middle_forward(
        token_rows, mixture_time, time_packed, space_packed, vec
    )
    clip = jnp.concatenate(
        [
            jnp.arange(PATCHES, dtype=jnp.int32) // size_tag[0],
            jnp.arange(UNITS, dtype=jnp.int32),
            jnp.full((padded - PATCHES - UNITS,), -1, jnp.int32),
        ]
    )
    mixture_space, total_space = space_forward(qkv_space, clip, features)
    (
        block_out,
        grad_second,
        grad_branch,
        grad_mixture,
        grad_feed_inner,
        grad_feed_outer,
        grad_feed_bias,
        grad_space_output,
        feed_sums,
    ) = feed_block(
        after_time,
        mixture_space,
        grad_result,
        space_packed,
        feed_inner_full,
        feed_outer_full,
        feed_bias_row,
        vec,
        tile=features,
        chunks=2,
    )
    grad_query, grad_keys, grad_values = space_backward(
        qkv_space, mixture_space, total_space, grad_mixture, clip, features
    )
    grad_first, grad_patch, grad_mixture_time, space_sums = middle_backward(
        grad_query, grad_keys, grad_values, after_time, grad_second, time_packed, space_packed, vec
    )
    grad_slots = rows_to_frames(grad_mixture_time, frame_count, frame_index)
    grad_space_project, grad_time_output = middle_weights(
        second_input, grad_query, grad_keys, grad_values, mixture_time, grad_patch
    )
    grad_joined_time, grad_time_project, time_sums = time_backward(
        grad_slots, qkv_time, prob_time, first_input
    )
    input_slots, input_sums = time_input(slots, grad_joined_time, time_packed, vec)
    grad_tokens = grad_first + frames_to_rows(input_slots, frame_count, frame_index).astype(
        jnp.float32
    )

    sizes = (batch_count, frame_count)
    indices = (batch_index, frame_index)
    vector_grads = jnp.concatenate(
        [
            input_sums[0:2],
            time_sums[0:2],
            space_sums[4:5],
            space_sums[0:4],
            feed_sums[3:4],
            feed_sums[0:3],
            grad_feed_bias.reshape(-1, features),
        ]
    )
    vector_grads = lax.psum(vector_grads, ("batch", "frame"))
    grad_feed_inner, grad_feed_outer = lax.psum(
        (grad_feed_inner, grad_feed_outer), ("batch", "frame")
    )
    (space_sum,) = sum_everywhere(
        [jnp.concatenate([grad_space_project, grad_space_output], axis=1)], sizes, indices
    )
    (time_sum,) = sum_everywhere(
        [jnp.concatenate([grad_time_project, grad_time_output], axis=1)], sizes, indices
    )
    space_sum = space_sum.astype(jnp.float32)
    time_sum = time_sum.astype(jnp.float32)
    return (
        block_out[None, :row_count],
        grad_tokens[None, :row_count],
        time_sum[:, : 3 * features],
        time_sum[:, 3 * features :],
        vector_grads[0:5],
        space_sum[:, : 3 * features],
        space_sum[:, 3 * features :],
        vector_grads[5:10],
        grad_feed_inner.astype(jnp.float32),
        vector_grads[13:].reshape(-1),
        grad_feed_outer.astype(jnp.float32),
        vector_grads[10:13],
    )


def solution(mesh):
    placed = (
        P("frame", "batch", None),
        P("batch"),
        P("frame", "batch", None),
        P("batch", None),
        P("batch", None),
        P(None, "batch"),
        P("batch", None),
        P("batch", None),
        P(None, "batch"),
        P("batch", None),
        P("batch"),
        P("batch", None),
        P(None, "batch"),
    )
    return jax.shard_map(
        body,
        mesh=mesh,
        in_specs=placed,
        out_specs=(
            P("frame", "batch", None),
            P("frame", "batch", None),
            P(),
            P(),
            P(),
            P(),
            P(),
            P(),
            P(),
            P(),
            P(),
            P(),
        ),
        check_vma=False,
    )
```

```python
import functools
import math

import jax
import jax.numpy as jnp
from jax import lax
from jax.experimental import pallas as pl
from jax.experimental.pallas import tpu as pltpu
from jax.sharding import PartitionSpec as P

HEADS = 12
UNITS = 4
PATCHES = 784
LOG2E = 1.4426950408889634
ROW_TILE = 16


def round_up(count, step):
    return -(-count // step) * step


def struct(shape, dtype):
    return jax.ShapeDtypeStruct(shape, dtype)


VMEM = pl.BlockSpec(memory_space=pltpu.VMEM)
SMEM = pl.BlockSpec(memory_space=pltpu.SMEM)


class Order:
    def __init__(self, flags):
        self.flags = flags
        self.token = None

    def run(self, kernel, operands, in_specs, out_specs, out_shape, grid=(), scratch=(), prefetch=0):
        token = [] if self.token is None else [self.token]
        inputs, outputs, ordered = len(operands), len(out_shape), len(token)

        def body(*refs):
            refs = refs[:prefetch] + refs[prefetch + ordered :]
            token_ref = refs[inputs + outputs]
            token_ref[...] = jnp.zeros(token_ref.shape, token_ref.dtype)
            kernel(*refs[: inputs + outputs], *refs[inputs + outputs + 1 :])

        token_spec = pl.BlockSpec((8, 128), lambda *index: (0, 0))
        results = pl.pallas_call(
            body,
            grid_spec=pltpu.PrefetchScalarGridSpec(
                num_scalar_prefetch=prefetch,
                grid=grid,
                in_specs=[pl.BlockSpec(memory_space=pl.ANY)] * ordered + list(in_specs),
                out_specs=list(out_specs) + [token_spec],
                scratch_shapes=list(scratch),
            ),
            out_shape=list(out_shape) + [struct((8, 128), jnp.float32)],
            compiler_params=pltpu.CompilerParams(vmem_limit_bytes=56 << 20),
        )(*operands[:prefetch], *token, *operands[prefetch:])
        self.token = results[-1]
        return results[:-1]


def shift_frames(block, frame_count, shift):
    if shift % frame_count == 0:
        return block
    pairs = [(index, (index + shift) % frame_count) for index in range(frame_count)]
    return lax.ppermute(block, "frame", pairs)


def rows_to_frames(rows, frame_count, frame_index):
    part = rows.shape[0] // frame_count
    slots = []
    for shift in range(frame_count):
        owner = (frame_index + shift) % frame_count
        block = lax.dynamic_slice_in_dim(rows, owner * part, part, 0)
        slots.append(shift_frames(block, frame_count, shift))
    return slots


def send_back(slots):
    return [shift_frames(slot, len(slots), -shift) for shift, slot in enumerate(slots)]


def swap_bit(block, axis, size, bit):
    pairs = [(index, index ^ (1 << bit)) for index in range(size)]
    return lax.ppermute(block, axis, pairs)


def shuffle_kernel(plan, source_count, flags_ref, *refs):
    sources, outputs = refs[:source_count], refs[source_count:]

    def emit(output, at, rows, terms):
        steps = [step for step in range(ROW_TILE, 65, ROW_TILE) if rows % step == 0]
        step = max(steps, default=rows)

        def some(index, carry):
            def load(term):
                source, start = term
                if steps:
                    return sources[source][pl.ds(pl.multiple_of(start + index * step, ROW_TILE), step)]
                return sources[source][start : start + step]

            value = load(terms[0])
            if len(terms) > 1:
                total = value.astype(jnp.float32)
                for term in terms[1:]:
                    total = total + load(term).astype(jnp.float32)
                value = total.astype(output.dtype)
            if steps:
                output[pl.ds(pl.multiple_of(at + index * step, ROW_TILE), step)] = value
            else:
                output[at : at + step] = value
            return carry

        if rows // step == 1:
            some(0, 0)
        else:
            lax.fori_loop(0, rows // step, some, 0)

    for output, segments in zip(outputs, plan):
        at = 0
        for rows, flag, *choices in segments:
            for value, terms in enumerate(choices):

                @pl.when(flags_ref[flag] == value)
                def _():
                    emit(output, at, rows, terms)

            at += rows


def shuffle(order, requests):
    sources, plan, counts = [], [], []
    for own_sources, own_plan in requests:
        base = len(sources)

        def lift(terms):
            return tuple((source + base, start) for source, start in terms)

        plan += [
            [(rows, flag, lift(low), lift(high)) for rows, flag, low, high in out] for out in own_plan
        ]
        sources += own_sources
        counts.append(len(own_plan))
    features = sources[0].shape[1]
    shapes = [struct((sum(segment[0] for segment in out), features), jnp.bfloat16) for out in plan]
    results = order.run(
        functools.partial(shuffle_kernel, plan, len(sources)),
        [order.flags, *sources],
        [SMEM] + [VMEM] * len(sources),
        [VMEM] * len(plan),
        shapes,
    )
    outputs = []
    for count in counts:
        outputs.append(results[:count])
        results = results[count:]
    return outputs


def split_plan(rows, flag, left, right):
    half = rows // 2
    low = ((left[0], left[1]), (right[0], right[1]))
    high = ((left[0], left[1] + half), (right[0], right[1] + half))
    return [[(half, flag, high, low)], [(half, flag, low, high)]]


def join_plan(rows, flag, own, arrived):
    return [(rows, flag, (own,), (arrived,)), (rows, flag, (arrived,), (own,))]


def sum_order(piece, sizes, rows):
    batch_bits, frame_bits = (size.bit_length() - 1 for size in sizes)
    batch, frame = divmod(piece, sizes[1])
    wide = list(range(1, batch_bits))
    size = rows // 4
    start = (batch & 1) * 2 * size + (frame & 1) * size
    for bit in wide[::-1] if frame & 1 else wide:
        size //= 2
        start += ((batch >> bit) & 1) * size
    for bit in range(1, frame_bits):
        size //= 2
        start += ((frame >> bit) & 1) * size
    return start


def sum_steps(kept, sent, sizes, spread):
    batch_bits, frame_bits = (size.bit_length() - 1 for size in sizes)
    wide = list(range(1, batch_bits))
    ways = (wide, wide[::-1])

    def over_batch(block, bit):
        return swap_bit(block, "batch", sizes[0], bit)

    def over_frame(block, bit):
        return swap_bit(block, "frame", sizes[1], bit)

    (arrived,) = yield [over_batch(sent, 0)]
    rows = kept.shape[0] // 2
    sources = [kept, arrived]
    pairs = [((0, 0), (1, 0)), ((0, rows), (1, rows))]
    for level in range(len(wide)):
        plan = []
        for (left, right), way in zip(pairs, ways):
            plan += split_plan(rows, way[level], left, right)
        first_out, first_kept, second_out, second_kept = yield sources, plan
        moved = yield [over_batch(first_out, ways[0][level]), over_batch(second_out, ways[1][level])]
        sources = [first_kept, moved[0], second_kept, moved[1]]
        pairs = [((0, 0), (1, 0)), ((2, 0), (3, 0))]
        rows //= 2
    flag = batch_bits
    plan = [[(rows, flag, pairs[1], pairs[0])], [(rows, flag, pairs[0], pairs[1])]]
    for bit in range(frame_bits):
        if bit:
            rows //= 2
            plan = split_plan(2 * rows, flag + bit, (0, 0), (1, 0))
        sent, kept = yield sources, plan
        (arrived,) = yield [over_frame(sent, bit)]
        sources = [kept, arrived]
    (block,) = yield sources, [[(rows, flag, ((0, 0), (1, 0)), ((0, 0), (1, 0)))]]
    if not spread:
        return block
    for bit in range(frame_bits)[:0:-1]:
        (arrived,) = yield [over_frame(block, bit)]
        (block,) = yield [block, arrived], [join_plan(rows, flag + bit, (0, 0), (1, 0))]
        rows *= 2
    (arrived,) = yield [over_frame(block, 0)]
    plan = [[(rows, flag, ((0, 0),), ((1, 0),))], [(rows, flag, ((1, 0),), ((0, 0),))]]
    blocks = yield [block, arrived], plan
    for level in range(len(wide))[::-1]:
        moved = yield [over_batch(block, way[level]) for block, way in zip(blocks, ways)]
        sources = [blocks[0], moved[0], blocks[1], moved[1]]
        plan = [join_plan(rows, ways[0][level], (0, 0), (1, 0))]
        plan += [join_plan(rows, ways[1][level], (2, 0), (3, 0))]
        if level == 0:
            plan = [plan[0] + plan[1]]
        blocks = yield sources, plan
        rows *= 2
    (arrived,) = yield [over_batch(blocks[0], 0)]
    return blocks[0], arrived


class Flight:
    def __init__(self, steps):
        self.steps, self.result = steps, None
        self.moved = next(steps)

    def send(self, value):
        try:
            return self.steps.send(value)
        except StopIteration as stop:
            self.result = stop.value
            return None


def advance(order, *flights):
    active, requests = [], []
    for flight in flights:
        request = flight.send(flight.moved) if flight.result is None else None
        if request is not None:
            active.append(flight)
            requests.append(request)
    if requests:
        for flight, outputs in zip(active, shuffle(order, requests)):
            flight.moved = flight.send(outputs)


def deliver_kernel(ranges, count, flags_ref, *refs):
    own_ref, arrived_ref = refs[0], refs[1]
    outputs = refs[len(refs) - len(ranges) :]
    whole = len(refs) - len(ranges) == 1
    step = pl.program_id(0)
    own = (step < count // 2) == (flags_ref[0] == 0)
    for output, (first, last, _) in zip(outputs, ranges):
        here = (step >= first) & (step < last)

        @pl.when(here if whole else here & own)
        def _():
            output[...] = own_ref[...].astype(output.dtype)

        if not whole:

            @pl.when(here & jnp.logical_not(own))
            def _():
                output[...] = arrived_ref[...].astype(output.dtype)


def deliver(order, sources, ranges, block):
    features = sources[0].shape[1]
    count = sum(source.shape[0] for source in sources) // block
    half = count // 2
    per = features // block

    def place(core, step):
        if len(sources) == 1:
            return step
        return jnp.where(core == 0, jnp.minimum(step, half - 1), jnp.maximum(step - half, 0))

    def spot(first, last, wide):
        def index(step, flags):
            at = jnp.clip(step - first, 0, last - first - 1)
            return (at % per, at // per) if wide else (at, 0)

        return pl.BlockSpec((block, features), index)

    def shape(first, last, wide):
        rows = (last - first) * block
        return (features, rows) if wide else (rows, features)

    specs = [
        pl.BlockSpec((block, features), lambda step, flags: (place(flags[0], step), 0)),
        pl.BlockSpec((block, features), lambda step, flags: (place(1 - flags[0], step), 0)),
    ]
    return order.run(
        functools.partial(deliver_kernel, ranges, count),
        [order.flags, *sources],
        specs[: len(sources)],
        [spot(*item) for item in ranges],
        [struct(shape(*item), jnp.float32) for item in ranges],
        grid=(count,),
        prefetch=1,
    )


def contract(x,y,dims):
    return lax.dot_general(x,y,((dims[0:1],dims[1:2]),((),())),preferred_element_type=jnp.float32)

def widen_rows(values, wide):
    rows, width = values.shape
    if wide == rows:
        return values
    return jnp.concatenate([values, jnp.zeros((wide - rows, width), values.dtype)])


def head_halves(width):
    lane = lax.broadcasted_iota(jnp.int32, (1, width), 1)
    return [lane < width // 2, lane >= width // 2]

def space_forward_kernel(scale, tile, column_ref, row_ref, q_ref, k_ref, v_ref, mixture_ref, total_ref, bias_ref, k_wide, v_wide):
    rows, width = q_ref.shape
    wide = k_wide.shape[0]
    @pl.when(pl.program_id(0) == 0)
    def _():
        bias_ref[...] = jnp.where(column_ref[...] == row_ref[...], 0.0, -1e30)
        if wide > rows:
            k_wide[rows:] = jnp.zeros((wide - rows, width), k_wide.dtype)
            v_wide[rows:] = jnp.zeros((wide - rows, width), v_wide.dtype)
    k_wide[:rows] = k_ref[...]
    v_wide[:rows] = v_ref[...]
    halves = head_halves(width)
    zero, one = jnp.zeros((), q_ref.dtype), jnp.ones((), q_ref.dtype)
    filled = [jnp.where(half, v_wide[...], one) for half in halves]
    for start in range(0, rows, tile):
        span = slice(start, start + tile)
        outs, tops = [], []
        for half, values in zip(halves, filled):
            queries = jnp.where(half, q_ref[span], zero)
            scores = contract(queries, k_wide[...], (1, 1)) * (scale * LOG2E) + bias_ref[span]
            top = jnp.max(scores, axis=1, keepdims=True)
            weights = jnp.exp2(scores - top)
            outs.append(contract(weights.astype(jnp.bfloat16), values, (1, 0)))
            tops.append(top)
        mass = pltpu.roll(jnp.where(halves[0], outs[1], outs[0]), width // 2, 1)
        mixture = jnp.where(halves[0], outs[0], outs[1]) / mass
        mixture_ref[span] = mixture.astype(mixture_ref.dtype)
        total_ref[span] = jnp.where(halves[0], tops[0], tops[1]) + jnp.log2(mass)


def space_specs(rows, features):
    pairs = HEADS // 2
    width = features // pairs
    wide = round_up(rows, 128)
    fixed = [pl.BlockSpec((rows, 1), lambda i: (0, 0)), pl.BlockSpec((1, wide), lambda i: (0, 0))]
    blocks = [pl.BlockSpec((rows, width), lambda i, o=o: (0, o + i)) for o in (0, pairs, 2 * pairs)]
    out = pl.BlockSpec((rows, width), lambda i: (0, i))
    scratch = [pltpu.VMEM((rows, wide), jnp.float32)]
    scratch += [pltpu.VMEM((wide, width), jnp.bfloat16)] * 2
    return pairs, (features // HEADS) ** -0.5, fixed + blocks, out, scratch


def clip_lines(clip):
    rows = clip.shape[0]
    row = jnp.pad(clip, (0, round_up(rows, 128) - rows), constant_values=-2)
    return clip[:, None], row[None]


def space_forward(order, qkv, clip, features):
    rows = qkv.shape[0]
    pairs, scale, specs, out, scratch = space_specs(rows, features)
    return order.run(
        functools.partial(space_forward_kernel, scale, rows),
        [*clip_lines(clip), qkv, qkv, qkv],
        specs,
        [out, out],
        [struct((rows, features), jnp.bfloat16), struct((rows, features), jnp.float32)],
        grid=(pairs,),
        scratch=scratch,
    )


def space_backward_kernel(scale, tile, column_ref, row_ref, q_ref, k_ref, v_ref, mixture_ref, total_ref, grad_ref, dq_ref, dk_ref, dv_ref, bias_ref, q_wide, g_wide):
    rows, width = q_ref.shape
    wide = q_wide.shape[0]
    @pl.when(pl.program_id(0) == 0)
    def _():
        bias_ref[...] = jnp.where(column_ref[...] == row_ref[...], 0.0, -1e30)
        if wide > rows:
            q_wide[rows:] = jnp.zeros((wide - rows, width), q_wide.dtype)
            g_wide[rows:] = jnp.zeros((wide - rows, width), g_wide.dtype)
    q_wide[:rows] = q_ref[...]
    g_wide[:rows] = grad_ref[...]
    halves = head_halves(width)
    zero = jnp.zeros((), q_ref.dtype)
    product = grad_ref[...].astype(jnp.float32) * mixture_ref[...].astype(jnp.float32)
    sums = [jnp.sum(jnp.where(half, product, 0.0), axis=1, keepdims=True) for half in halves]
    delta = widen_rows(jnp.where(halves[0], sums[0], sums[1]), wide).T
    total = widen_rows(total_ref[...], wide).T
    dq_parts = [None, None]
    for start in range(0, rows, tile):
        span = slice(start, start + tile)
        dk, dv = [], []
        for index, half in enumerate(halves):
            at = index * (width // 2)
            keys = jnp.where(half, k_ref[span], zero)
            values = jnp.where(half, v_ref[span], zero)
            scores = contract(keys, q_wide[...], (1, 1)) * (scale * LOG2E)
            weights = jnp.exp2(scores + (bias_ref[span] - total[at:at + 1]))
            slopes = contract(values, g_wide[...], (1, 1))
            slopes = (weights * (slopes - delta[at:at + 1])).astype(jnp.bfloat16)
            dv.append(contract(weights.astype(jnp.bfloat16), g_wide[...], (1, 0)))
            dk.append(contract(slopes, q_wide[...], (1, 0)))
            part = contract(slopes, keys, (0, 0))
            dq_parts[index] = part if start == 0 else dq_parts[index] + part
        dk_ref[span] = (jnp.where(halves[0], dk[0], dk[1]) * scale).astype(dk_ref.dtype)
        dv_ref[span] = jnp.where(halves[0], dv[0], dv[1]).astype(dv_ref.dtype)
    dq_ref[...] = ((dq_parts[0] + dq_parts[1])[:rows] * scale).astype(dq_ref.dtype)

def space_backward(order, qkv, mixture, total, grad, clip, features):
    rows = qkv.shape[0]
    pairs, scale, specs, out, scratch = space_specs(rows, features)
    return order.run(
        functools.partial(space_backward_kernel, scale, rows),
        [*clip_lines(clip), qkv, qkv, qkv, mixture, total, grad],
        specs + [out] * 3,
        [out] * 3,
        [struct((rows, features), jnp.bfloat16)] * 3,
        grid=(pairs,),
        scratch=scratch,
    )


def norm_parts(values):
    average = jnp.mean(values, axis=1, keepdims=True)
    centered = values - average
    spread = lax.rsqrt(jnp.mean(centered * centered, axis=1, keepdims=True) + 1e-06)
    return centered * spread, spread
def norm_back(grad, normed, spread, gain):
    scaled = grad * gain
    return spread * (scaled - jnp.mean(scaled, axis=1, keepdims=True) - normed * jnp.mean(scaled * normed, axis=1, keepdims=True))
def column_sum(values):
    return jnp.sum(values, axis=0, keepdims=True)

def feed_kernel(chunks, x1_ref, mixture_ref, dz_ref, so_ref, fi_ref, fo_ref, fb_ref, vec_ref,
                out_ref, dx2_ref, dys_ref, dos_ref, grad_ref, gfb_ref, gvec_ref,
                x2_s, a3_s, a3t_s, acc_s, da_s, g_s, dh_s):
    step = pl.program_id(0)
    rows = x1_ref.shape[0]
    @pl.when(step == 0)
    def _():
        x2 = x1_ref[...] + contract(mixture_ref[...], so_ref[...], (1, 0)) + vec_ref[9:10]
        x2_s[...] = x2
        normed, _ = norm_parts(x2)
        a3 = (normed * vec_ref[10:11] + vec_ref[11:12]).astype(jnp.bfloat16)
        a3_s[...] = a3
        a3t_s[...] = a3.T
        acc_s[...] = x2 + vec_ref[12:13]
        da_s[...] = jnp.zeros_like(da_s)
    part = rows // chunks
    for chunk in range(chunks):
        span = slice(chunk * part, (chunk + 1) * part)
        hidden = contract(a3_s[span], fi_ref[...], (1, 0)) + fb_ref[...]
        cdf = 0.5 + 0.5 * lax.erf(hidden * math.sqrt(0.5))
        slope = cdf + hidden * jnp.exp(hidden * hidden * -0.5) * (1.0 / math.sqrt(2.0 * math.pi))
        active = (hidden * cdf).astype(jnp.bfloat16)
        g_s[span] = active
        dh = (contract(dz_ref[span], fo_ref[...], (1, 1)) * slope).astype(jnp.bfloat16)
        dh_s[span] = dh
        acc_s[span] += contract(active, fo_ref[...], (1, 0))
        da_s[span] += contract(dh, fi_ref[...], (1, 1))
    grad_ref[0] = contract(a3t_s[...], dh_s[...], (1, 0)).astype(grad_ref.dtype)
    grad_ref[1] = contract(g_s[...], dz_ref[...], (0, 0)).astype(grad_ref.dtype)
    gfb_ref[...] = column_sum(dh_s[...].astype(jnp.float32))
    @pl.when(step == pl.num_programs(0) - 1)
    def _():
        out_ref[...] = acc_s[...].astype(out_ref.dtype)
        normed, spread = norm_parts(x2_s[...])
        grad = da_s[...]
        dz = dz_ref[...].astype(jnp.float32)
        dx2 = dz + norm_back(grad, normed, spread, vec_ref[10:11])
        dx2_ref[...] = dx2
        dys = dx2.astype(jnp.bfloat16)
        dys_ref[...] = dys
        dos_ref[...] = contract(dys, so_ref[...], (1, 1)).astype(dos_ref.dtype)
        gvec_ref[0:1] = column_sum(grad * normed)
        gvec_ref[1:2] = column_sum(grad)
        gvec_ref[2:3] = column_sum(dz)
        gvec_ref[3:4] = column_sum(dys.astype(jnp.float32))
        gvec_ref[4:8] = jnp.zeros((4, gvec_ref.shape[1]), jnp.float32)

def feed_block(order, x1, mixture, dz, space_packed, fi, fo, fb, vec, tile, chunks):
    rows, features = x1.shape
    hidden = fi.shape[1]
    whole = pl.BlockSpec((rows, features), lambda j: (0, 0))
    fi_spec = pl.BlockSpec((features, tile), lambda j: (0, j))
    fo_spec = pl.BlockSpec((tile, features), lambda j: (j, 0))
    fb_spec = pl.BlockSpec((1, tile), lambda j: (0, j))
    last = space_packed.shape[1] // features - 1
    low, full = jnp.bfloat16, jnp.float32
    return order.run(
        functools.partial(feed_kernel, chunks),
        [x1, mixture, dz, space_packed, fi, fo, fb, vec],
        [whole, whole, whole]
        + [pl.BlockSpec((features, features), lambda j: (0, last)), fi_spec, fo_spec, fb_spec]
        + [pl.BlockSpec(vec.shape, lambda j: (0, 0))],
        [whole] * 4
        + [pl.BlockSpec((2, tile, features), lambda j: (0, j, 0)), fb_spec]
        + [pl.BlockSpec((8, features), lambda j: (0, 0))],
        [
            struct((rows, features), low),
            struct((rows, features), full),
            struct((rows, features), low),
            struct((rows, features), low),
            struct((2, *fo.shape), low),
            struct((1, hidden), full),
            struct((8, features), full),
        ],
        grid=(hidden // tile,),
        scratch=[
            pltpu.VMEM((rows, features), full),
            pltpu.VMEM((rows, features), low),
            pltpu.VMEM((features, rows), low),
            pltpu.VMEM((rows, features), full),
            pltpu.VMEM((rows, features), full),
            pltpu.VMEM((rows, tile), low),
            pltpu.VMEM((rows, tile), low),
        ],
    )


def gather_rows(count, frame, slots, rows_s):
    part = slots[0].shape[0]
    for shift in range(count):
        owner = lax.rem(frame + shift, count)
        rows_s[pl.ds(pl.multiple_of(owner * part, ROW_TILE), part)] = slots[shift][...]


def middle_kernel(count, frame_flag, flags_ref, token_ref, *refs):
    slots, (to_ref, sp_ref, vec_ref) = refs[:count], refs[count : count + 3]
    mixture_ref, x1_ref, a2_ref, qkv_ref = refs[count + 3 :]
    rows, features = token_ref.shape
    gather_rows(count, flags_ref[frame_flag], slots, mixture_ref)
    number = lax.broadcasted_iota(jnp.int32, (rows, 1), 0)
    branch = contract(mixture_ref[...], to_ref[...], (1, 0)) + vec_ref[4:5]
    x1 = token_ref[...].astype(jnp.float32) + jnp.where(number < PATCHES, branch, 0.0)
    x1_ref[...] = x1
    normed, _ = norm_parts(x1)
    a2 = (normed * vec_ref[5:6] + vec_ref[6:7]).astype(jnp.bfloat16)
    a2_ref[...] = a2
    for third in range(3):
        span = slice(third * features, (third + 1) * features)
        joined = contract(a2, sp_ref[:, span], (1, 0))
        if third != 1:
            joined = joined + vec_ref[7 + third // 2 : 8 + third // 2]
        qkv_ref[:, span] = joined.astype(jnp.bfloat16)


def project_specs(features, vec):
    return [
        pl.BlockSpec((features, features), lambda i: (0, 3)),
        pl.BlockSpec((features, 3 * features), lambda i: (0, 0)),
        pl.BlockSpec(vec.shape, lambda i: (0, 0)),
    ]


def middle_forward(order, tokens, slots, time_packed, space_packed, vec):
    rows, features = tokens.shape
    low = jnp.bfloat16
    return order.run(
        functools.partial(middle_kernel, len(slots), order.flags.shape[0] - 1),
        [order.flags, tokens, *slots, time_packed, space_packed, vec],
        [SMEM] + [VMEM] * (len(slots) + 1) + project_specs(features, vec),
        [VMEM] * 4,
        [
            struct((rows, features), low),
            struct((rows, features), jnp.float32),
            struct((rows, features), low),
            struct((rows, 3 * features), low),
        ],
        grid=(1,),
    )


def middle_back_kernel(
    count, frame_flag, flags_ref, dq_ref, dk_ref, dv_ref, x1_ref, dx2_ref, to_ref, sp_ref, vec_ref, *refs
):
    dx1_ref, dyt_ref, sums_ref = refs[:3]
    slots, rows_s = refs[3 : 3 + count], refs[3 + count]
    rows, features = x1_ref.shape
    grad = 0.0
    for third, piece in enumerate((dq_ref, dk_ref, dv_ref)):
        span = slice(third * features, (third + 1) * features)
        grad = grad + contract(piece[...], sp_ref[:, span], (1, 1))
    normed, spread = norm_parts(x1_ref[...])
    dx1 = dx2_ref[...] + norm_back(grad, normed, spread, vec_ref[5:6])
    dx1_ref[...] = dx1
    number = lax.broadcasted_iota(jnp.int32, (rows, 1), 0)
    dyt = jnp.where(number < PATCHES, dx1, 0.0).astype(jnp.bfloat16)
    dyt_ref[...] = dyt
    rows_s[...] = contract(dyt, to_ref[...], (1, 1)).astype(rows_s.dtype)
    part = rows // count
    for shift in range(count):
        owner = lax.rem(flags_ref[frame_flag] + shift, count)
        slots[shift][...] = rows_s[pl.ds(pl.multiple_of(owner * part, ROW_TILE), part)]
    sums_ref[0:1] = column_sum(grad * normed)
    sums_ref[1:2] = column_sum(grad)
    sums_ref[2:3] = column_sum(dq_ref[...].astype(jnp.float32))
    sums_ref[3:4] = column_sum(dv_ref[...].astype(jnp.float32))
    sums_ref[4:5] = column_sum(dyt.astype(jnp.float32))
    sums_ref[5:8] = jnp.zeros((3, features), jnp.float32)


def middle_backward(order, count, dq, dk, dv, x1, dx2, time_packed, space_packed, vec):
    rows, features = x1.shape
    low, full = jnp.bfloat16, jnp.float32
    results = order.run(
        functools.partial(middle_back_kernel, count, order.flags.shape[0] - 1),
        [order.flags, dq, dk, dv, x1, dx2, time_packed, space_packed, vec],
        [SMEM] + [VMEM] * 5 + project_specs(features, vec),
        [VMEM] * (3 + count),
        [struct((rows, features), full), struct((rows, features), low), struct((8, features), full)]
        + [struct((rows // count, features), low)] * count,
        grid=(1,),
        scratch=[pltpu.VMEM((rows, features), low)],
    )
    return results[0], results[1], results[2], results[3:]


def put_rows(core_ref, kept_ref, sent_ref, sizes, at, value):
    half = kept_ref.shape[0]
    low = value.astype(kept_ref.dtype)
    part = 2 * half // (sizes[0] * sizes[1]) if sizes else math.gcd(half, low.shape[0])
    for offset in range(0, low.shape[0], part):
        start = at + offset
        if sizes:
            start = sum_order(start // part, sizes, 2 * half)
        piece = low[offset : offset + part]
        span = slice(start % half, start % half + part)

        @pl.when(core_ref[0] == start // half)
        def _():
            kept_ref[span] = piece

        @pl.when(core_ref[0] != start // half)
        def _():
            sent_ref[span] = piece


def fill_rows(pieces, rows, features):
    used = sum(piece.shape[0] for piece in pieces)
    return jnp.concatenate([*pieces, jnp.zeros((rows - used, features), jnp.float32)])


def middle_weights_kernel(
    sizes, flags_ref, a2_ref, dq_ref, dk_ref, dv_ref, time_ref, dyt_ref, space_ref, dys_ref, sums_ref, feed_ref,
    bias_ref, kept_ref, sent_ref
):
    features = a2_ref.shape[1]
    turned = a2_ref[...].T
    put = functools.partial(put_rows, flags_ref, kept_ref, sent_ref, sizes)
    for third, piece in enumerate((dq_ref, dk_ref, dv_ref)):
        put(third * features, contract(turned, piece[...], (1, 0)))
    put(3 * features, contract(time_ref[...], dyt_ref[...], (0, 0)))
    put(4 * features, contract(space_ref[...], dys_ref[...], (0, 0)))
    bias = bias_ref[...]
    lines = [bias[:, at : at + features] for at in range(0, bias.shape[1], features)]
    pieces = [sums_ref[0:4], feed_ref[3:4], feed_ref[0:3], *lines]
    put(5 * features, fill_rows(pieces, 2 * kept_ref.shape[0] - 5 * features, features))


def middle_weights(order, sizes, *operands):
    features = operands[0].shape[1]
    half = struct((round_up(5 * features + 16, 512) // 2, features), jnp.bfloat16)
    return order.run(
        functools.partial(middle_weights_kernel, sizes),
        [order.flags, *operands],
        [SMEM] + [VMEM] * len(operands),
        [VMEM] * 2,
        [half, half],
    )


CHUNK = 16
def head_map(features, lanes=128):
    head = jnp.arange(features, dtype=jnp.int32) // (features // HEADS)
    return (head[:, None] == jnp.arange(lanes, dtype=jnp.int32)[None]).astype(jnp.bfloat16)

def pair_sums(left, right, gather_ref, pair_s):
    count = len(left)
    for f in range(count):
        for g in range(count):
            at = (f * count + g) * CHUNK
            pair_s[at:at + CHUNK] = (left[f] * right[g]).astype(jnp.bfloat16)
    return contract(pair_s[...], gather_ref[...], (1, 0))

def time_forward_kernel(count, scale, *refs):
    slots, (tp_ref, vec_ref, gather_ref, spread_ref) = refs[:count], refs[count:count + 4]
    outs, (qkv_ref, prob_ref, a1_ref) = refs[count + 4:2 * count + 4], refs[2 * count + 4:2 * count + 7]
    pair_s, weight_s = refs[2 * count + 7:]
    part, features = slots[0].shape
    for s in range(count):
        normed, _ = norm_parts(slots[s][...].astype(jnp.float32))
        a1_ref[s * part:(s + 1) * part] = (normed * vec_ref[0:1] + vec_ref[1:2]).astype(jnp.bfloat16)
    for third in range(3):
        span = slice(third * features, (third + 1) * features)
        joined = contract(a1_ref[...], tp_ref[:, span], (1, 0))
        if third != 1:
            joined = joined + vec_ref[2 + third // 2:3 + third // 2]
        qkv_ref[:, span] = joined.astype(jnp.bfloat16)

    def chunk_step(index, carry):
        def rows_of(s, third):
            start = pl.multiple_of(s * part + index * CHUNK, CHUNK)
            return qkv_ref[pl.ds(start, CHUNK), third * features:(third + 1) * features].astype(jnp.float32)
        queries, keys, values = ([rows_of(s, third) for s in range(count)] for third in range(3))
        scores = pair_sums(queries, keys, gather_ref, pair_s) * (scale * LOG2E)
        place = pl.ds(pl.multiple_of(index * CHUNK, CHUNK), CHUNK)
        for f in range(count):
            row = [scores[(f * count + g) * CHUNK:(f * count + g + 1) * CHUNK] for g in range(count)]
            top = functools.reduce(jnp.maximum, row)
            raised = [jnp.exp2(item - top) for item in row]
            mass = functools.reduce(jnp.add, raised)
            for g in range(count):
                weight = raised[g] / mass
                prob_ref[f * count + g, place] = weight
                at = (f * count + g) * CHUNK
                weight_s[at:at + CHUNK] = weight.astype(jnp.bfloat16)
        wide = contract(weight_s[...], spread_ref[...], (1, 0))
        for f in range(count):
            total = 0.0
            for g in range(count):
                at = (f * count + g) * CHUNK
                total = total + wide[at:at + CHUNK] * values[g]
            outs[f][place] = total.astype(jnp.bfloat16)
        return carry
    lax.fori_loop(0, part // CHUNK, chunk_step, 0)

def time_forward(order, slots, time_packed, vec):
    count = len(slots)
    part, features = slots[0].shape
    gather = head_map(features)
    low, full = jnp.bfloat16, jnp.float32
    results = order.run(
        functools.partial(time_forward_kernel, count, (features // HEADS) ** -0.5),
        [*slots, time_packed, vec, gather, gather.T],
        [VMEM] * count + [pl.BlockSpec((features, 3 * features), lambda i: (0, 0)), VMEM, VMEM, VMEM],
        [VMEM] * (count + 3),
        [struct((part, features), low)] * count
        + [
            struct((count * part, 3 * features), low),
            struct((count * count, part, 128), full),
            struct((count * part, features), low),
        ],
        grid=(1,),
        scratch=[
            pltpu.VMEM((count * count * CHUNK, features), low),
            pltpu.VMEM((count * count * CHUNK, 128), low),
        ],
    )
    return results[:count], results[count], results[count + 1], results[count + 2]


def time_backward_kernel(count, scale, flags_ref, *refs):
    grads, slots = refs[:count], refs[count : 2 * count]
    qkv_ref, prob_ref, a1_ref, gather_ref, spread_ref, tp_ref, vec_ref, other_ref = refs[2 * count : 2 * count + 8]
    refs = refs[2 * count + 8 :]
    outs, (kept_ref, sent_ref, dqkv_ref, pair_s, weight_s) = refs[:count], refs[count:]
    part, features = grads[0].shape
    def chunk_step(index, carry):
        place = pl.ds(pl.multiple_of(index * CHUNK, CHUNK), CHUNK)
        def rows_of(s, third):
            start = pl.multiple_of(s * part + index * CHUNK, CHUNK)
            return qkv_ref[pl.ds(start, CHUNK), third * features:(third + 1) * features].astype(jnp.float32)
        queries, keys, values = ([rows_of(s, third) for s in range(count)] for third in range(3))
        outer = [grads[s][place].astype(jnp.float32) for s in range(count)]
        slopes = pair_sums(outer, values, gather_ref, pair_s)
        size = count * count * CHUNK
        for f in range(count):
            row = [slopes[(f * count + g) * CHUNK:(f * count + g + 1) * CHUNK] for g in range(count)]
            weights = [prob_ref[f * count + g, place] for g in range(count)]
            delta = functools.reduce(jnp.add, [w * s for w, s in zip(weights, row)])
            for g in range(count):
                at = (f * count + g) * CHUNK
                weight_s[at:at + CHUNK] = weights[g].astype(jnp.bfloat16)
                weight_s[size + at:size + at + CHUNK] = (weights[g] * (row[g] - delta)).astype(jnp.bfloat16)
        wide = contract(weight_s[...], spread_ref[...], (1, 0))
        for s in range(count):
            dq, dk, dv = 0.0, 0.0, 0.0
            for t in range(count):
                forth, back = (s * count + t) * CHUNK, (t * count + s) * CHUNK
                dq = dq + wide[size + forth:size + forth + CHUNK] * keys[t]
                dk = dk + wide[size + back:size + back + CHUNK] * queries[t]
                dv = dv + wide[back:back + CHUNK] * outer[t]
            start = pl.ds(pl.multiple_of(s * part + index * CHUNK, CHUNK), CHUNK)
            for third, value in enumerate((dq * scale, dk * scale, dv)):
                dqkv_ref[start, third * features:(third + 1) * features] = value.astype(jnp.bfloat16)
        return carry
    lax.fori_loop(0, part // CHUNK, chunk_step, 0)
    a1t = a1_ref[...].T
    put = functools.partial(put_rows, flags_ref, kept_ref, sent_ref, None)
    for third in range(3):
        span = slice(third * features, (third + 1) * features)
        put(third * features, contract(a1t, dqkv_ref[:, span], (1, 0)))
    grad = contract(dqkv_ref[...], tp_ref[...], (1, 1))
    gain, shift = 0.0, 0.0
    for s in range(count):
        piece = grad[s * part : (s + 1) * part]
        normed, spread = norm_parts(slots[s][...].astype(jnp.float32))
        outs[s][...] = norm_back(piece, normed, spread, vec_ref[0:1]).astype(jnp.bfloat16)
        gain = gain + column_sum(piece * normed)
        shift = shift + column_sum(piece)
    sums = [
        gain,
        shift,
        column_sum(dqkv_ref[:, :features].astype(jnp.float32)),
        column_sum(dqkv_ref[:, 2 * features :].astype(jnp.float32)),
        other_ref[4:5],
    ]
    put(3 * features, fill_rows(sums, 2 * kept_ref.shape[0] - 3 * features, features))


def time_backward(order, grads, slots, qkv, prob, a1, time_packed, vec, other):
    count = len(grads)
    part, features = grads[0].shape
    gather = head_map(features)
    low = jnp.bfloat16
    half = struct((round_up(3 * features + 16, 512) // 2, features), low)
    results = order.run(
        functools.partial(time_backward_kernel, count, (features // HEADS) ** -0.5),
        [order.flags, *grads, *slots, qkv, prob, a1, gather, gather.T, time_packed, vec, other],
        [SMEM] + [VMEM] * (2 * count + 5)
        + [pl.BlockSpec((features, 3 * features), lambda i: (0, 0)), VMEM, VMEM],
        [VMEM] * (count + 2),
        [struct((part, features), low)] * count + [half, half],
        grid=(1,),
        scratch=[
            pltpu.VMEM(qkv.shape, low),
            pltpu.VMEM((count * count * CHUNK, features), low),
            pltpu.VMEM((2 * count * count * CHUNK, 128), low),
        ],
    )
    return results[:count], results[count], results[count + 1]


def last_kernel(count, frame_flag, flags_ref, first_ref, *refs):
    slots, out_ref, rows_s = refs[:count], refs[count], refs[count + 1]
    gather_rows(count, flags_ref[frame_flag], slots, rows_s)
    rows = out_ref.shape[1]
    out_ref[0] = (first_ref[...] + rows_s[...].astype(jnp.float32))[:rows]


def add_branch(order, first, slots, row_count):
    features = first.shape[1]
    return order.run(
        functools.partial(last_kernel, len(slots), order.flags.shape[0] - 1),
        [order.flags, first, *slots],
        [SMEM] + [VMEM] * (len(slots) + 1),
        [VMEM],
        [struct((1, row_count, features), jnp.float32)],
        scratch=[pltpu.VMEM(first.shape, jnp.bfloat16)],
    )[0]


def body(
    tokens,
    size_tag,
    cotangent,
    time_project,
    time_output,
    time_vector,
    space_project,
    space_output,
    space_vector,
    feed_inner,
    feed_bias,
    feed_outer,
    feed_vector,
):
    frame_count = lax.axis_size("frame")
    batch_count = lax.axis_size("batch")
    sizes = (batch_count, frame_count)
    frame_index = lax.axis_index("frame")
    batch_index = lax.axis_index("batch")
    flags = [(batch_index >> bit) & 1 for bit in range(batch_count.bit_length() - 1)]
    flags += [(frame_index >> bit) & 1 for bit in range(frame_count.bit_length() - 1)]
    order = Order(jnp.stack([*flags, frame_index]).astype(jnp.int32))
    features = tokens.shape[2]
    row_count = tokens.shape[1]
    part = round_up(-(-PATCHES // frame_count), ROW_TILE)
    padded = part * frame_count
    token_rows = jnp.pad(tokens[0], ((0, padded - row_count), (0, 0)))
    grad_result = jnp.pad(cotangent[0], ((0, padded - row_count), (0, 0)))

    vectors = jnp.concatenate(
        [time_vector, space_vector, feed_vector, feed_bias.reshape(-1, time_vector.shape[1])], axis=0
    )
    vectors = lax.all_gather(vectors, "batch", axis=0)
    vec = vectors[:, :13].transpose(1, 0, 2).reshape(13, features).astype(jnp.float32)
    vec = jnp.pad(vec, ((0, 3), (0, 0)))
    feed_bias_row = vectors[:, 13:].reshape(1, -1).astype(jnp.float32)
    time_packed = lax.all_gather(
        jnp.concatenate([time_project, time_output], axis=1), "batch", axis=0, tiled=True
    )
    space_packed = lax.all_gather(
        jnp.concatenate([space_project, space_output], axis=1), "batch", axis=0, tiled=True
    )
    feed_inner_full = lax.all_gather(feed_inner, "batch", axis=0, tiled=True)
    feed_outer_full = lax.all_gather(feed_outer, "batch", axis=0, tiled=True)
    clip = jnp.concatenate(
        [
            jnp.arange(PATCHES, dtype=jnp.int32) // size_tag[0],
            jnp.arange(UNITS, dtype=jnp.int32),
            jnp.full((padded - PATCHES - UNITS,), -1, jnp.int32),
        ]
    )

    slots = rows_to_frames(token_rows, frame_count, frame_index)
    mixture_slots, qkv_time, prob_time, first_input = time_forward(order, slots, time_packed, vec)
    mixture_time, after_time, second_input, qkv_space = middle_forward(
        order, token_rows, send_back(mixture_slots), time_packed, space_packed, vec
    )
    mixture_space, total_space = space_forward(order, qkv_space, clip, features)
    (
        block_out,
        grad_second,
        grad_branch,
        grad_mixture,
        feed_grads,
        grad_feed_bias,
        feed_sums,
    ) = feed_block(
        order,
        after_time,
        mixture_space,
        grad_result,
        space_packed,
        feed_inner_full,
        feed_outer_full,
        feed_bias_row,
        vec,
        tile=features,
        chunks=2,
    )
    feed_total = lax.psum(feed_grads.reshape(-1, features), ("batch", "frame"))
    grad_query, grad_keys, grad_values = space_backward(
        order, qkv_space, mixture_space, total_space, grad_mixture, clip, features
    )
    grad_first, grad_patch, space_sums, grad_slots = middle_backward(
        order,
        frame_count,
        grad_query,
        grad_keys,
        grad_values,
        after_time,
        grad_second,
        time_packed,
        space_packed,
        vec,
    )
    grad_slots = [
        shift_frames(slot, frame_count, shift) for shift, slot in enumerate(grad_slots)
    ]
    space_kept, space_sent = middle_weights(
        order,
        sizes,
        second_input,
        grad_query,
        grad_keys,
        grad_values,
        mixture_time,
        grad_patch,
        mixture_space,
        grad_branch,
        space_sums,
        feed_sums,
        grad_feed_bias,
    )
    space_flight = Flight(sum_steps(space_kept, space_sent, sizes, False))
    input_slots, time_kept, time_sent = time_backward(
        order,
        grad_slots,
        slots,
        qkv_time,
        prob_time,
        first_input,
        time_packed,
        vec,
        space_sums,
    )
    time_flight = Flight(sum_steps(time_kept, time_sent, sizes, True))
    input_slots = send_back(input_slots)
    while space_flight.result is None:
        advance(order, time_flight, space_flight)
    space_total = lax.all_gather(space_flight.result, ("batch", "frame"), axis=0, tiled=True)
    advance(order, time_flight)
    grad_tokens = add_branch(order, grad_first, input_slots, row_count)
    while time_flight.result is None:
        advance(order, time_flight)
    block = 256
    per = features // block
    grad_feed_inner, grad_feed_outer = deliver(
        order, [feed_total], [(0, 4 * per, True), (4 * per, 8 * per, False)], block
    )
    count = 2 * time_flight.result[0].shape[0] // block
    grad_time_project, time_vectors = deliver(
        order, time_flight.result, [(0, 3 * per, True), (3 * per, count, False)], block
    )
    count = space_total.shape[0] // block
    grad_space_project, grad_time_output, grad_space_output, some_vectors = deliver(
        order,
        [space_total],
        [
            (0, 3 * per, True),
            (3 * per, 4 * per, False),
            (4 * per, 5 * per, False),
            (5 * per, count, False),
        ],
        block,
    )
    return (
        block_out[None, :row_count],
        grad_tokens,
        grad_time_project,
        grad_time_output,
        time_vectors[0:5],
        grad_space_project,
        grad_space_output,
        some_vectors[0:5],
        grad_feed_inner,
        some_vectors[8:12].reshape(-1),
        grad_feed_outer,
        some_vectors[5:8],
    )


def solution(mesh):
    placed = (
        P("frame", "batch", None),
        P("batch"),
        P("frame", "batch", None),
        P("batch", None),
        P("batch", None),
        P(None, "batch"),
        P("batch", None),
        P("batch", None),
        P(None, "batch"),
        P("batch", None),
        P("batch"),
        P("batch", None),
        P(None, "batch"),
    )
    return jax.shard_map(
        body,
        mesh=mesh,
        in_specs=placed,
        out_specs=(
            P("frame", "batch", None),
            P("frame", "batch", None),
            P(),
            P(),
            P(),
            P(),
            P(),
            P(),
            P(),
            P(),
            P(),
            P(),
        ),
        check_vma=False,
    )
```

```python
import functools
import math

import jax
import jax.numpy as jnp
from jax import lax
from jax.experimental import pallas as pl
from jax.experimental.pallas import tpu as pltpu
from jax.sharding import PartitionSpec as P

HEADS = 12
UNITS = 4
PATCHES = 784
LOG2E = 1.4426950408889634
ROW_TILE = 16
FEED_BLOCKS = 8


def round_up(count, step):
    return -(-count // step) * step


def struct(shape, dtype):
    return jax.ShapeDtypeStruct(shape, dtype)


VMEM = pl.BlockSpec(memory_space=pltpu.VMEM)
SMEM = pl.BlockSpec(memory_space=pltpu.SMEM)


class Order:
    def __init__(self, flags):
        self.flags = flags
        self.token = None

    def run(
        self, kernel, operands, in_specs, out_specs, out_shape, grid=(), scratch=(), prefetch=0, after=()
    ):
        token = [*after] if self.token is None else [self.token, *after]
        inputs, outputs, ordered = len(operands), len(out_shape), len(token)

        def body(*refs):
            refs = refs[:prefetch] + refs[prefetch + ordered :]
            token_ref = refs[inputs + outputs]
            token_ref[...] = jnp.zeros(token_ref.shape, token_ref.dtype)
            kernel(*refs[: inputs + outputs], *refs[inputs + outputs + 1 :])

        token_spec = pl.BlockSpec((8, 128), lambda *index: (0, 0))
        results = pl.pallas_call(
            body,
            grid_spec=pltpu.PrefetchScalarGridSpec(
                num_scalar_prefetch=prefetch,
                grid=grid,
                in_specs=[pl.BlockSpec(memory_space=pl.ANY)] * ordered + list(in_specs),
                out_specs=list(out_specs) + [token_spec],
                scratch_shapes=list(scratch),
            ),
            out_shape=list(out_shape) + [struct((8, 128), jnp.float32)],
            compiler_params=pltpu.CompilerParams(vmem_limit_bytes=56 << 20),
        )(*operands[:prefetch], *token, *operands[prefetch:])
        self.token = results[-1]
        return results[:-1]


def shift_frames(block, frame_count, shift):
    if shift % frame_count == 0:
        return block
    pairs = [(index, (index + shift) % frame_count) for index in range(frame_count)]
    return lax.ppermute(block, "frame", pairs)


def rows_to_frames(rows, frame_count, frame_index):
    part = rows.shape[0] // frame_count
    slots = []
    for shift in range(frame_count):
        owner = (frame_index + shift) % frame_count
        block = lax.dynamic_slice_in_dim(rows, owner * part, part, 0)
        slots.append(shift_frames(block, frame_count, shift))
    return slots


def send_back(slots):
    return [shift_frames(slot, len(slots), -shift) for shift, slot in enumerate(slots)]


def swap_bit(block, axis, size, bit):
    pairs = [(index, index ^ (1 << bit)) for index in range(size)]
    return lax.ppermute(block, axis, pairs)


def shuffle_kernel(plan, source_count, flags_ref, *refs):
    sources, outputs = refs[:source_count], refs[source_count:]

    def emit(output, at, rows, terms):
        steps = [step for step in range(ROW_TILE, 65, ROW_TILE) if rows % step == 0]
        step = max(steps, default=rows)

        def some(index, carry):
            def load(term):
                source, start = term
                if steps:
                    return sources[source][pl.ds(pl.multiple_of(start + index * step, ROW_TILE), step)]
                return sources[source][start : start + step]

            value = load(terms[0])
            if len(terms) > 1:
                total = value.astype(jnp.float32)
                for term in terms[1:]:
                    total = total + load(term).astype(jnp.float32)
                value = total.astype(output.dtype)
            if steps:
                output[pl.ds(pl.multiple_of(at + index * step, ROW_TILE), step)] = value
            else:
                output[at : at + step] = value
            return carry

        if rows // step == 1:
            some(0, 0)
        else:
            lax.fori_loop(0, rows // step, some, 0)

    for output, segments in zip(outputs, plan):
        at = 0
        for rows, flag, *choices in segments:
            for value, terms in enumerate(choices):

                @pl.when(flags_ref[flag] == value)
                def _():
                    emit(output, at, rows, terms)

            at += rows


def shuffle(order, requests, after):
    sources, plan, counts = [], [], []
    for own_sources, own_plan in requests:
        base = len(sources)

        def lift(terms):
            return tuple((source + base, start) for source, start in terms)

        plan += [
            [(rows, flag, *map(lift, choices)) for rows, flag, *choices in out] for out in own_plan
        ]
        sources += own_sources
        counts.append(len(own_plan))
    features = sources[0].shape[1]
    shapes = [struct((sum(segment[0] for segment in out), features), jnp.bfloat16) for out in plan]
    results = order.run(
        functools.partial(shuffle_kernel, plan, len(sources)),
        [order.flags, *sources],
        [SMEM] + [VMEM] * len(sources),
        [VMEM] * len(plan),
        shapes,
        after=after,
    )
    outputs = []
    for count in counts:
        outputs.append(results[:count])
        results = results[count:]
    return outputs


def split_plan(rows, flag, left, right):
    half = rows // 2
    low = ((left[0], left[1]), (right[0], right[1]))
    high = ((left[0], left[1] + half), (right[0], right[1] + half))
    return [[(half, flag, high, low)], [(half, flag, low, high)]]


def join_plan(rows, flag, own, arrived):
    return [(rows, flag, (own,), (arrived,)), (rows, flag, (arrived,), (own,))]


def frame_parts(rows, frame_count, flag, terms_at):
    part = rows // frame_count
    return [
        [
            (part, flag)
            + tuple(terms_at((frame + shift) % frame_count * part) for frame in range(frame_count))
        ]
        for shift in range(frame_count)
    ]


def send_parts(parts):
    return [shift_frames(part, len(parts), shift) for shift, part in enumerate(parts)]


def add_parts(rows, flag, frame_count):
    terms = tuple((source, 0) for source in range(frame_count))
    return [[(rows // frame_count, flag, *[terms] * frame_count)]]


def frame_steps(block, frame_count, flag):
    (block,) = yield [block]
    rows = block.shape[0]
    parts = yield [block], frame_parts(rows, frame_count, flag, lambda at: ((0, at),))
    parts = yield send_parts(parts)
    return list(parts), add_parts(rows, flag, frame_count)


def core_steps(pairs, batch_size):
    moved = yield [swap_bit(sent, "batch", batch_size, 0) for _, sent in pairs]
    sources, segments = [], []
    for (kept, _), arrived in zip(pairs, moved):
        terms = ((len(sources), 0), (len(sources) + 1, 0))
        segments.append((kept.shape[0], 0, terms, terms))
        sources += [kept, arrived]
    return sources, [segments]


def sum_chips(block, batch_size):
    groups = [list(range(core, batch_size, 2)) for core in range(2)]
    return lax.psum_scatter(
        block, "batch", scatter_dimension=0, axis_index_groups=groups, tiled=True
    )


def sum_steps(kept, sent, sizes, flag):
    wide = list(range(1, sizes[0].bit_length() - 1))
    ways = (wide, wide[::-1])
    frame_count = sizes[1]

    def over_batch(block, bit):
        return swap_bit(block, "batch", sizes[0], bit)

    (arrived,) = yield [over_batch(sent, 0)]
    rows = kept.shape[0] // 2
    sources = [kept, arrived]
    pairs = [((0, 0), (1, 0)), ((0, rows), (1, rows))]
    for level in range(len(wide)):
        plan = []
        for (left, right), way in zip(pairs, ways):
            plan += split_plan(rows, way[level], left, right)
        first_out, first_kept, second_out, second_kept = yield sources, plan
        moved = yield [over_batch(first_out, ways[0][level]), over_batch(second_out, ways[1][level])]
        sources = [first_kept, moved[0], second_kept, moved[1]]
        pairs = [((0, 0), (1, 0)), ((2, 0), (3, 0))]
        rows //= 2

    def terms_at(start):
        (left, right), at = pairs[start // rows], start % rows
        return (left[0], left[1] + at), (right[0], right[1] + at)

    parts = yield sources, frame_parts(2 * rows, frame_count, flag, terms_at)
    parts = yield send_parts(parts)
    (part,) = yield parts, add_parts(2 * rows, flag, frame_count)
    parts = yield [shift_frames(part, frame_count, shift) for shift in range(frame_count)]
    size = 2 * rows // frame_count
    segments = [
        (size, flag) + tuple((((frame - owner) % frame_count, 0),) for frame in range(frame_count))
        for owner in range(frame_count)
    ]
    blocks = yield parts, [segments[: frame_count // 2], segments[frame_count // 2 :]]
    for level in range(len(wide))[::-1]:
        moved = yield [over_batch(block, way[level]) for block, way in zip(blocks, ways)]
        sources = [blocks[0], moved[0], blocks[1], moved[1]]
        plan = [join_plan(rows, ways[0][level], (0, 0), (1, 0))]
        plan += [join_plan(rows, ways[1][level], (2, 0), (3, 0))]
        if level == 0:
            plan = [plan[0] + plan[1]]
        blocks = yield sources, plan
        rows *= 2
    (arrived,) = yield [over_batch(blocks[0], 0)]
    return blocks[0], arrived


def gather_steps(shard, batch_size):
    wide = list(range(1, batch_size.bit_length() - 1))
    ways = (wide, wide[::-1])
    half = shard.shape[0] // 2

    def over_batch(block, bit):
        return swap_bit(block, "batch", batch_size, bit)

    blocks = [shard[:half], shard[half:]]
    done = [[], []]
    for level in range(len(wide)):
        moved = yield [over_batch(block, way[level]) for block, way in zip(blocks, ways)]
        plan = []
        for index, way in enumerate(ways):
            bit, before = way[level], done[index]
            done[index] = sorted([*before, bit])
            segments = []
            for place in range(2 ** len(done[index])):
                value = {one: (place >> at) & 1 for at, one in enumerate(done[index])}
                row = half * sum(value[one] << at for at, one in enumerate(before))
                own, other = ((2 * index, row),), ((2 * index + 1, row),)
                segments.append((half, bit, *((other, own) if value[bit] else (own, other))))
            plan.append(segments)
        if level == len(wide) - 1:
            plan = [plan[0] + plan[1]]
        blocks = yield [blocks[0], moved[0], blocks[1], moved[1]], plan
    (block,) = blocks
    (arrived,) = yield [over_batch(block, 0)]
    segments = []
    for place in range(batch_size):
        for index in range(2):
            row = (index * batch_size // 2 + (place >> 1)) * half
            own, other = ((0, row),), ((1, row),)
            segments.append((half, 0, *((other, own) if place & 1 else (own, other))))
    (whole,) = yield [block, arrived], [segments]
    return whole


class Flight:
    def __init__(self, steps):
        self.steps, self.result = steps, None
        self.moved = next(steps)

    def send(self, value):
        try:
            return self.steps.send(value)
        except StopIteration as stop:
            self.result = stop.value
            return None


def advance(order, *flights, after=()):
    active, requests = [], []
    for flight in flights:
        if flight.result is not None:
            continue
        request = flight.send(flight.moved)
        if request is None and isinstance(flight.result[0], list):
            request = flight.result
        if request is not None:
            active.append(flight)
            requests.append(request)
    if requests:
        for flight, outputs in zip(active, shuffle(order, requests, after)):
            if flight.result is None:
                flight.moved = flight.send(outputs)
            else:
                flight.result = outputs


def finish_together(order, *flights):
    sources, segments = [], []
    for flight in flights:
        if flight.result is None:
            flight.send(flight.moved)
            parts, ((segment,),) = flight.result
        else:
            parts = flight.result
            segment = (parts[0].shape[0], 0, ((0, 0),), ((0, 0),))
        rows, flag, *choices = segment
        base = len(sources)
        segments.append(
            (rows, flag, *[tuple((source + base, at) for source, at in terms) for terms in choices])
        )
        sources += parts
    ((whole,),) = shuffle(order, [(sources, [segments])], ())
    return whole


def deliver_kernel(flags_ref, own_ref, arrived_ref, out_ref, rest_ref):
    half, features = own_ref.shape
    columns = out_ref.shape[1] // features
    for core in range(2):

        @pl.when(flags_ref[0] == core)
        def _():
            for index in range(columns + 1):
                first = index * features
                height = features if index < columns else rest_ref.shape[0]
                while height:
                    owner, at = divmod(first, half)
                    size = min(height, half - at)
                    piece = (own_ref if owner == core else arrived_ref)[at : at + size]
                    piece = piece.astype(jnp.float32)
                    row = first % features
                    if index < columns:
                        span = slice(index * features, (index + 1) * features)
                        out_ref[row : row + size, span] = piece
                    else:
                        rest_ref[row : row + size] = piece
                    first, height = first + size, height - size


def deliver_halves(order, own, arrived):
    half, features = own.shape
    columns = 2 * half // features
    return order.run(
        deliver_kernel,
        [order.flags, own, arrived],
        [SMEM, VMEM, VMEM],
        [VMEM, VMEM],
        [struct((features, columns * features), jnp.float32), struct((8, features), jnp.float32)],
    )


def deliver_parts_kernel(outputs, counts, *refs):
    steps = pl.program_id(0)
    feed_refs, space_refs = refs[: counts[0]], refs[counts[0] : sum(counts)]
    for output, (first, last, _) in zip(refs[sum(counts) :], outputs):

        @pl.when((steps >= first) & (steps < last))
        def _():
            sources = feed_refs if last <= FEED_BLOCKS else space_refs
            rows = sources[0].shape[1]
            for piece in range(sources[0].shape[0]):
                for index, source in enumerate(sources):
                    at = (piece * len(sources) + index) * rows
                    output[at : at + rows] = source[piece].astype(output.dtype)


def deliver_parts(order, gathered, space_part):
    _, part, features = gathered.shape
    feed_part = part - space_part
    unit = math.gcd(space_part, feed_part)

    def source(rows, first, step_of, index):
        def place(step):
            return step_of(step), first // unit + index, 0

        return pl.BlockSpec((features // rows, unit, features), place)

    counts = (feed_part // unit, space_part // unit)
    feed_specs = [
        source(feed_part, space_part, lambda step: jnp.minimum(step, FEED_BLOCKS - 1), index)
        for index in range(counts[0])
    ]
    space_specs_ = [
        source(space_part, 0, lambda step: jnp.maximum(step - FEED_BLOCKS, 0), index)
        for index in range(counts[1])
    ]
    half = FEED_BLOCKS // 2
    outputs = [(0, half, True), (half, FEED_BLOCKS, False)]
    for first, last, wide in ((0, 3, True), (3, 4, False), (4, 5, False)):
        outputs.append((FEED_BLOCKS + first, FEED_BLOCKS + last, wide))

    def spot(first, last, wide):
        def index(step):
            at = jnp.clip(step - first, 0, last - first - 1)
            return (0, at) if wide else (at, 0)

        return pl.BlockSpec((features, features), index)

    def shape(first, last, wide):
        rows = (last - first) * features
        return struct((features, rows) if wide else (rows, features), jnp.float32)

    return order.run(
        functools.partial(deliver_parts_kernel, outputs, counts),
        [gathered] * sum(counts),
        feed_specs + space_specs_,
        [spot(*item) for item in outputs],
        [shape(*item) for item in outputs],
        grid=(outputs[-1][1],),
    )


def contract(x,y,dims):
    return lax.dot_general(x,y,((dims[0:1],dims[1:2]),((),())),preferred_element_type=jnp.float32)

def widen_rows(values, wide):
    rows, width = values.shape
    if wide == rows:
        return values
    return jnp.concatenate([values, jnp.zeros((wide - rows, width), values.dtype)])


def head_halves(width):
    lane = lax.broadcasted_iota(jnp.int32, (1, width), 1)
    return [lane < width // 2, lane >= width // 2]

def space_forward_kernel(scale, tile, column_ref, row_ref, q_ref, k_ref, v_ref, mixture_ref, total_ref, bias_ref, k_wide, v_wide):
    rows, width = q_ref.shape
    wide = k_wide.shape[0]
    @pl.when(pl.program_id(0) == 0)
    def _():
        bias_ref[...] = jnp.where(column_ref[...] == row_ref[...], 0.0, -1e30)
        if wide > rows:
            k_wide[rows:] = jnp.zeros((wide - rows, width), k_wide.dtype)
            v_wide[rows:] = jnp.zeros((wide - rows, width), v_wide.dtype)
    k_wide[:rows] = k_ref[...]
    v_wide[:rows] = v_ref[...]
    halves = head_halves(width)
    zero, one = jnp.zeros((), q_ref.dtype), jnp.ones((), q_ref.dtype)
    filled = [jnp.where(half, v_wide[...], one) for half in halves]
    for start in range(0, rows, tile):
        span = slice(start, start + tile)
        outs, tops = [], []
        for half, values in zip(halves, filled):
            queries = jnp.where(half, q_ref[span], zero)
            scores = contract(queries, k_wide[...], (1, 1)) * (scale * LOG2E) + bias_ref[span]
            top = jnp.max(scores, axis=1, keepdims=True)
            weights = jnp.exp2(scores - top)
            outs.append(contract(weights.astype(jnp.bfloat16), values, (1, 0)))
            tops.append(top)
        mass = pltpu.roll(jnp.where(halves[0], outs[1], outs[0]), width // 2, 1)
        mixture = jnp.where(halves[0], outs[0], outs[1]) / mass
        mixture_ref[span] = mixture.astype(mixture_ref.dtype)
        total_ref[span] = jnp.where(halves[0], tops[0], tops[1]) + jnp.log2(mass)


def space_specs(rows, features):
    pairs = HEADS // 2
    width = features // pairs
    wide = round_up(rows, 128)
    fixed = [pl.BlockSpec((rows, 1), lambda i: (0, 0)), pl.BlockSpec((1, wide), lambda i: (0, 0))]
    blocks = [pl.BlockSpec((rows, width), lambda i, o=o: (0, o + i)) for o in (0, pairs, 2 * pairs)]
    out = pl.BlockSpec((rows, width), lambda i: (0, i))
    scratch = [pltpu.VMEM((rows, wide), jnp.float32)]
    scratch += [pltpu.VMEM((wide, width), jnp.bfloat16)] * 2
    return pairs, (features // HEADS) ** -0.5, fixed + blocks, out, scratch


def clip_lines(clip):
    rows = clip.shape[0]
    row = jnp.pad(clip, (0, round_up(rows, 128) - rows), constant_values=-2)
    return clip[:, None], row[None]


def space_forward(order, qkv, clip, features):
    rows = qkv.shape[0]
    pairs, scale, specs, out, scratch = space_specs(rows, features)
    return order.run(
        functools.partial(space_forward_kernel, scale, rows),
        [*clip_lines(clip), qkv, qkv, qkv],
        specs,
        [out, out],
        [struct((rows, features), jnp.bfloat16), struct((rows, features), jnp.float32)],
        grid=(pairs,),
        scratch=scratch,
    )


def space_backward_kernel(scale, tile, column_ref, row_ref, q_ref, k_ref, v_ref, mixture_ref, total_ref, grad_ref, dq_ref, dk_ref, dv_ref, bias_ref, q_wide, g_wide):
    rows, width = q_ref.shape
    wide = q_wide.shape[0]
    @pl.when(pl.program_id(0) == 0)
    def _():
        bias_ref[...] = jnp.where(column_ref[...] == row_ref[...], 0.0, -1e30)
        if wide > rows:
            q_wide[rows:] = jnp.zeros((wide - rows, width), q_wide.dtype)
            g_wide[rows:] = jnp.zeros((wide - rows, width), g_wide.dtype)
    q_wide[:rows] = q_ref[...]
    g_wide[:rows] = grad_ref[...]
    halves = head_halves(width)
    zero = jnp.zeros((), q_ref.dtype)
    product = grad_ref[...].astype(jnp.float32) * mixture_ref[...].astype(jnp.float32)
    sums = [jnp.sum(jnp.where(half, product, 0.0), axis=1, keepdims=True) for half in halves]
    delta = widen_rows(jnp.where(halves[0], sums[0], sums[1]), wide).T
    total = widen_rows(total_ref[...], wide).T
    dq_parts = [None, None]
    for start in range(0, rows, tile):
        span = slice(start, start + tile)
        dk, dv = [], []
        for index, half in enumerate(halves):
            at = index * (width // 2)
            keys = jnp.where(half, k_ref[span], zero)
            values = jnp.where(half, v_ref[span], zero)
            scores = contract(keys, q_wide[...], (1, 1)) * (scale * LOG2E)
            weights = jnp.exp2(scores + (bias_ref[span] - total[at:at + 1]))
            slopes = contract(values, g_wide[...], (1, 1))
            slopes = (weights * (slopes - delta[at:at + 1])).astype(jnp.bfloat16)
            dv.append(contract(weights.astype(jnp.bfloat16), g_wide[...], (1, 0)))
            dk.append(contract(slopes, q_wide[...], (1, 0)))
            part = contract(slopes, keys, (0, 0))
            dq_parts[index] = part if start == 0 else dq_parts[index] + part
        dk_ref[span] = (jnp.where(halves[0], dk[0], dk[1]) * scale).astype(dk_ref.dtype)
        dv_ref[span] = jnp.where(halves[0], dv[0], dv[1]).astype(dv_ref.dtype)
    dq_ref[...] = ((dq_parts[0] + dq_parts[1])[:rows] * scale).astype(dq_ref.dtype)

def space_backward(order, qkv, mixture, total, grad, clip, features):
    rows = qkv.shape[0]
    pairs, scale, specs, out, scratch = space_specs(rows, features)
    return order.run(
        functools.partial(space_backward_kernel, scale, rows),
        [*clip_lines(clip), qkv, qkv, qkv, mixture, total, grad],
        specs + [out] * 3,
        [out] * 3,
        [struct((rows, features), jnp.bfloat16)] * 3,
        grid=(pairs,),
        scratch=scratch,
    )


def norm_parts(values):
    average = jnp.mean(values, axis=1, keepdims=True)
    centered = values - average
    spread = lax.rsqrt(jnp.mean(centered * centered, axis=1, keepdims=True) + 1e-06)
    return centered * spread, spread
def norm_back(grad, normed, spread, gain):
    scaled = grad * gain
    return spread * (scaled - jnp.mean(scaled, axis=1, keepdims=True) - normed * jnp.mean(scaled * normed, axis=1, keepdims=True))
def column_sum(values):
    return jnp.sum(values, axis=0, keepdims=True)

def square_spec(packed, index):
    batch_count, _, features = packed.shape
    return pl.BlockSpec((batch_count, features // batch_count, features), lambda i: (0, index, 0))


def square(ref):
    return ref[...].reshape(-1, ref.shape[-1])


def feed_kernel(chunks, x1_ref, mixture_ref, dz_ref, so_ref, fi_ref, fo_ref, fb_ref, vec_ref,
                out_ref, dx2_ref, dys_ref, dos_ref, grad_ref, gfb_ref, gvec_ref,
                x2_s, a3_s, a3t_s, acc_s, da_s, g_s, dh_s):
    step = pl.program_id(0)
    rows = x1_ref.shape[0]
    @pl.when(step == 0)
    def _():
        x2 = x1_ref[...] + contract(mixture_ref[...], square(so_ref), (1, 0)) + vec_ref[9:10]
        x2_s[...] = x2
        normed, _ = norm_parts(x2)
        a3 = (normed * vec_ref[10:11] + vec_ref[11:12]).astype(jnp.bfloat16)
        a3_s[...] = a3
        a3t_s[...] = a3.T
        acc_s[...] = x2 + vec_ref[12:13]
        da_s[...] = jnp.zeros_like(da_s)
    inner, outer = square(fi_ref), square(fo_ref)
    part = rows // chunks
    for chunk in range(chunks):
        span = slice(chunk * part, (chunk + 1) * part)
        hidden = contract(a3_s[span], inner, (1, 0)) + fb_ref[...]
        cdf = 0.5 + 0.5 * lax.erf(hidden * math.sqrt(0.5))
        slope = cdf + hidden * jnp.exp(hidden * hidden * -0.5) * (1.0 / math.sqrt(2.0 * math.pi))
        active = (hidden * cdf).astype(jnp.bfloat16)
        g_s[span] = active
        dh = (contract(dz_ref[span], outer, (1, 1)) * slope).astype(jnp.bfloat16)
        dh_s[span] = dh
        acc_s[span] += contract(active, outer, (1, 0))
        da_s[span] += contract(dh, inner, (1, 1))
    grad_ref[0] = contract(a3t_s[...], dh_s[...], (1, 0)).astype(grad_ref.dtype)
    grad_ref[1] = contract(g_s[...], dz_ref[...], (0, 0)).astype(grad_ref.dtype)
    gfb_ref[...] = column_sum(dh_s[...].astype(jnp.float32))
    @pl.when(step == pl.num_programs(0) - 1)
    def _():
        out_ref[0] = acc_s[: out_ref.shape[1]].astype(out_ref.dtype)
        normed, spread = norm_parts(x2_s[...])
        grad = da_s[...]
        dz = dz_ref[...].astype(jnp.float32)
        dx2 = dz + norm_back(grad, normed, spread, vec_ref[10:11])
        dx2_ref[...] = dx2
        dys = dx2.astype(jnp.bfloat16)
        dys_ref[...] = dys
        dos_ref[...] = contract(dys, square(so_ref), (1, 1)).astype(dos_ref.dtype)
        gvec_ref[0:1] = column_sum(grad * normed)
        gvec_ref[1:2] = column_sum(grad)
        gvec_ref[2:3] = column_sum(dz)
        gvec_ref[3:4] = column_sum(dys.astype(jnp.float32))
        gvec_ref[4:8] = jnp.zeros((4, gvec_ref.shape[1]), jnp.float32)

def feed_block(order, row_count, x1, mixture, dz, packed, feed_packed, bias, vec, chunks):
    rows, features = x1.shape
    batch_count = feed_packed.shape[0]
    hidden = bias.shape[1]
    whole = pl.BlockSpec((rows, features), lambda j: (0, 0))
    line = pl.BlockSpec((1, features), lambda j: (0, j))
    shard = hidden // batch_count
    low, full = jnp.bfloat16, jnp.float32
    return order.run(
        functools.partial(feed_kernel, chunks),
        [x1, mixture, dz, packed, feed_packed, feed_packed, bias, vec],
        [
            whole,
            whole,
            whole,
            square_spec(packed, 4),
            pl.BlockSpec((batch_count, features // batch_count, features), lambda j: (0, j, 0)),
            pl.BlockSpec((features // shard, shard, features), lambda j: (j, 1, 0)),
            line,
            pl.BlockSpec(vec.shape, lambda j: (0, 0)),
        ],
        [
            pl.BlockSpec((1, row_count, features), lambda j: (0, 0, 0)),
            whole,
            whole,
            whole,
            pl.BlockSpec((2, features, features), lambda j: (0, j, 0)),
            line,
            pl.BlockSpec((8, features), lambda j: (0, 0)),
        ],
        [
            struct((1, row_count, features), low),
            struct((rows, features), full),
            struct((rows, features), low),
            struct((rows, features), low),
            struct((2, hidden, features), low),
            struct((1, hidden), full),
            struct((8, features), full),
        ],
        grid=(hidden // features,),
        scratch=[
            pltpu.VMEM((rows, features), full),
            pltpu.VMEM((rows, features), low),
            pltpu.VMEM((features, rows), low),
            pltpu.VMEM((rows, features), full),
            pltpu.VMEM((rows, features), full),
            pltpu.VMEM((rows, features), low),
            pltpu.VMEM((rows, features), low),
        ],
    )


def gather_rows(count, frame, slots, rows_s):
    part = slots[0].shape[0]
    for shift in range(count):
        owner = lax.rem(frame + shift, count)
        rows_s[pl.ds(pl.multiple_of(owner * part, ROW_TILE), part)] = slots[shift][...]


def middle_kernel(count, frame_flag, flags_ref, token_ref, *refs):
    slots, (to_ref, *sp_refs, vec_ref) = refs[:count], refs[count : count + 5]
    mixture_ref, x1_ref, a2_ref, qkv_ref = refs[count + 5 :]
    rows, features = token_ref.shape
    gather_rows(count, flags_ref[frame_flag], slots, mixture_ref)
    number = lax.broadcasted_iota(jnp.int32, (rows, 1), 0)
    branch = contract(mixture_ref[...], square(to_ref), (1, 0)) + vec_ref[4:5]
    x1 = token_ref[...].astype(jnp.float32) + jnp.where(number < PATCHES, branch, 0.0)
    x1_ref[...] = x1
    normed, _ = norm_parts(x1)
    a2 = (normed * vec_ref[5:6] + vec_ref[6:7]).astype(jnp.bfloat16)
    a2_ref[...] = a2
    for third in range(3):
        span = slice(third * features, (third + 1) * features)
        joined = contract(a2, square(sp_refs[third]), (1, 0))
        if third != 1:
            joined = joined + vec_ref[7 + third // 2 : 8 + third // 2]
        qkv_ref[:, span] = joined.astype(jnp.bfloat16)


def project_specs(packed, vec):
    return [square_spec(packed, index) for index in range(4)] + [
        pl.BlockSpec(vec.shape, lambda i: (0, 0))
    ]


def middle_forward(order, tokens, slots, packed, vec):
    rows, features = tokens.shape
    low = jnp.bfloat16
    return order.run(
        functools.partial(middle_kernel, len(slots), order.flags.shape[0] - 1),
        [order.flags, tokens, *slots, *[packed] * 4, vec],
        [SMEM] + [VMEM] * (len(slots) + 1) + project_specs(packed, vec),
        [VMEM] * 4,
        [
            struct((rows, features), low),
            struct((rows, features), jnp.float32),
            struct((rows, features), low),
            struct((rows, 3 * features), low),
        ],
        grid=(1,),
    )


def middle_back_kernel(
    sizes, part, flags_ref, dq_ref, dk_ref, dv_ref, x1_ref, dx2_ref, to_ref, *refs
):
    *sp_refs, vec_ref, time_ref, feed_ref, bias_ref = refs[:7]
    dx1_ref, sums_ref, kept_ref, sent_ref = refs[7:11]
    count = sizes[1]
    slots, rows_s = refs[11 : 11 + count], refs[11 + count]
    rows, features = x1_ref.shape
    grad = 0.0
    for third, piece in enumerate((dq_ref, dk_ref, dv_ref)):
        grad = grad + contract(piece[...], square(sp_refs[third]), (1, 1))
    normed, spread = norm_parts(x1_ref[...])
    dx1 = dx2_ref[...] + norm_back(grad, normed, spread, vec_ref[5:6])
    dx1_ref[...] = dx1
    number = lax.broadcasted_iota(jnp.int32, (rows, 1), 0)
    dyt = jnp.where(number < PATCHES, dx1, 0.0).astype(jnp.bfloat16)
    rows_s[...] = contract(dyt, square(to_ref), (1, 1)).astype(rows_s.dtype)
    block = rows // count
    for shift in range(count):
        owner = lax.rem(flags_ref[flags_ref.shape[0] - 1] + shift, count)
        slots[shift][...] = rows_s[pl.ds(pl.multiple_of(owner * block, ROW_TILE), block)]
    sums_ref[0:1] = column_sum(grad * normed)
    sums_ref[1:2] = column_sum(grad)
    sums_ref[2:3] = column_sum(dq_ref[...].astype(jnp.float32))
    sums_ref[3:4] = column_sum(dv_ref[...].astype(jnp.float32))
    sums_ref[4:5] = column_sum(dyt.astype(jnp.float32))
    sums_ref[5:8] = jnp.zeros((3, features), jnp.float32)
    first = 4 * features
    put = functools.partial(put_parts, flags_ref, kept_ref, sent_ref, sizes, part, first)
    put(first, contract(time_ref[...], dyt, (0, 0)))
    bias = bias_ref[...]
    lines = [bias[:, at : at + features] for at in range(0, bias.shape[1], features)]
    pieces = [sums_ref[0:4], feed_ref[3:4], feed_ref[0:3], *lines]
    put(first + features, fill_rows(pieces, 2 * kept_ref.shape[0] - features, features))


def middle_backward(order, sizes, dq, dk, dv, x1, dx2, packed, vec, mixture, feed_sums, bias):
    rows, features = x1.shape
    count = sizes[1]
    low, full = jnp.bfloat16, jnp.float32
    total, part = space_rows(sizes, features)
    half = struct(((total - 4 * features) // 2, features), low)
    results = order.run(
        functools.partial(middle_back_kernel, sizes, part),
        [order.flags, dq, dk, dv, x1, dx2, *[packed] * 4, vec, mixture, feed_sums, bias],
        [SMEM] + [VMEM] * 5 + project_specs(packed, vec) + [VMEM] * 3,
        [VMEM] * (4 + count),
        [struct((rows, features), full), struct((8, features), full), half, half]
        + [struct((rows // count, features), low)] * count,
        grid=(1,),
        scratch=[pltpu.VMEM((rows, features), low)],
    )
    return results[0], results[1], results[2:4], results[4:]


def put_half(core_ref, kept_ref, sent_ref, at, value):
    half = kept_ref.shape[0]
    low = value.astype(kept_ref.dtype)
    part = math.gcd(half, low.shape[0])
    for offset in range(0, low.shape[0], part):
        owner, first = divmod(at + offset, half)
        piece = low[offset : offset + part]

        @pl.when(core_ref[0] == owner)
        def _():
            kept_ref[first : first + part] = piece

        @pl.when(core_ref[0] != owner)
        def _():
            sent_ref[first : first + part] = piece


def fill_rows(pieces, rows, features):
    used = sum(piece.shape[0] for piece in pieces)
    return jnp.concatenate([*pieces, jnp.zeros((rows - used, features), jnp.float32)])


def put_parts(core_ref, kept_ref, sent_ref, sizes, part, first, at, value):
    low = value.astype(kept_ref.dtype)
    for offset in range(0, low.shape[0], part):
        batch, frame = divmod((at + offset) // part, sizes[1])
        start = ((batch >> 1) * sizes[1] + frame) * part - first // 2
        piece = low[offset : offset + part]

        @pl.when(core_ref[0] == batch & 1)
        def _():
            kept_ref[start : start + part] = piece

        @pl.when(core_ref[0] != batch & 1)
        def _():
            sent_ref[start : start + part] = piece


def space_rows(sizes, features):
    rows = round_up(5 * features + ROW_TILE, sizes[0] * sizes[1] * ROW_TILE)
    return rows, rows // (sizes[0] * sizes[1])


def space_weights_kernel(
    sizes, part, flags_ref, a2_ref, dq_ref, dk_ref, dv_ref, mixture_ref, dys_ref, kept_ref, sent_ref
):
    features = a2_ref.shape[1]
    put = functools.partial(put_parts, flags_ref, kept_ref, sent_ref, sizes, part, 0)
    turned = a2_ref[...].T
    for third, piece in enumerate((dq_ref, dk_ref, dv_ref)):
        put(third * features, contract(turned, piece[...], (1, 0)))
    put(3 * features, contract(mixture_ref[...], dys_ref[...], (0, 0)))


def space_weights(order, sizes, *operands):
    features = operands[0].shape[1]
    part = space_rows(sizes, features)[1]
    half = struct((2 * features, features), jnp.bfloat16)
    return order.run(
        functools.partial(space_weights_kernel, sizes, part),
        [order.flags, *operands],
        [SMEM] + [VMEM] * len(operands),
        [VMEM] * 2,
        [half, half],
    )


CHUNK = 16
def head_map(features, lanes=128):
    head = jnp.arange(features, dtype=jnp.int32) // (features // HEADS)
    return (head[:, None] == jnp.arange(lanes, dtype=jnp.int32)[None]).astype(jnp.bfloat16)

def pair_sums(left, right, gather_ref, pair_s):
    count = len(left)
    for f in range(count):
        for g in range(count):
            at = (f * count + g) * CHUNK
            pair_s[at:at + CHUNK] = (left[f] * right[g]).astype(jnp.bfloat16)
    return contract(pair_s[...], gather_ref[...], (1, 0))

def time_forward_kernel(count, scale, *refs):
    slots, (tp_ref, vec_ref, gather_ref, spread_ref) = refs[:count], refs[count:count + 4]
    outs, (qkv_ref, prob_ref, a1_ref) = refs[count + 4:2 * count + 4], refs[2 * count + 4:2 * count + 7]
    pair_s, weight_s = refs[2 * count + 7:]
    part, features = slots[0].shape
    for s in range(count):
        normed, _ = norm_parts(slots[s][...].astype(jnp.float32))
        a1_ref[s * part:(s + 1) * part] = (normed * vec_ref[0:1] + vec_ref[1:2]).astype(jnp.bfloat16)
    for third in range(3):
        span = slice(third * features, (third + 1) * features)
        joined = contract(a1_ref[...], tp_ref[:, span], (1, 0))
        if third != 1:
            joined = joined + vec_ref[2 + third // 2:3 + third // 2]
        qkv_ref[:, span] = joined.astype(jnp.bfloat16)

    def chunk_step(index, carry):
        def rows_of(s, third):
            start = pl.multiple_of(s * part + index * CHUNK, CHUNK)
            return qkv_ref[pl.ds(start, CHUNK), third * features:(third + 1) * features].astype(jnp.float32)
        queries, keys, values = ([rows_of(s, third) for s in range(count)] for third in range(3))
        scores = pair_sums(queries, keys, gather_ref, pair_s) * (scale * LOG2E)
        place = pl.ds(pl.multiple_of(index * CHUNK, CHUNK), CHUNK)
        for f in range(count):
            row = [scores[(f * count + g) * CHUNK:(f * count + g + 1) * CHUNK] for g in range(count)]
            top = functools.reduce(jnp.maximum, row)
            raised = [jnp.exp2(item - top) for item in row]
            mass = functools.reduce(jnp.add, raised)
            for g in range(count):
                weight = raised[g] / mass
                prob_ref[f * count + g, place] = weight
                at = (f * count + g) * CHUNK
                weight_s[at:at + CHUNK] = weight.astype(jnp.bfloat16)
        wide = contract(weight_s[...], spread_ref[...], (1, 0))
        for f in range(count):
            total = 0.0
            for g in range(count):
                at = (f * count + g) * CHUNK
                total = total + wide[at:at + CHUNK] * values[g]
            outs[f][place] = total.astype(jnp.bfloat16)
        return carry
    lax.fori_loop(0, part // CHUNK, chunk_step, 0)

def time_forward(order, slots, time_weight, vec):
    count = len(slots)
    part, features = slots[0].shape
    gather = head_map(features)
    low, full = jnp.bfloat16, jnp.float32
    results = order.run(
        functools.partial(time_forward_kernel, count, (features // HEADS) ** -0.5),
        [*slots, time_weight, vec, gather, gather.T],
        [VMEM] * count + [pl.BlockSpec((features, 3 * features), lambda i: (0, 0)), VMEM, VMEM, VMEM],
        [VMEM] * (count + 3),
        [struct((part, features), low)] * count
        + [
            struct((count * part, 3 * features), low),
            struct((count * count, part, 128), full),
            struct((count * part, features), low),
        ],
        grid=(1,),
        scratch=[
            pltpu.VMEM((count * count * CHUNK, features), low),
            pltpu.VMEM((count * count * CHUNK, 128), low),
        ],
    )
    return results[:count], results[count], results[count + 1], results[count + 2]


def time_backward_kernel(count, scale, flags_ref, *refs):
    grads, slots = refs[:count], refs[count : 2 * count]
    qkv_ref, prob_ref, a1_ref, gather_ref, spread_ref, tp_ref, vec_ref, other_ref = refs[2 * count : 2 * count + 8]
    refs = refs[2 * count + 8 :]
    outs, (kept_ref, sent_ref, dqkv_ref, pair_s, weight_s) = refs[:count], refs[count:]
    part, features = grads[0].shape
    def chunk_step(index, carry):
        place = pl.ds(pl.multiple_of(index * CHUNK, CHUNK), CHUNK)
        def rows_of(s, third):
            start = pl.multiple_of(s * part + index * CHUNK, CHUNK)
            return qkv_ref[pl.ds(start, CHUNK), third * features:(third + 1) * features].astype(jnp.float32)
        queries, keys, values = ([rows_of(s, third) for s in range(count)] for third in range(3))
        outer = [grads[s][place].astype(jnp.float32) for s in range(count)]
        slopes = pair_sums(outer, values, gather_ref, pair_s)
        size = count * count * CHUNK
        for f in range(count):
            row = [slopes[(f * count + g) * CHUNK:(f * count + g + 1) * CHUNK] for g in range(count)]
            weights = [prob_ref[f * count + g, place] for g in range(count)]
            delta = functools.reduce(jnp.add, [w * s for w, s in zip(weights, row)])
            for g in range(count):
                at = (f * count + g) * CHUNK
                weight_s[at:at + CHUNK] = weights[g].astype(jnp.bfloat16)
                weight_s[size + at:size + at + CHUNK] = (weights[g] * (row[g] - delta)).astype(jnp.bfloat16)
        wide = contract(weight_s[...], spread_ref[...], (1, 0))
        for s in range(count):
            dq, dk, dv = 0.0, 0.0, 0.0
            for t in range(count):
                forth, back = (s * count + t) * CHUNK, (t * count + s) * CHUNK
                dq = dq + wide[size + forth:size + forth + CHUNK] * keys[t]
                dk = dk + wide[size + back:size + back + CHUNK] * queries[t]
                dv = dv + wide[back:back + CHUNK] * outer[t]
            start = pl.ds(pl.multiple_of(s * part + index * CHUNK, CHUNK), CHUNK)
            for third, value in enumerate((dq * scale, dk * scale, dv)):
                dqkv_ref[start, third * features:(third + 1) * features] = value.astype(jnp.bfloat16)
        return carry
    lax.fori_loop(0, part // CHUNK, chunk_step, 0)
    a1t = a1_ref[...].T
    put = functools.partial(put_half, flags_ref, kept_ref, sent_ref)
    for third in range(3):
        span = slice(third * features, (third + 1) * features)
        put(third * features, contract(a1t, dqkv_ref[:, span], (1, 0)))
    grad = contract(dqkv_ref[...], tp_ref[...], (1, 1))
    gain, shift = 0.0, 0.0
    for s in range(count):
        piece = grad[s * part : (s + 1) * part]
        normed, spread = norm_parts(slots[s][...].astype(jnp.float32))
        outs[s][...] = norm_back(piece, normed, spread, vec_ref[0:1]).astype(jnp.bfloat16)
        gain = gain + column_sum(piece * normed)
        shift = shift + column_sum(piece)
    sums = [
        gain,
        shift,
        column_sum(dqkv_ref[:, :features].astype(jnp.float32)),
        column_sum(dqkv_ref[:, 2 * features :].astype(jnp.float32)),
        other_ref[4:5],
    ]
    put(3 * features, fill_rows(sums, 2 * kept_ref.shape[0] - 3 * features, features))


def time_backward(order, grads, slots, qkv, prob, a1, time_weight, vec, other):
    count = len(grads)
    part, features = grads[0].shape
    gather = head_map(features)
    low = jnp.bfloat16
    half = struct((round_up(3 * features + 16, 512) // 2, features), low)
    results = order.run(
        functools.partial(time_backward_kernel, count, (features // HEADS) ** -0.5),
        [order.flags, *grads, *slots, qkv, prob, a1, gather, gather.T, time_weight, vec, other],
        [SMEM] + [VMEM] * (2 * count + 5)
        + [pl.BlockSpec((features, 3 * features), lambda i: (0, 0)), VMEM, VMEM],
        [VMEM] * (count + 2),
        [struct((part, features), low)] * count + [half, half],
        grid=(1,),
        scratch=[
            pltpu.VMEM(qkv.shape, low),
            pltpu.VMEM((count * count * CHUNK, features), low),
            pltpu.VMEM((2 * count * count * CHUNK, 128), low),
        ],
    )
    return results[:count], results[count], results[count + 1]


def place_kernel(count, flags_ref, *refs):
    gather_rows(count, flags_ref[flags_ref.shape[0] - 1], refs[:count], refs[count])


def place_slots(order, slots):
    part, features = slots[0].shape
    return order.run(
        functools.partial(place_kernel, len(slots)),
        [order.flags, *slots],
        [SMEM] + [VMEM] * len(slots),
        [VMEM],
        [struct((len(slots) * part, features), slots[0].dtype)],
    )[0]


def body(
    tokens,
    size_tag,
    cotangent,
    time_project,
    time_output,
    time_vector,
    space_project,
    space_output,
    space_vector,
    feed_inner,
    feed_bias,
    feed_outer,
    feed_vector,
):
    frame_count = lax.axis_size("frame")
    batch_count = lax.axis_size("batch")
    sizes = (batch_count, frame_count)
    frame_index = lax.axis_index("frame")
    batch_index = lax.axis_index("batch")
    flags = [(batch_index >> bit) & 1 for bit in range(batch_count.bit_length() - 1)]
    frame_flag = len(flags)
    order = Order(jnp.stack([*flags, frame_index]).astype(jnp.int32))
    features = tokens.shape[2]
    row_count = tokens.shape[1]
    part = round_up(-(-PATCHES // frame_count), ROW_TILE)
    padded = part * frame_count

    time_weight = lax.all_gather(time_project, "batch", axis=0, tiled=True)
    token_rows = jnp.pad(tokens[0], ((0, padded - row_count), (0, 0)))
    grad_result = jnp.pad(cotangent[0], ((0, padded - row_count), (0, 0)))
    slots = rows_to_frames(token_rows, frame_count, frame_index)
    vectors = jnp.concatenate(
        [time_vector, space_vector, feed_vector, feed_bias.reshape(-1, time_vector.shape[1])], axis=0
    )
    vectors = lax.all_gather(vectors, "batch", axis=0)
    vec = vectors[:, :13].transpose(1, 0, 2).reshape(13, features).astype(jnp.float32)
    vec = jnp.pad(vec, ((0, 3), (0, 0)))
    feed_bias_row = vectors[:, 13:].reshape(1, -1).astype(jnp.float32)

    def stack_columns(weight):
        return [weight[:, at : at + features] for at in range(0, weight.shape[1], features)]

    packed = jnp.concatenate([time_output, *stack_columns(space_project), space_output], axis=0)
    feed_packed = jnp.concatenate([*stack_columns(feed_inner), feed_outer], axis=0)
    feed_packed = lax.all_gather(feed_packed, "batch", axis=0)
    clip = jnp.concatenate(
        [
            jnp.arange(PATCHES, dtype=jnp.int32) // size_tag[0],
            jnp.arange(UNITS, dtype=jnp.int32),
            jnp.full((padded - PATCHES - UNITS,), -1, jnp.int32),
        ]
    )

    weight_flight = Flight(gather_steps(packed, batch_count))
    advance(order, weight_flight)
    mixture_slots, qkv_time, prob_time, first_input = time_forward(order, slots, time_weight, vec)
    mixture_slots = send_back(mixture_slots)
    while weight_flight.result is None:
        advance(order, weight_flight)
    packed = weight_flight.result.reshape(batch_count, -1, features)
    mixture_time, after_time, second_input, qkv_space = middle_forward(
        order, token_rows, mixture_slots, packed, vec
    )
    mixture_space, total_space = space_forward(order, qkv_space, clip, features)
    (
        block_out,
        grad_second,
        grad_branch,
        grad_mixture,
        feed_grads,
        grad_feed_bias,
        feed_sums,
    ) = feed_block(
        order,
        row_count,
        after_time,
        mixture_space,
        grad_result,
        packed,
        feed_packed,
        feed_bias_row,
        vec,
        chunks=2,
    )

    def sum_batch(block):
        return lax.psum_scatter(block, "batch", scatter_dimension=0, tiled=True)

    feed_part = sum_batch(feed_grads.reshape(-1, features))
    grad_query, grad_keys, grad_values = space_backward(
        order, qkv_space, mixture_space, total_space, grad_mixture, clip, features
    )
    space_pair = space_weights(
        order,
        sizes,
        second_input,
        grad_query,
        grad_keys,
        grad_values,
        mixture_space,
        grad_branch,
    )
    grad_first, space_sums, other_pair, grad_slots = middle_backward(
        order,
        sizes,
        grad_query,
        grad_keys,
        grad_values,
        after_time,
        grad_second,
        packed,
        vec,
        mixture_time,
        feed_sums,
        grad_feed_bias,
    )
    grad_slots = send_parts(grad_slots)
    core_flight = Flight(core_steps([space_pair, other_pair], batch_count))
    advance(order, core_flight)
    space_part = sum_chips(core_flight.result[0], batch_count)
    feed_flight = Flight(frame_steps(feed_part, frame_count, frame_flag))
    advance(order, feed_flight, after=grad_slots[1:])
    input_slots, time_kept, time_sent = time_backward(
        order,
        grad_slots,
        slots,
        qkv_time,
        prob_time,
        first_input,
        time_weight,
        vec,
        space_sums,
    )
    time_flight = Flight(sum_steps(time_kept, time_sent, sizes, frame_flag))
    input_slots = send_back(input_slots)
    space_flight = Flight(frame_steps(space_part, frame_count, frame_flag))
    advance(order, feed_flight, space_flight)
    whole = finish_together(order, space_flight, feed_flight)
    whole = lax.all_gather(whole, ("batch", "frame"), axis=0)
    while time_flight.result is None:
        advance(order, time_flight)
    grad_time_project, time_vectors = deliver_halves(order, *time_flight.result)
    space_part_rows = space_part.shape[0] // frame_count
    (
        grad_feed_inner,
        grad_feed_outer,
        grad_space_project,
        grad_space_output,
        grad_time_output,
    ) = deliver_parts(order, whole, space_part_rows)
    some_vectors = whole[5 * features // space_part_rows, :ROW_TILE].astype(jnp.float32)
    input_rows = place_slots(order, input_slots)
    grad_tokens = (grad_first[:row_count] + input_rows[:row_count].astype(jnp.float32))[None]
    return (
        block_out,
        grad_tokens,
        grad_time_project,
        grad_time_output,
        time_vectors[0:5],
        grad_space_project,
        grad_space_output,
        some_vectors[0:5],
        grad_feed_inner,
        some_vectors[8:12].reshape(-1),
        grad_feed_outer,
        some_vectors[5:8],
    )


def solution(mesh):
    placed = (
        P("frame", "batch", None),
        P("batch"),
        P("frame", "batch", None),
        P("batch", None),
        P("batch", None),
        P(None, "batch"),
        P("batch", None),
        P("batch", None),
        P(None, "batch"),
        P("batch", None),
        P("batch"),
        P("batch", None),
        P(None, "batch"),
    )
    return jax.shard_map(
        body,
        mesh=mesh,
        in_specs=placed,
        out_specs=(
            P("frame", "batch", None),
            P("frame", "batch", None),
            P(),
            P(),
            P(),
            P(),
            P(),
            P(),
            P(),
            P(),
            P(),
            P(),
        ),
        check_vma=False,
    )
```

```python
import functools
import math

import jax
import jax.numpy as jnp
from jax import lax
from jax.experimental import pallas as pl
from jax.experimental.pallas import tpu as pltpu
from jax.sharding import PartitionSpec as P

HEADS = 12
UNITS = 4
PATCHES = 784
LOG2E = 1.4426950408889634
ROW_TILE = 16
FEED_BLOCKS = 8


def round_up(count, step):
    return -(-count // step) * step


def struct(shape, dtype):
    return jax.ShapeDtypeStruct(shape, dtype)


VMEM = pl.BlockSpec(memory_space=pltpu.VMEM)
SMEM = pl.BlockSpec(memory_space=pltpu.SMEM)


class Order:
    def __init__(self, flags):
        self.flags = flags
        self.token = None

    def run(
        self, kernel, operands, in_specs, out_specs, out_shape, grid=(), scratch=(), prefetch=0, after=()
    ):
        token = [*after] if self.token is None else [self.token, *after]
        inputs, outputs, ordered = len(operands), len(out_shape), len(token)

        def body(*refs):
            refs = refs[:prefetch] + refs[prefetch + ordered :]
            token_ref = refs[inputs + outputs]
            token_ref[...] = jnp.zeros(token_ref.shape, token_ref.dtype)
            kernel(*refs[: inputs + outputs], *refs[inputs + outputs + 1 :])

        token_spec = pl.BlockSpec((8, 128), lambda *index: (0, 0))
        results = pl.pallas_call(
            body,
            grid_spec=pltpu.PrefetchScalarGridSpec(
                num_scalar_prefetch=prefetch,
                grid=grid,
                in_specs=[pl.BlockSpec(memory_space=pl.ANY)] * ordered + list(in_specs),
                out_specs=list(out_specs) + [token_spec],
                scratch_shapes=list(scratch),
            ),
            out_shape=list(out_shape) + [struct((8, 128), jnp.float32)],
            compiler_params=pltpu.CompilerParams(vmem_limit_bytes=56 << 20),
        )(*operands[:prefetch], *token, *operands[prefetch:])
        self.token = results[-1]
        return results[:-1]


def shift_frames(block, frame_count, shift):
    if shift % frame_count == 0:
        return block
    pairs = [(index, (index + shift) % frame_count) for index in range(frame_count)]
    return lax.ppermute(block, "frame", pairs)


def rows_to_frames(rows, frame_count, frame_index):
    part = rows.shape[0] // frame_count
    slots = []
    for shift in range(frame_count):
        owner = (frame_index + shift) % frame_count
        block = lax.dynamic_slice_in_dim(rows, owner * part, part, 0)
        slots.append(shift_frames(block, frame_count, shift))
    return slots


def send_back(slots):
    return [shift_frames(slot, len(slots), -shift) for shift, slot in enumerate(slots)]


def swap_bit(block, axis, size, bit):
    pairs = [(index, index ^ (1 << bit)) for index in range(size)]
    return lax.ppermute(block, axis, pairs)


def shuffle_kernel(plan, source_count, flags_ref, *refs):
    sources, outputs = refs[:source_count], refs[source_count:]

    def emit(output, at, rows, terms):
        steps = [step for step in range(ROW_TILE, 65, ROW_TILE) if rows % step == 0]
        step = max(steps, default=rows)

        def some(index, carry):
            def load(term):
                source, start = term
                if steps:
                    return sources[source][pl.ds(pl.multiple_of(start + index * step, ROW_TILE), step)]
                return sources[source][start : start + step]

            value = load(terms[0])
            if len(terms) > 1:
                total = value.astype(jnp.float32)
                for term in terms[1:]:
                    total = total + load(term).astype(jnp.float32)
                value = total.astype(output.dtype)
            if steps:
                output[pl.ds(pl.multiple_of(at + index * step, ROW_TILE), step)] = value
            else:
                output[at : at + step] = value
            return carry

        if rows // step == 1:
            some(0, 0)
        else:
            lax.fori_loop(0, rows // step, some, 0)

    for output, segments in zip(outputs, plan):
        at = 0
        for rows, flag, *choices in segments:
            for value, terms in enumerate(choices):

                @pl.when(flags_ref[flag] == value)
                def _():
                    emit(output, at, rows, terms)

            at += rows


def shuffle(order, requests, after):
    sources, plan, counts = [], [], []
    for own_sources, own_plan in requests:
        base = len(sources)

        def lift(terms):
            return tuple((source + base, start) for source, start in terms)

        plan += [
            [(rows, flag, *map(lift, choices)) for rows, flag, *choices in out] for out in own_plan
        ]
        sources += own_sources
        counts.append(len(own_plan))
    features = sources[0].shape[1]
    shapes = [struct((sum(segment[0] for segment in out), features), jnp.bfloat16) for out in plan]
    results = order.run(
        functools.partial(shuffle_kernel, plan, len(sources)),
        [order.flags, *sources],
        [SMEM] + [VMEM] * len(sources),
        [VMEM] * len(plan),
        shapes,
        after=after,
    )
    outputs = []
    for count in counts:
        outputs.append(results[:count])
        results = results[count:]
    return outputs


def split_plan(rows, flag, left, right):
    half = rows // 2
    low = ((left[0], left[1]), (right[0], right[1]))
    high = ((left[0], left[1] + half), (right[0], right[1] + half))
    return [[(half, flag, high, low)], [(half, flag, low, high)]]


def join_plan(rows, flag, own, arrived):
    return [(rows, flag, (own,), (arrived,)), (rows, flag, (arrived,), (own,))]


def frame_parts(rows, frame_count, flag, terms_at):
    part = rows // frame_count
    return [
        [
            (part, flag)
            + tuple(terms_at((frame + shift) % frame_count * part) for frame in range(frame_count))
        ]
        for shift in range(frame_count)
    ]


def send_parts(parts):
    return [shift_frames(part, len(parts), shift) for shift, part in enumerate(parts)]


def add_parts(rows, flag, frame_count):
    terms = tuple((source, 0) for source in range(frame_count))
    return [[(rows // frame_count, flag, *[terms] * frame_count)]]


def frame_steps(block, frame_count, flag):
    (block,) = yield [block]
    rows = block.shape[0]
    parts = yield [block], frame_parts(rows, frame_count, flag, lambda at: ((0, at),))
    parts = yield send_parts(parts)
    return list(parts), add_parts(rows, flag, frame_count)


def core_steps(pairs, batch_size):
    moved = yield [swap_bit(sent, "batch", batch_size, 0) for _, sent in pairs]
    sources, segments = [], []
    for (kept, _), arrived in zip(pairs, moved):
        terms = ((len(sources), 0), (len(sources) + 1, 0))
        segments.append((kept.shape[0], 0, terms, terms))
        sources += [kept, arrived]
    return sources, [segments]


def sum_chips(block, batch_size):
    groups = [list(range(core, batch_size, 2)) for core in range(2)]
    return lax.psum_scatter(
        block, "batch", scatter_dimension=0, axis_index_groups=groups, tiled=True
    )


def sum_steps(kept, sent, sizes, flag):
    wide = list(range(1, sizes[0].bit_length() - 1))
    ways = (wide, wide[::-1])
    frame_count = sizes[1]

    def over_batch(block, bit):
        return swap_bit(block, "batch", sizes[0], bit)

    (arrived,) = yield [over_batch(sent, 0)]
    rows = kept.shape[0] // 2
    sources = [kept, arrived]
    pairs = [((0, 0), (1, 0)), ((0, rows), (1, rows))]
    for level in range(len(wide)):
        plan = []
        for (left, right), way in zip(pairs, ways):
            plan += split_plan(rows, way[level], left, right)
        first_out, first_kept, second_out, second_kept = yield sources, plan
        moved = yield [over_batch(first_out, ways[0][level]), over_batch(second_out, ways[1][level])]
        sources = [first_kept, moved[0], second_kept, moved[1]]
        pairs = [((0, 0), (1, 0)), ((2, 0), (3, 0))]
        rows //= 2

    def terms_at(start):
        (left, right), at = pairs[start // rows], start % rows
        return (left[0], left[1] + at), (right[0], right[1] + at)

    parts = yield sources, frame_parts(2 * rows, frame_count, flag, terms_at)
    parts = yield send_parts(parts)
    (part,) = yield parts, add_parts(2 * rows, flag, frame_count)
    parts = yield [shift_frames(part, frame_count, shift) for shift in range(frame_count)]
    size = 2 * rows // frame_count
    segments = [
        (size, flag) + tuple((((frame - owner) % frame_count, 0),) for frame in range(frame_count))
        for owner in range(frame_count)
    ]
    blocks = yield parts, [segments[: frame_count // 2], segments[frame_count // 2 :]]
    for level in range(len(wide))[::-1]:
        moved = yield [over_batch(block, way[level]) for block, way in zip(blocks, ways)]
        sources = [blocks[0], moved[0], blocks[1], moved[1]]
        plan = [join_plan(rows, ways[0][level], (0, 0), (1, 0))]
        plan += [join_plan(rows, ways[1][level], (2, 0), (3, 0))]
        if level == 0:
            plan = [plan[0] + plan[1]]
        blocks = yield sources, plan
        rows *= 2
    (arrived,) = yield [over_batch(blocks[0], 0)]
    return blocks[0], arrived


def gather_steps(shard, batch_size):
    wide = list(range(1, batch_size.bit_length() - 1))
    ways = (wide, wide[::-1])
    half = shard.shape[0] // 2

    def over_batch(block, bit):
        return swap_bit(block, "batch", batch_size, bit)

    blocks = [shard[:half], shard[half:]]
    done = [[], []]
    for level in range(len(wide)):
        moved = yield [over_batch(block, way[level]) for block, way in zip(blocks, ways)]
        plan = []
        for index, way in enumerate(ways):
            bit, before = way[level], done[index]
            done[index] = sorted([*before, bit])
            segments = []
            for place in range(2 ** len(done[index])):
                value = {one: (place >> at) & 1 for at, one in enumerate(done[index])}
                row = half * sum(value[one] << at for at, one in enumerate(before))
                own, other = ((2 * index, row),), ((2 * index + 1, row),)
                segments.append((half, bit, *((other, own) if value[bit] else (own, other))))
            plan.append(segments)
        if level == len(wide) - 1:
            plan = [plan[0] + plan[1]]
        blocks = yield [blocks[0], moved[0], blocks[1], moved[1]], plan
    (block,) = blocks
    (arrived,) = yield [over_batch(block, 0)]
    segments = []
    for place in range(batch_size):
        for index in range(2):
            row = (index * batch_size // 2 + (place >> 1)) * half
            own, other = ((0, row),), ((1, row),)
            segments.append((half, 0, *((other, own) if place & 1 else (own, other))))
    (whole,) = yield [block, arrived], [segments]
    return whole


class Flight:
    def __init__(self, steps):
        self.steps, self.result = steps, None
        self.moved = next(steps)

    def send(self, value):
        try:
            return self.steps.send(value)
        except StopIteration as stop:
            self.result = stop.value
            return None


def advance(order, *flights, after=()):
    active, requests = [], []
    for flight in flights:
        if flight.result is not None:
            continue
        request = flight.send(flight.moved)
        if request is None and isinstance(flight.result[0], list):
            request = flight.result
        if request is not None:
            active.append(flight)
            requests.append(request)
    if requests:
        for flight, outputs in zip(active, shuffle(order, requests, after)):
            if flight.result is None:
                flight.moved = flight.send(outputs)
            else:
                flight.result = outputs


def finish_together(order, *flights):
    sources, segments = [], []
    for flight in flights:
        if flight.result is None:
            flight.send(flight.moved)
            parts, ((segment,),) = flight.result
        else:
            parts = flight.result
            segment = (parts[0].shape[0], 0, ((0, 0),), ((0, 0),))
        rows, flag, *choices = segment
        base = len(sources)
        segments.append(
            (rows, flag, *[tuple((source + base, at) for source, at in terms) for terms in choices])
        )
        sources += parts
    ((whole,),) = shuffle(order, [(sources, [segments])], ())
    return whole


def deliver_kernel(flags_ref, own_ref, arrived_ref, out_ref, rest_ref):
    half, features = own_ref.shape
    columns = out_ref.shape[1] // features
    for core in range(2):

        @pl.when(flags_ref[0] == core)
        def _():
            for index in range(columns + 1):
                first = index * features
                height = features if index < columns else rest_ref.shape[0]
                while height:
                    owner, at = divmod(first, half)
                    size = min(height, half - at)
                    piece = (own_ref if owner == core else arrived_ref)[at : at + size]
                    piece = piece.astype(jnp.float32)
                    row = first % features
                    if index < columns:
                        span = slice(index * features, (index + 1) * features)
                        out_ref[row : row + size, span] = piece
                    else:
                        rest_ref[row : row + size] = piece
                    first, height = first + size, height - size


def deliver_halves(order, own, arrived):
    half, features = own.shape
    columns = 2 * half // features
    return order.run(
        deliver_kernel,
        [order.flags, own, arrived],
        [SMEM, VMEM, VMEM],
        [VMEM, VMEM],
        [struct((features, columns * features), jnp.float32), struct((8, features), jnp.float32)],
    )


def deliver_parts_kernel(outputs, counts, *refs):
    steps = pl.program_id(0)
    feed_refs, space_refs = refs[: counts[0]], refs[counts[0] : sum(counts)]
    for output, (first, last, _) in zip(refs[sum(counts) :], outputs):

        @pl.when((steps >= first) & (steps < last))
        def _():
            sources = feed_refs if last <= FEED_BLOCKS else space_refs
            rows = sources[0].shape[1]
            for piece in range(sources[0].shape[0]):
                for index, source in enumerate(sources):
                    at = (piece * len(sources) + index) * rows
                    output[at : at + rows] = source[piece].astype(output.dtype)


def deliver_parts(order, gathered, space_part):
    _, part, features = gathered.shape
    feed_part = part - space_part
    unit = math.gcd(space_part, feed_part)

    def source(rows, first, step_of, index):
        def place(step):
            return step_of(step), first // unit + index, 0

        return pl.BlockSpec((features // rows, unit, features), place)

    counts = (feed_part // unit, space_part // unit)
    feed_specs = [
        source(feed_part, space_part, lambda step: jnp.minimum(step, FEED_BLOCKS - 1), index)
        for index in range(counts[0])
    ]
    space_specs_ = [
        source(space_part, 0, lambda step: jnp.maximum(step - FEED_BLOCKS, 0), index)
        for index in range(counts[1])
    ]
    half = FEED_BLOCKS // 2
    outputs = [(0, half, True), (half, FEED_BLOCKS, False)]
    for first, last, wide in ((0, 3, True), (3, 4, False), (4, 5, False)):
        outputs.append((FEED_BLOCKS + first, FEED_BLOCKS + last, wide))

    def spot(first, last, wide):
        def index(step):
            at = jnp.clip(step - first, 0, last - first - 1)
            return (0, at) if wide else (at, 0)

        return pl.BlockSpec((features, features), index)

    def shape(first, last, wide):
        rows = (last - first) * features
        return struct((features, rows) if wide else (rows, features), jnp.float32)

    return order.run(
        functools.partial(deliver_parts_kernel, outputs, counts),
        [gathered] * sum(counts),
        feed_specs + space_specs_,
        [spot(*item) for item in outputs],
        [shape(*item) for item in outputs],
        grid=(outputs[-1][1],),
    )


def contract(x,y,dims):
    return lax.dot_general(x,y,((dims[0:1],dims[1:2]),((),())),preferred_element_type=jnp.float32)

def widen_rows(values, wide):
    rows, width = values.shape
    if wide == rows:
        return values
    return jnp.concatenate([values, jnp.zeros((wide - rows, width), values.dtype)])


def head_halves(width):
    lane = lax.broadcasted_iota(jnp.int32, (1, width), 1)
    return [lane < width // 2, lane >= width // 2]

def space_forward_kernel(
    scale, mark_q_ref, mark_k_ref, q_ref, k_ref, v_ref, mixture_ref, total_ref, k_wide, v_wide
):
    rows, width = q_ref.shape
    wide = k_wide.shape[0]
    if wide > rows:

        @pl.when(pl.program_id(0) == 0)
        def _():
            k_wide[rows:] = jnp.zeros((wide - rows, width), k_wide.dtype)
            v_wide[rows:] = jnp.zeros((wide - rows, width), v_wide.dtype)

    k_wide[:rows] = k_ref[...]
    v_wide[:rows] = v_ref[...]
    halves = head_halves(width)
    one = jnp.ones((), q_ref.dtype)
    outs, tops = [], []
    for half in halves:
        queries = jnp.where(half, q_ref[...], mark_q_ref[:rows])
        keys = jnp.where(half, k_wide[...], mark_k_ref[...])
        scores = contract(queries, keys, (1, 1)) * (scale * LOG2E)
        top = jnp.max(scores, axis=1, keepdims=True)
        weights = jnp.exp2(scores - top)
        values = jnp.where(half, v_wide[...], one)
        outs.append(contract(weights.astype(jnp.bfloat16), values, (1, 0)))
        tops.append(top)
    mass = pltpu.roll(jnp.where(halves[0], outs[1], outs[0]), width // 2, 1)
    mixture = jnp.where(halves[0], outs[0], outs[1]) / mass
    mixture_ref[...] = mixture.astype(mixture_ref.dtype)
    total_ref[...] = jnp.where(halves[0], tops[0], tops[1]) + jnp.log2(mass)


def space_specs(rows, features):
    pairs = HEADS // 2
    width = features // pairs
    wide = round_up(rows, 128)
    fixed = [pl.BlockSpec((wide, width), lambda i: (0, 0))] * 2
    blocks = [pl.BlockSpec((rows, width), lambda i, o=o: (0, o + i)) for o in (0, pairs, 2 * pairs)]
    out = pl.BlockSpec((rows, width), lambda i: (0, i))
    scratch = [pltpu.VMEM((wide, width), jnp.bfloat16)] * 2
    return pairs, (features // HEADS) ** -0.5, fixed + blocks, out, scratch


def clip_marks(clip, width):
    rows = clip.shape[0]
    clip = jnp.pad(clip, (0, round_up(rows, 128) - rows), constant_values=-2)
    same = (clip[:, None] + 2) == jnp.arange(width, dtype=jnp.int32)[None] % (width // 2)
    return same.astype(jnp.bfloat16), jnp.where(same, 0.0, -1e30).astype(jnp.bfloat16)


def space_forward(order, qkv, clip, features):
    rows = qkv.shape[0]
    pairs, scale, specs, out, scratch = space_specs(rows, features)
    return order.run(
        functools.partial(space_forward_kernel, scale),
        [*clip_marks(clip, features // pairs), qkv, qkv, qkv],
        specs,
        [out, out],
        [struct((rows, features), jnp.bfloat16), struct((rows, features), jnp.float32)],
        grid=(pairs,),
        scratch=scratch,
    )


def space_backward_kernel(
    scale, mark_q_ref, mark_k_ref, q_ref, k_ref, v_ref, mixture_ref, total_ref, grad_ref, dq_ref, dk_ref, dv_ref,
    q_wide, g_wide
):
    rows, width = q_ref.shape
    wide = q_wide.shape[0]
    if wide > rows:

        @pl.when(pl.program_id(0) == 0)
        def _():
            q_wide[rows:] = jnp.zeros((wide - rows, width), q_wide.dtype)
            g_wide[rows:] = jnp.zeros((wide - rows, width), g_wide.dtype)

    q_wide[:rows] = q_ref[...]
    g_wide[:rows] = grad_ref[...]
    halves = head_halves(width)
    zero = jnp.zeros((), q_ref.dtype)
    product = grad_ref[...].astype(jnp.float32) * mixture_ref[...].astype(jnp.float32)
    sums = [jnp.sum(jnp.where(half, product, 0.0), axis=1, keepdims=True) for half in halves]
    delta = widen_rows(jnp.where(halves[0], sums[0], sums[1]), wide).T
    total = widen_rows(total_ref[...], wide).T
    dq, dk, dv = [], [], []
    for index, half in enumerate(halves):
        at = index * (width // 2)
        queries = jnp.where(half, q_wide[...], mark_q_ref[...])
        keys = jnp.where(half, k_ref[...], mark_k_ref[:rows])
        values = jnp.where(half, v_ref[...], zero)
        scores = contract(keys, queries, (1, 1)) * (scale * LOG2E)
        weights = jnp.exp2(scores - total[at : at + 1])
        slopes = contract(values, g_wide[...], (1, 1))
        slopes = (weights * (slopes - delta[at : at + 1])).astype(jnp.bfloat16)
        dv.append(contract(weights.astype(jnp.bfloat16), g_wide[...], (1, 0)))
        dk.append(contract(slopes, q_wide[...], (1, 0)))
        dq.append(contract(slopes, k_ref[...], (0, 0)))
    dk_ref[...] = (jnp.where(halves[0], dk[0], dk[1]) * scale).astype(dk_ref.dtype)
    dv_ref[...] = jnp.where(halves[0], dv[0], dv[1]).astype(dv_ref.dtype)
    dq_ref[...] = (jnp.where(halves[0], dq[0], dq[1])[:rows] * scale).astype(dq_ref.dtype)


def space_backward(order, qkv, mixture, total, grad, clip, features):
    rows = qkv.shape[0]
    pairs, scale, specs, out, scratch = space_specs(rows, features)
    return order.run(
        functools.partial(space_backward_kernel, scale),
        [*clip_marks(clip, features // pairs), qkv, qkv, qkv, mixture, total, grad],
        specs + [out] * 3,
        [out] * 3,
        [struct((rows, features), jnp.bfloat16)] * 3,
        grid=(pairs,),
        scratch=scratch,
    )


def norm_parts(values):
    average = jnp.mean(values, axis=1, keepdims=True)
    centered = values - average
    spread = lax.rsqrt(jnp.mean(centered * centered, axis=1, keepdims=True) + 1e-06)
    return centered * spread, spread
def norm_back(grad, normed, spread, gain):
    scaled = grad * gain
    return spread * (scaled - jnp.mean(scaled, axis=1, keepdims=True) - normed * jnp.mean(scaled * normed, axis=1, keepdims=True))
def column_sum(values):
    return jnp.sum(values, axis=0, keepdims=True)

def square_spec(packed, index):
    batch_count, _, features = packed.shape
    return pl.BlockSpec((batch_count, features // batch_count, features), lambda i: (0, index, 0))


def square(ref):
    return ref[...].reshape(-1, ref.shape[-1])


def feed_kernel(chunks, x1_ref, mixture_ref, dz_ref, so_ref, fi_ref, fo_ref, fb_ref, vec_ref,
                out_ref, dx2_ref, dys_ref, dos_ref, grad_ref, gfb_ref, gvec_ref,
                x2_s, a3_s, a3t_s, acc_s, da_s, g_s, dh_s):
    step = pl.program_id(0)
    rows = x1_ref.shape[0]
    @pl.when(step == 0)
    def _():
        x2 = x1_ref[...] + contract(mixture_ref[...], square(so_ref), (1, 0)) + vec_ref[9:10]
        x2_s[...] = x2
        normed, _ = norm_parts(x2)
        a3 = (normed * vec_ref[10:11] + vec_ref[11:12]).astype(jnp.bfloat16)
        a3_s[...] = a3
        a3t_s[...] = a3.T
        acc_s[...] = x2 + vec_ref[12:13]
        da_s[...] = jnp.zeros_like(da_s)
    inner, outer = square(fi_ref), square(fo_ref)
    part = rows // chunks
    for chunk in range(chunks):
        span = slice(chunk * part, (chunk + 1) * part)
        hidden = contract(a3_s[span], inner, (1, 0)) + fb_ref[...]
        cdf = 0.5 + 0.5 * lax.erf(hidden * math.sqrt(0.5))
        slope = cdf + hidden * jnp.exp(hidden * hidden * -0.5) * (1.0 / math.sqrt(2.0 * math.pi))
        active = (hidden * cdf).astype(jnp.bfloat16)
        g_s[span] = active
        dh = (contract(dz_ref[span], outer, (1, 1)) * slope).astype(jnp.bfloat16)
        dh_s[span] = dh
        acc_s[span] += contract(active, outer, (1, 0))
        da_s[span] += contract(dh, inner, (1, 1))
    grad_ref[0] = contract(a3t_s[...], dh_s[...], (1, 0)).astype(grad_ref.dtype)
    grad_ref[1] = contract(g_s[...], dz_ref[...], (0, 0)).astype(grad_ref.dtype)
    gfb_ref[...] = column_sum(dh_s[...].astype(jnp.float32))
    @pl.when(step == pl.num_programs(0) - 1)
    def _():
        out_ref[0] = acc_s[: out_ref.shape[1]].astype(out_ref.dtype)
        normed, spread = norm_parts(x2_s[...])
        grad = da_s[...]
        dz = dz_ref[...].astype(jnp.float32)
        dx2 = dz + norm_back(grad, normed, spread, vec_ref[10:11])
        dx2_ref[...] = dx2
        dys = dx2.astype(jnp.bfloat16)
        dys_ref[...] = dys
        dos_ref[...] = contract(dys, square(so_ref), (1, 1)).astype(dos_ref.dtype)
        gvec_ref[0:1] = column_sum(grad * normed)
        gvec_ref[1:2] = column_sum(grad)
        gvec_ref[2:3] = column_sum(dz)
        gvec_ref[3:4] = column_sum(dys.astype(jnp.float32))
        gvec_ref[4:8] = jnp.zeros((4, gvec_ref.shape[1]), jnp.float32)

def feed_block(order, row_count, x1, mixture, dz, feed_packed, bias, vec, chunks):
    rows, features = x1.shape
    batch_count = feed_packed.shape[0]
    hidden = bias.shape[1]
    whole = pl.BlockSpec((rows, features), lambda j: (0, 0))
    line = pl.BlockSpec((1, features), lambda j: (0, j))
    shard = hidden // batch_count
    low, full = jnp.bfloat16, jnp.float32
    return order.run(
        functools.partial(feed_kernel, chunks),
        [x1, mixture, dz, feed_packed, feed_packed, feed_packed, bias, vec],
        [
            whole,
            whole,
            whole,
            square_spec(feed_packed, 2 * hidden // features),
            pl.BlockSpec((batch_count, features // batch_count, features), lambda j: (0, j, 0)),
            pl.BlockSpec((features // shard, shard, features), lambda j: (j, 1, 0)),
            line,
            pl.BlockSpec(vec.shape, lambda j: (0, 0)),
        ],
        [
            pl.BlockSpec((1, row_count, features), lambda j: (0, 0, 0)),
            whole,
            whole,
            whole,
            pl.BlockSpec((2, features, features), lambda j: (0, j, 0)),
            line,
            pl.BlockSpec((8, features), lambda j: (0, 0)),
        ],
        [
            struct((1, row_count, features), low),
            struct((rows, features), full),
            struct((rows, features), low),
            struct((rows, features), low),
            struct((2, hidden, features), low),
            struct((1, hidden), full),
            struct((8, features), full),
        ],
        grid=(hidden // features,),
        scratch=[
            pltpu.VMEM((rows, features), full),
            pltpu.VMEM((rows, features), low),
            pltpu.VMEM((features, rows), low),
            pltpu.VMEM((rows, features), full),
            pltpu.VMEM((rows, features), full),
            pltpu.VMEM((rows, features), low),
            pltpu.VMEM((rows, features), low),
        ],
    )


def gather_rows(count, frame, slots, rows_s):
    part = slots[0].shape[0]
    for shift in range(count):
        owner = lax.rem(frame + shift, count)
        rows_s[pl.ds(pl.multiple_of(owner * part, ROW_TILE), part)] = slots[shift][...]


def middle_kernel(count, frame_flag, flags_ref, token_ref, *refs):
    slots, (to_ref, *sp_refs, vec_ref) = refs[:count], refs[count : count + 5]
    mixture_ref, x1_ref, a2_ref, qkv_ref = refs[count + 5 :]
    rows, features = token_ref.shape
    gather_rows(count, flags_ref[frame_flag], slots, mixture_ref)
    number = lax.broadcasted_iota(jnp.int32, (rows, 1), 0)
    branch = contract(mixture_ref[...], square(to_ref), (1, 0)) + vec_ref[4:5]
    x1 = token_ref[...].astype(jnp.float32) + jnp.where(number < PATCHES, branch, 0.0)
    x1_ref[...] = x1
    normed, _ = norm_parts(x1)
    a2 = (normed * vec_ref[5:6] + vec_ref[6:7]).astype(jnp.bfloat16)
    a2_ref[...] = a2
    for third in range(3):
        span = slice(third * features, (third + 1) * features)
        joined = contract(a2, square(sp_refs[third]), (1, 0))
        if third != 1:
            joined = joined + vec_ref[7 + third // 2 : 8 + third // 2]
        qkv_ref[:, span] = joined.astype(jnp.bfloat16)


def project_specs(packed, vec):
    return [square_spec(packed, index) for index in range(4)] + [
        pl.BlockSpec(vec.shape, lambda i: (0, 0))
    ]


def middle_forward(order, tokens, slots, packed, vec):
    rows, features = tokens.shape
    low = jnp.bfloat16
    return order.run(
        functools.partial(middle_kernel, len(slots), order.flags.shape[0] - 1),
        [order.flags, tokens, *slots, *[packed] * 4, vec],
        [SMEM] + [VMEM] * (len(slots) + 1) + project_specs(packed, vec),
        [VMEM] * 4,
        [
            struct((rows, features), low),
            struct((rows, features), jnp.float32),
            struct((rows, features), low),
            struct((rows, 3 * features), low),
        ],
        grid=(1,),
    )


def middle_back_kernel(
    sizes, part, flags_ref, dq_ref, dk_ref, dv_ref, x1_ref, dx2_ref, to_ref, *refs
):
    *sp_refs, vec_ref, time_ref, feed_ref, bias_ref = refs[:7]
    dx1_ref, sums_ref, kept_ref, sent_ref = refs[7:11]
    count = sizes[1]
    slots, rows_s = refs[11 : 11 + count], refs[11 + count]
    rows, features = x1_ref.shape
    grad = 0.0
    for third, piece in enumerate((dq_ref, dk_ref, dv_ref)):
        grad = grad + contract(piece[...], square(sp_refs[third]), (1, 1))
    normed, spread = norm_parts(x1_ref[...])
    dx1 = dx2_ref[...] + norm_back(grad, normed, spread, vec_ref[5:6])
    dx1_ref[...] = dx1
    number = lax.broadcasted_iota(jnp.int32, (rows, 1), 0)
    dyt = jnp.where(number < PATCHES, dx1, 0.0).astype(jnp.bfloat16)
    rows_s[...] = contract(dyt, square(to_ref), (1, 1)).astype(rows_s.dtype)
    block = rows // count
    for shift in range(count):
        owner = lax.rem(flags_ref[flags_ref.shape[0] - 1] + shift, count)
        slots[shift][...] = rows_s[pl.ds(pl.multiple_of(owner * block, ROW_TILE), block)]
    sums_ref[0:1] = column_sum(grad * normed)
    sums_ref[1:2] = column_sum(grad)
    sums_ref[2:3] = column_sum(dq_ref[...].astype(jnp.float32))
    sums_ref[3:4] = column_sum(dv_ref[...].astype(jnp.float32))
    sums_ref[4:5] = column_sum(dyt.astype(jnp.float32))
    sums_ref[5:8] = jnp.zeros((3, features), jnp.float32)
    first = 4 * features
    put = functools.partial(put_parts, flags_ref, kept_ref, sent_ref, sizes, part, first)
    put(first, contract(time_ref[...], dyt, (0, 0)))
    bias = bias_ref[...]
    lines = [bias[:, at : at + features] for at in range(0, bias.shape[1], features)]
    pieces = [sums_ref[0:4], feed_ref[3:4], feed_ref[0:3], *lines]
    put(first + features, fill_rows(pieces, 2 * kept_ref.shape[0] - features, features))


def middle_backward(order, sizes, dq, dk, dv, x1, dx2, packed, vec, mixture, feed_sums, bias):
    rows, features = x1.shape
    count = sizes[1]
    low, full = jnp.bfloat16, jnp.float32
    total, part = space_rows(sizes, features)
    half = struct(((total - 4 * features) // 2, features), low)
    results = order.run(
        functools.partial(middle_back_kernel, sizes, part),
        [order.flags, dq, dk, dv, x1, dx2, *[packed] * 4, vec, mixture, feed_sums, bias],
        [SMEM] + [VMEM] * 5 + project_specs(packed, vec) + [VMEM] * 3,
        [VMEM] * (4 + count),
        [struct((rows, features), full), struct((8, features), full), half, half]
        + [struct((rows // count, features), low)] * count,
        grid=(1,),
        scratch=[pltpu.VMEM((rows, features), low)],
    )
    return results[0], results[1], results[2:4], results[4:]


def put_half(core_ref, kept_ref, sent_ref, at, value):
    half = kept_ref.shape[0]
    low = value.astype(kept_ref.dtype)
    part = math.gcd(half, low.shape[0])
    for offset in range(0, low.shape[0], part):
        owner, first = divmod(at + offset, half)
        piece = low[offset : offset + part]

        @pl.when(core_ref[0] == owner)
        def _():
            kept_ref[first : first + part] = piece

        @pl.when(core_ref[0] != owner)
        def _():
            sent_ref[first : first + part] = piece


def fill_rows(pieces, rows, features):
    used = sum(piece.shape[0] for piece in pieces)
    return jnp.concatenate([*pieces, jnp.zeros((rows - used, features), jnp.float32)])


def put_parts(core_ref, kept_ref, sent_ref, sizes, part, first, at, value):
    low = value.astype(kept_ref.dtype)
    for offset in range(0, low.shape[0], part):
        batch, frame = divmod((at + offset) // part, sizes[1])
        start = ((batch >> 1) * sizes[1] + frame) * part - first // 2
        piece = low[offset : offset + part]

        @pl.when(core_ref[0] == batch & 1)
        def _():
            kept_ref[start : start + part] = piece

        @pl.when(core_ref[0] != batch & 1)
        def _():
            sent_ref[start : start + part] = piece


def space_rows(sizes, features):
    rows = round_up(5 * features + ROW_TILE, sizes[0] * sizes[1] * ROW_TILE)
    return rows, rows // (sizes[0] * sizes[1])


def space_weights_kernel(
    sizes, part, flags_ref, a2_ref, dq_ref, dk_ref, dv_ref, mixture_ref, dys_ref, kept_ref, sent_ref
):
    features = a2_ref.shape[1]
    put = functools.partial(put_parts, flags_ref, kept_ref, sent_ref, sizes, part, 0)
    turned = a2_ref[...].T
    for third, piece in enumerate((dq_ref, dk_ref, dv_ref)):
        put(third * features, contract(turned, piece[...], (1, 0)))
    put(3 * features, contract(mixture_ref[...], dys_ref[...], (0, 0)))


def space_weights(order, sizes, *operands):
    features = operands[0].shape[1]
    part = space_rows(sizes, features)[1]
    half = struct((2 * features, features), jnp.bfloat16)
    return order.run(
        functools.partial(space_weights_kernel, sizes, part),
        [order.flags, *operands],
        [SMEM] + [VMEM] * len(operands),
        [VMEM] * 2,
        [half, half],
    )


CHUNK = 16
def head_map(features, lanes=128):
    head = jnp.arange(features, dtype=jnp.int32) // (features // HEADS)
    return (head[:, None] == jnp.arange(lanes, dtype=jnp.int32)[None]).astype(jnp.bfloat16)

def pair_sums(left, right, gather_ref, pair_s):
    count = len(left)
    for f in range(count):
        for g in range(count):
            at = (f * count + g) * CHUNK
            pair_s[at:at + CHUNK] = (left[f] * right[g]).astype(jnp.bfloat16)
    return contract(pair_s[...], gather_ref[...], (1, 0))

def time_forward_kernel(count, scale, *refs):
    slots, (tp_ref, vec_ref, gather_ref, spread_ref) = refs[:count], refs[count:count + 4]
    outs, (qkv_ref, prob_ref, a1_ref) = refs[count + 4:2 * count + 4], refs[2 * count + 4:2 * count + 7]
    pair_s, weight_s = refs[2 * count + 7:]
    part, features = slots[0].shape
    for s in range(count):
        normed, _ = norm_parts(slots[s][...].astype(jnp.float32))
        a1_ref[s * part:(s + 1) * part] = (normed * vec_ref[0:1] + vec_ref[1:2]).astype(jnp.bfloat16)
    for third in range(3):
        span = slice(third * features, (third + 1) * features)
        joined = contract(a1_ref[...], tp_ref[:, span], (1, 0))
        if third != 1:
            joined = joined + vec_ref[2 + third // 2:3 + third // 2]
        qkv_ref[:, span] = joined.astype(jnp.bfloat16)

    def chunk_step(index, carry):
        def rows_of(s, third):
            start = pl.multiple_of(s * part + index * CHUNK, CHUNK)
            return qkv_ref[pl.ds(start, CHUNK), third * features:(third + 1) * features].astype(jnp.float32)
        queries, keys, values = ([rows_of(s, third) for s in range(count)] for third in range(3))
        scores = pair_sums(queries, keys, gather_ref, pair_s) * (scale * LOG2E)
        place = pl.ds(pl.multiple_of(index * CHUNK, CHUNK), CHUNK)
        for f in range(count):
            row = [scores[(f * count + g) * CHUNK:(f * count + g + 1) * CHUNK] for g in range(count)]
            top = functools.reduce(jnp.maximum, row)
            raised = [jnp.exp2(item - top) for item in row]
            mass = functools.reduce(jnp.add, raised)
            for g in range(count):
                weight = raised[g] / mass
                prob_ref[f * count + g, place] = weight
                at = (f * count + g) * CHUNK
                weight_s[at:at + CHUNK] = weight.astype(jnp.bfloat16)
        wide = contract(weight_s[...], spread_ref[...], (1, 0))
        for f in range(count):
            total = 0.0
            for g in range(count):
                at = (f * count + g) * CHUNK
                total = total + wide[at:at + CHUNK] * values[g]
            outs[f][place] = total.astype(jnp.bfloat16)
        return carry
    lax.fori_loop(0, part // CHUNK, chunk_step, 0, unroll=True)

def time_forward(order, slots, time_weight, vec):
    count = len(slots)
    part, features = slots[0].shape
    gather = head_map(features)
    low, full = jnp.bfloat16, jnp.float32
    results = order.run(
        functools.partial(time_forward_kernel, count, (features // HEADS) ** -0.5),
        [*slots, time_weight, vec, gather, gather.T],
        [VMEM] * count + [pl.BlockSpec((features, 3 * features), lambda i: (0, 0)), VMEM, VMEM, VMEM],
        [VMEM] * (count + 3),
        [struct((part, features), low)] * count
        + [
            struct((count * part, 3 * features), low),
            struct((count * count, part, 128), full),
            struct((count * part, features), low),
        ],
        grid=(1,),
        scratch=[
            pltpu.VMEM((count * count * CHUNK, features), low),
            pltpu.VMEM((count * count * CHUNK, 128), low),
        ],
    )
    return results[:count], results[count], results[count + 1], results[count + 2]


def time_backward_kernel(count, scale, flags_ref, *refs):
    grads, slots = refs[:count], refs[count : 2 * count]
    qkv_ref, prob_ref, a1_ref, gather_ref, spread_ref, tp_ref, vec_ref, other_ref = refs[2 * count : 2 * count + 8]
    refs = refs[2 * count + 8 :]
    outs, (kept_ref, sent_ref, dqkv_ref, pair_s, weight_s) = refs[:count], refs[count:]
    part, features = grads[0].shape
    def chunk_step(index, carry):
        place = pl.ds(pl.multiple_of(index * CHUNK, CHUNK), CHUNK)
        def rows_of(s, third):
            start = pl.multiple_of(s * part + index * CHUNK, CHUNK)
            return qkv_ref[pl.ds(start, CHUNK), third * features:(third + 1) * features].astype(jnp.float32)
        queries, keys, values = ([rows_of(s, third) for s in range(count)] for third in range(3))
        outer = [grads[s][place].astype(jnp.float32) for s in range(count)]
        slopes = pair_sums(outer, values, gather_ref, pair_s)
        size = count * count * CHUNK
        for f in range(count):
            row = [slopes[(f * count + g) * CHUNK:(f * count + g + 1) * CHUNK] for g in range(count)]
            weights = [prob_ref[f * count + g, place] for g in range(count)]
            delta = functools.reduce(jnp.add, [w * s for w, s in zip(weights, row)])
            for g in range(count):
                at = (f * count + g) * CHUNK
                weight_s[at:at + CHUNK] = weights[g].astype(jnp.bfloat16)
                weight_s[size + at:size + at + CHUNK] = (weights[g] * (row[g] - delta)).astype(jnp.bfloat16)
        wide = contract(weight_s[...], spread_ref[...], (1, 0))
        for s in range(count):
            dq, dk, dv = 0.0, 0.0, 0.0
            for t in range(count):
                forth, back = (s * count + t) * CHUNK, (t * count + s) * CHUNK
                dq = dq + wide[size + forth:size + forth + CHUNK] * keys[t]
                dk = dk + wide[size + back:size + back + CHUNK] * queries[t]
                dv = dv + wide[back:back + CHUNK] * outer[t]
            start = pl.ds(pl.multiple_of(s * part + index * CHUNK, CHUNK), CHUNK)
            for third, value in enumerate((dq * scale, dk * scale, dv)):
                dqkv_ref[start, third * features:(third + 1) * features] = value.astype(jnp.bfloat16)
        return carry
    lax.fori_loop(0, part // CHUNK, chunk_step, 0, unroll=True)
    a1t = a1_ref[...].T
    put = functools.partial(put_half, flags_ref, kept_ref, sent_ref)
    for third in range(3):
        span = slice(third * features, (third + 1) * features)
        put(third * features, contract(a1t, dqkv_ref[:, span], (1, 0)))
    grad = contract(dqkv_ref[...], tp_ref[...], (1, 1))
    gain, shift = 0.0, 0.0
    for s in range(count):
        piece = grad[s * part : (s + 1) * part]
        normed, spread = norm_parts(slots[s][...].astype(jnp.float32))
        outs[s][...] = norm_back(piece, normed, spread, vec_ref[0:1]).astype(jnp.bfloat16)
        gain = gain + column_sum(piece * normed)
        shift = shift + column_sum(piece)
    sums = [
        gain,
        shift,
        column_sum(dqkv_ref[:, :features].astype(jnp.float32)),
        column_sum(dqkv_ref[:, 2 * features :].astype(jnp.float32)),
        other_ref[4:5],
    ]
    put(3 * features, fill_rows(sums, 2 * kept_ref.shape[0] - 3 * features, features))


def time_backward(order, grads, slots, qkv, prob, a1, time_weight, vec, other):
    count = len(grads)
    part, features = grads[0].shape
    gather = head_map(features)
    low = jnp.bfloat16
    half = struct((round_up(3 * features + 16, 512) // 2, features), low)
    results = order.run(
        functools.partial(time_backward_kernel, count, (features // HEADS) ** -0.5),
        [order.flags, *grads, *slots, qkv, prob, a1, gather, gather.T, time_weight, vec, other],
        [SMEM] + [VMEM] * (2 * count + 5)
        + [pl.BlockSpec((features, 3 * features), lambda i: (0, 0)), VMEM, VMEM],
        [VMEM] * (count + 2),
        [struct((part, features), low)] * count + [half, half],
        grid=(1,),
        scratch=[
            pltpu.VMEM(qkv.shape, low),
            pltpu.VMEM((count * count * CHUNK, features), low),
            pltpu.VMEM((2 * count * count * CHUNK, 128), low),
        ],
    )
    return results[:count], results[count], results[count + 1]


def place_kernel(flags_ref, first_ref, *refs):
    slots, out_ref, rows_s = refs[:-2], refs[-2], refs[-1]
    gather_rows(len(slots), flags_ref[flags_ref.shape[0] - 1], slots, rows_s)
    lanes = out_ref.shape[1]
    parts = first_ref.shape[1] // lanes
    rows = out_ref.shape[0] // parts
    for index in range(parts):
        span = slice(index * lanes, (index + 1) * lanes)
        total = first_ref[:rows, span] + rows_s[:rows, span].astype(jnp.float32)
        out_ref[pl.ds(index, rows, stride=parts)] = total


def add_slots(order, first, slots, row_count):
    features = first.shape[1]
    return order.run(
        place_kernel,
        [order.flags, first, *slots],
        [SMEM] + [VMEM] * (len(slots) + 1),
        [VMEM],
        [struct((row_count * features // 128, 128), jnp.float32)],
        scratch=[pltpu.VMEM(first.shape, slots[0].dtype)],
    )[0]


def body(
    tokens,
    size_tag,
    cotangent,
    time_project,
    time_output,
    time_vector,
    space_project,
    space_output,
    space_vector,
    feed_inner,
    feed_bias,
    feed_outer,
    feed_vector,
):
    frame_count = lax.axis_size("frame")
    batch_count = lax.axis_size("batch")
    sizes = (batch_count, frame_count)
    frame_index = lax.axis_index("frame")
    batch_index = lax.axis_index("batch")
    flags = [(batch_index >> bit) & 1 for bit in range(batch_count.bit_length() - 1)]
    frame_flag = len(flags)
    order = Order(jnp.stack([*flags, frame_index]).astype(jnp.int32))
    features = tokens.shape[2]
    row_count = tokens.shape[1]
    part = round_up(-(-PATCHES // frame_count), ROW_TILE)
    padded = part * frame_count

    time_weight = lax.all_gather(time_project, "batch", axis=0, tiled=True)
    token_rows = jnp.pad(tokens[0], ((0, padded - row_count), (0, 0)))
    grad_result = jnp.pad(cotangent[0], ((0, padded - row_count), (0, 0)))
    slots = rows_to_frames(token_rows, frame_count, frame_index)
    vectors = jnp.concatenate(
        [time_vector, space_vector, feed_vector, feed_bias.reshape(-1, time_vector.shape[1])], axis=0
    )
    vectors = lax.all_gather(vectors, "batch", axis=0)
    vec = vectors[:, :13].transpose(1, 0, 2).reshape(13, features).astype(jnp.float32)
    vec = jnp.pad(vec, ((0, 3), (0, 0)))
    feed_bias_row = vectors[:, 13:].reshape(1, -1).astype(jnp.float32)

    def stack_columns(weight):
        return [weight[:, at : at + features] for at in range(0, weight.shape[1], features)]

    feed_packed = jnp.concatenate([*stack_columns(feed_inner), feed_outer, space_output], axis=0)
    feed_packed = lax.all_gather(feed_packed, "batch", axis=0)
    clip = jnp.concatenate(
        [
            jnp.arange(PATCHES, dtype=jnp.int32) // size_tag[0],
            jnp.arange(UNITS, dtype=jnp.int32),
            jnp.full((padded - PATCHES - UNITS,), -1, jnp.int32),
        ]
    )

    packed = jnp.concatenate([time_output, *stack_columns(space_project)], axis=0)
    weight_flight = Flight(gather_steps(packed, batch_count))
    advance(order, weight_flight)
    mixture_slots, qkv_time, prob_time, first_input = time_forward(order, slots, time_weight, vec)
    mixture_slots = send_back(mixture_slots)
    while weight_flight.result is None:
        advance(order, weight_flight)
    packed = weight_flight.result.reshape(batch_count, -1, features)
    mixture_time, after_time, second_input, qkv_space = middle_forward(
        order, token_rows, mixture_slots, packed, vec
    )
    mixture_space, total_space = space_forward(order, qkv_space, clip, features)
    (
        block_out,
        grad_second,
        grad_branch,
        grad_mixture,
        feed_grads,
        grad_feed_bias,
        feed_sums,
    ) = feed_block(
        order,
        row_count,
        after_time,
        mixture_space,
        grad_result,
        feed_packed,
        feed_bias_row,
        vec,
        chunks=2,
    )

    def sum_batch(block):
        return lax.psum_scatter(block, "batch", scatter_dimension=0, tiled=True)

    feed_part = sum_batch(feed_grads.reshape(-1, features))
    grad_query, grad_keys, grad_values = space_backward(
        order, qkv_space, mixture_space, total_space, grad_mixture, clip, features
    )
    space_pair = space_weights(
        order,
        sizes,
        second_input,
        grad_query,
        grad_keys,
        grad_values,
        mixture_space,
        grad_branch,
    )
    grad_first, space_sums, other_pair, grad_slots = middle_backward(
        order,
        sizes,
        grad_query,
        grad_keys,
        grad_values,
        after_time,
        grad_second,
        packed,
        vec,
        mixture_time,
        feed_sums,
        grad_feed_bias,
    )
    grad_slots = send_parts(grad_slots)
    core_flight = Flight(core_steps([space_pair, other_pair], batch_count))
    advance(order, core_flight)
    space_part = sum_chips(core_flight.result[0], batch_count)
    feed_flight = Flight(frame_steps(feed_part, frame_count, frame_flag))
    advance(order, feed_flight, after=grad_slots[1:])
    input_slots, time_kept, time_sent = time_backward(
        order,
        grad_slots,
        slots,
        qkv_time,
        prob_time,
        first_input,
        time_weight,
        vec,
        space_sums,
    )
    time_flight = Flight(sum_steps(time_kept, time_sent, sizes, frame_flag))
    input_slots = send_back(input_slots)
    space_flight = Flight(frame_steps(space_part, frame_count, frame_flag))
    advance(order, feed_flight, space_flight)
    whole = finish_together(order, space_flight, feed_flight)
    whole = lax.all_gather(whole, ("batch", "frame"), axis=0)
    while time_flight.result is None:
        advance(order, time_flight)
    space_part_rows = space_part.shape[0] // frame_count
    (
        grad_feed_inner,
        grad_feed_outer,
        grad_space_project,
        grad_space_output,
        grad_time_output,
    ) = deliver_parts(order, whole, space_part_rows)
    grad_time_project, time_vectors = deliver_halves(order, *time_flight.result)
    some_vectors = whole[5 * features // space_part_rows, :ROW_TILE].astype(jnp.float32)
    grad_tokens = add_slots(order, grad_first, input_slots, row_count)
    grad_tokens = grad_tokens.reshape(1, row_count, features)
    return (
        block_out,
        grad_tokens,
        grad_time_project,
        grad_time_output,
        time_vectors[0:5],
        grad_space_project,
        grad_space_output,
        some_vectors[0:5],
        grad_feed_inner,
        some_vectors[8:12].reshape(-1),
        grad_feed_outer,
        some_vectors[5:8],
    )


def solution(mesh):
    placed = (
        P("frame", "batch", None),
        P("batch"),
        P("frame", "batch", None),
        P("batch", None),
        P("batch", None),
        P(None, "batch"),
        P("batch", None),
        P("batch", None),
        P(None, "batch"),
        P("batch", None),
        P("batch"),
        P("batch", None),
        P(None, "batch"),
    )
    return jax.shard_map(
        body,
        mesh=mesh,
        in_specs=placed,
        out_specs=(
            P("frame", "batch", None),
            P("frame", "batch", None),
            P(),
            P(),
            P(),
            P(),
            P(),
            P(),
            P(),
            P(),
            P(),
            P(),
        ),
        check_vma=False,
    )
```

```python
import functools
import math

import jax
import jax.numpy as jnp
from jax import lax
from jax.experimental import pallas as pl
from jax.experimental.pallas import tpu as pltpu
from jax.sharding import PartitionSpec as P

HEADS = 12
UNITS = 4
PATCHES = 784
LOG2E = 1.4426950408889634
ROW_TILE = 16
FEED_BLOCKS = 8
LIMIT = 56
ROOM = 64


def round_up(count, step):
    return -(-count // step) * step


def struct(shape, dtype):
    return jax.ShapeDtypeStruct(shape, dtype)


def block_bytes(array, spec):
    shape = spec.block_shape or array.shape
    return math.prod(shape) * jnp.dtype(array.dtype).itemsize


VMEM = pl.BlockSpec(memory_space=pltpu.VMEM)
SMEM = pl.BlockSpec(memory_space=pltpu.SMEM)


class Order:
    def __init__(self, flags):
        self.flags = flags
        self.token = None

    def run(
        self,
        kernel,
        operands,
        in_specs,
        out_specs,
        out_shape,
        grid=(),
        scratch=(),
        prefetch=0,
        after=(),
        room=ROOM,
    ):
        token = [*after] if self.token is None else [self.token, *after]
        inputs, outputs, ordered = len(operands), len(out_shape), len(token)

        def body(*refs):
            refs = refs[:prefetch] + refs[prefetch + ordered :]
            token_ref = refs[inputs + outputs]
            token_ref[...] = jnp.zeros(token_ref.shape, token_ref.dtype)
            kernel(*refs[: inputs + outputs], *refs[inputs + outputs + 1 :])

        pairs = [*zip(operands[prefetch:], in_specs), *zip(out_shape, out_specs)]
        limit = sum(block_bytes(*pair) for pair in pairs) * (2 if math.prod(grid) > 1 else 1)
        limit += sum(math.prod(item.shape) * item.dtype.itemsize for item in scratch)
        limit = min(limit + (room << 20), LIMIT << 20)
        token_spec = pl.BlockSpec((8, 128), lambda *index: (0, 0))
        results = pl.pallas_call(
            body,
            grid_spec=pltpu.PrefetchScalarGridSpec(
                num_scalar_prefetch=prefetch,
                grid=grid,
                in_specs=[pl.BlockSpec(memory_space=pl.ANY)] * ordered + list(in_specs),
                out_specs=list(out_specs) + [token_spec],
                scratch_shapes=list(scratch),
            ),
            out_shape=list(out_shape) + [struct((8, 128), jnp.float32)],
            compiler_params=pltpu.CompilerParams(vmem_limit_bytes=limit),
        )(*operands[:prefetch], *token, *operands[prefetch:])
        self.token = results[-1]
        return results[:-1]


def shift_frames(block, frame_count, shift):
    if shift % frame_count == 0:
        return block
    pairs = [(index, (index + shift) % frame_count) for index in range(frame_count)]
    return lax.ppermute(block, "frame", pairs)


def rows_to_frames(rows, frame_count, frame_index):
    part = rows.shape[0] // frame_count
    slots = []
    for shift in range(frame_count):
        owner = (frame_index + shift) % frame_count
        block = lax.dynamic_slice_in_dim(rows, owner * part, part, 0)
        slots.append(shift_frames(block, frame_count, shift))
    return slots


def send_back(slots):
    return [shift_frames(slot, len(slots), -shift) for shift, slot in enumerate(slots)]


def swap_bit(block, axis, size, bit):
    pairs = [(index, index ^ (1 << bit)) for index in range(size)]
    return lax.ppermute(block, axis, pairs)


def shuffle_kernel(plan, source_count, flags_ref, *refs):
    sources, outputs = refs[:source_count], refs[source_count:]

    def emit(output, at, rows, terms):
        steps = [step for step in range(ROW_TILE, 65, ROW_TILE) if rows % step == 0]
        step = max(steps, default=rows)

        def some(index, carry):
            def load(term):
                source, start = term
                if steps:
                    return sources[source][pl.ds(pl.multiple_of(start + index * step, ROW_TILE), step)]
                return sources[source][start : start + step]

            value = load(terms[0])
            if len(terms) > 1:
                total = value.astype(jnp.float32)
                for term in terms[1:]:
                    total = total + load(term).astype(jnp.float32)
                value = total.astype(output.dtype)
            if steps:
                output[pl.ds(pl.multiple_of(at + index * step, ROW_TILE), step)] = value
            else:
                output[at : at + step] = value
            return carry

        if rows // step == 1:
            some(0, 0)
        else:
            lax.fori_loop(0, rows // step, some, 0)

    for output, segments in zip(outputs, plan):
        at = 0
        for rows, flag, *choices in segments:
            for value, terms in enumerate(choices):

                @pl.when(flags_ref[flag] == value)
                def _():
                    emit(output, at, rows, terms)

            at += rows


def shuffle(order, requests, after, room):
    sources, plan, counts = [], [], []
    for own_sources, own_plan in requests:
        base = len(sources)

        def lift(terms):
            return tuple((source + base, start) for source, start in terms)

        plan += [
            [(rows, flag, *map(lift, choices)) for rows, flag, *choices in out] for out in own_plan
        ]
        sources += own_sources
        counts.append(len(own_plan))
    features = sources[0].shape[1]
    shapes = [struct((sum(segment[0] for segment in out), features), jnp.bfloat16) for out in plan]
    results = order.run(
        functools.partial(shuffle_kernel, plan, len(sources)),
        [order.flags, *sources],
        [SMEM] + [VMEM] * len(sources),
        [VMEM] * len(plan),
        shapes,
        after=after,
        room=room,
    )
    outputs = []
    for count in counts:
        outputs.append(results[:count])
        results = results[count:]
    return outputs


def split_plan(rows, flag, left, right):
    half = rows // 2
    low = ((left[0], left[1]), (right[0], right[1]))
    high = ((left[0], left[1] + half), (right[0], right[1] + half))
    return [[(half, flag, high, low)], [(half, flag, low, high)]]


def join_plan(rows, flag, own, arrived):
    return [(rows, flag, (own,), (arrived,)), (rows, flag, (arrived,), (own,))]


def frame_parts(rows, frame_count, flag, terms_at):
    part = rows // frame_count
    return [
        [
            (part, flag)
            + tuple(terms_at((frame + shift) % frame_count * part) for frame in range(frame_count))
        ]
        for shift in range(frame_count)
    ]


def send_parts(parts):
    return [shift_frames(part, len(parts), shift) for shift, part in enumerate(parts)]


def add_parts(rows, flag, frame_count):
    terms = tuple((source, 0) for source in range(frame_count))
    return [[(rows // frame_count, flag, *[terms] * frame_count)]]


def frame_steps(block, frame_count, flag):
    (block,) = yield [block]
    rows = block.shape[0]
    parts = yield [block], frame_parts(rows, frame_count, flag, lambda at: ((0, at),))
    parts = yield send_parts(parts)
    return list(parts), add_parts(rows, flag, frame_count)


def core_steps(pairs, batch_size):
    moved = yield [swap_bit(sent, "batch", batch_size, 0) for _, sent in pairs]
    sources, segments = [], []
    for (kept, _), arrived in zip(pairs, moved):
        terms = ((len(sources), 0), (len(sources) + 1, 0))
        segments.append((kept.shape[0], 0, terms, terms))
        sources += [kept, arrived]
    return sources, [segments]


def sum_chips(block, batch_size):
    groups = [list(range(core, batch_size, 2)) for core in range(2)]
    return lax.psum_scatter(
        block, "batch", scatter_dimension=0, axis_index_groups=groups, tiled=True
    )


def sum_steps(kept, sent, sizes, flag):
    wide = list(range(1, sizes[0].bit_length() - 1))
    ways = (wide, wide[::-1])
    frame_count = sizes[1]

    def over_batch(block, bit):
        return swap_bit(block, "batch", sizes[0], bit)

    (arrived,) = yield [over_batch(sent, 0)]
    rows = kept.shape[0] // 2
    sources = [kept, arrived]
    pairs = [((0, 0), (1, 0)), ((0, rows), (1, rows))]
    for level in range(len(wide)):
        plan = []
        for (left, right), way in zip(pairs, ways):
            plan += split_plan(rows, way[level], left, right)
        first_out, first_kept, second_out, second_kept = yield sources, plan
        moved = yield [over_batch(first_out, ways[0][level]), over_batch(second_out, ways[1][level])]
        sources = [first_kept, moved[0], second_kept, moved[1]]
        pairs = [((0, 0), (1, 0)), ((2, 0), (3, 0))]
        rows //= 2

    def terms_at(start):
        (left, right), at = pairs[start // rows], start % rows
        return (left[0], left[1] + at), (right[0], right[1] + at)

    parts = yield sources, frame_parts(2 * rows, frame_count, flag, terms_at)
    parts = yield send_parts(parts)
    (part,) = yield parts, add_parts(2 * rows, flag, frame_count)
    parts = yield [shift_frames(part, frame_count, shift) for shift in range(frame_count)]
    size = 2 * rows // frame_count
    segments = [
        (size, flag) + tuple((((frame - owner) % frame_count, 0),) for frame in range(frame_count))
        for owner in range(frame_count)
    ]
    blocks = yield parts, [segments[: frame_count // 2], segments[frame_count // 2 :]]
    for level in range(len(wide))[::-1]:
        moved = yield [over_batch(block, way[level]) for block, way in zip(blocks, ways)]
        sources = [blocks[0], moved[0], blocks[1], moved[1]]
        plan = [join_plan(rows, ways[0][level], (0, 0), (1, 0))]
        plan += [join_plan(rows, ways[1][level], (2, 0), (3, 0))]
        if level == 0:
            plan = [plan[0] + plan[1]]
        blocks = yield sources, plan
        rows *= 2
    (arrived,) = yield [over_batch(blocks[0], 0)]
    return blocks[0], arrived


def gather_steps(shard, batch_size):
    wide = list(range(1, batch_size.bit_length() - 1))
    ways = (wide, wide[::-1])
    half = shard.shape[0] // 2

    def over_batch(block, bit):
        return swap_bit(block, "batch", batch_size, bit)

    blocks = [shard[:half], shard[half:]]
    done = [[], []]
    for level in range(len(wide)):
        moved = yield [over_batch(block, way[level]) for block, way in zip(blocks, ways)]
        plan = []
        for index, way in enumerate(ways):
            bit, before = way[level], done[index]
            done[index] = sorted([*before, bit])
            segments = []
            for place in range(2 ** len(done[index])):
                value = {one: (place >> at) & 1 for at, one in enumerate(done[index])}
                row = half * sum(value[one] << at for at, one in enumerate(before))
                own, other = ((2 * index, row),), ((2 * index + 1, row),)
                segments.append((half, bit, *((other, own) if value[bit] else (own, other))))
            plan.append(segments)
        if level == len(wide) - 1:
            plan = [plan[0] + plan[1]]
        blocks = yield [blocks[0], moved[0], blocks[1], moved[1]], plan
    (block,) = blocks
    (arrived,) = yield [over_batch(block, 0)]
    segments = []
    for place in range(batch_size):
        for index in range(2):
            row = (index * batch_size // 2 + (place >> 1)) * half
            own, other = ((0, row),), ((1, row),)
            segments.append((half, 0, *((other, own) if place & 1 else (own, other))))
    (whole,) = yield [block, arrived], [segments]
    return whole


class Flight:
    def __init__(self, steps):
        self.steps, self.result = steps, None
        self.moved = next(steps)

    def send(self, value):
        try:
            return self.steps.send(value)
        except StopIteration as stop:
            self.result = stop.value
            return None


def advance(order, *flights, after=(), room=ROOM):
    active, requests = [], []
    for flight in flights:
        if flight.result is not None:
            continue
        request = flight.send(flight.moved)
        if request is None and isinstance(flight.result[0], list):
            request = flight.result
        if request is not None:
            active.append(flight)
            requests.append(request)
    if requests:
        for flight, outputs in zip(active, shuffle(order, requests, after, room)):
            if flight.result is None:
                flight.moved = flight.send(outputs)
            else:
                flight.result = outputs


def finish_together(order, *flights):
    sources, segments = [], []
    for flight in flights:
        if flight.result is None:
            flight.send(flight.moved)
            parts, ((segment,),) = flight.result
        else:
            parts = flight.result
            segment = (parts[0].shape[0], 0, ((0, 0),), ((0, 0),))
        rows, flag, *choices = segment
        base = len(sources)
        segments.append(
            (rows, flag, *[tuple((source + base, at) for source, at in terms) for terms in choices])
        )
        sources += parts
    ((whole,),) = shuffle(order, [(sources, [segments])], (), 4)
    return whole


def deliver_kernel(flags_ref, own_ref, arrived_ref, out_ref, rest_ref):
    half, features = own_ref.shape
    columns = out_ref.shape[1] // features
    for core in range(2):

        @pl.when(flags_ref[0] == core)
        def _():
            for index in range(columns + 1):
                first = index * features
                height = features if index < columns else rest_ref.shape[0]
                while height:
                    owner, at = divmod(first, half)
                    size = min(height, half - at)
                    piece = (own_ref if owner == core else arrived_ref)[at : at + size]
                    piece = piece.astype(jnp.float32)
                    row = first % features
                    if index < columns:
                        span = slice(index * features, (index + 1) * features)
                        out_ref[row : row + size, span] = piece
                    else:
                        rest_ref[row : row + size] = piece
                    first, height = first + size, height - size


def deliver_halves(order, own, arrived):
    half, features = own.shape
    columns = 2 * half // features
    return order.run(
        deliver_kernel,
        [order.flags, own, arrived],
        [SMEM, VMEM, VMEM],
        [VMEM, VMEM],
        [struct((features, columns * features), jnp.float32), struct((8, features), jnp.float32)],
    )


def deliver_parts_kernel(outputs, counts, *refs):
    step = pl.program_id(0)
    feed_refs, space_refs = refs[: counts[0]], refs[counts[0] : sum(counts)]
    for number, (output, (first, last, _)) in enumerate(zip(refs[sum(counts) :], outputs)):
        sources = feed_refs if number < 2 else space_refs

        @pl.when((step >= first) & (step < last))
        def _():
            rows = sources[0].shape[1]
            for piece in range(sources[0].shape[0]):
                for index, source in enumerate(sources):
                    at = (piece * len(sources) + index) * rows
                    output[at : at + rows] = source[piece].astype(output.dtype)


def deliver_parts(order, gathered, space_part):
    _, part, features = gathered.shape
    feed_part = part - space_part
    unit = math.gcd(space_part, feed_part)

    def source(rows, first, step_of, index):
        def place(step):
            return step_of(step), first // unit + index, 0

        return pl.BlockSpec((features // rows, unit, features), place)

    counts = (feed_part // unit, space_part // unit)
    feed_specs = [
        source(feed_part, space_part, lambda step: jnp.minimum(step, FEED_BLOCKS - 1), index)
        for index in range(counts[0])
    ]
    space_specs_ = [
        source(space_part, 0, lambda step: jnp.minimum(step, 4), index)
        for index in range(counts[1])
    ]
    half = FEED_BLOCKS // 2
    outputs = [(0, half, True), (half, FEED_BLOCKS, False)]
    for first, last, wide in ((0, 3, True), (3, 4, False), (4, 5, False)):
        outputs.append((first, last, wide))

    def spot(first, last, wide):
        def index(step):
            at = jnp.clip(step - first, 0, last - first - 1)
            return (0, at) if wide else (at, 0)

        return pl.BlockSpec((features, features), index)

    def shape(first, last, wide):
        rows = (last - first) * features
        return struct((features, rows) if wide else (rows, features), jnp.float32)

    return order.run(
        functools.partial(deliver_parts_kernel, outputs, counts),
        [gathered] * sum(counts),
        feed_specs + space_specs_,
        [spot(*item) for item in outputs],
        [shape(*item) for item in outputs],
        grid=(FEED_BLOCKS,),
    )


def contract(x,y,dims):
    return lax.dot_general(x,y,((dims[0:1],dims[1:2]),((),())),preferred_element_type=jnp.float32)

def widen_rows(values, wide):
    rows, width = values.shape
    if wide == rows:
        return values
    return jnp.concatenate([values, jnp.zeros((wide - rows, width), values.dtype)])


def head_halves(width):
    lane = lax.broadcasted_iota(jnp.int32, (1, width), 1)
    return [lane < width // 2, lane >= width // 2]

def space_forward_kernel(
    scale, mark_q_ref, mark_k_ref, q_ref, k_ref, v_ref, mixture_ref, total_ref, k_wide, v_wide
):
    rows, width = q_ref.shape
    wide = k_wide.shape[0]
    if wide > rows:

        @pl.when(pl.program_id(0) == 0)
        def _():
            k_wide[rows:] = jnp.zeros((wide - rows, width), k_wide.dtype)
            v_wide[rows:] = jnp.zeros((wide - rows, width), v_wide.dtype)

    k_wide[:rows] = k_ref[...]
    v_wide[:rows] = v_ref[...]
    halves = head_halves(width)
    one = jnp.ones((), q_ref.dtype)
    outs, tops = [], []
    for half in halves:
        queries = jnp.where(half, q_ref[...], mark_q_ref[:rows])
        keys = jnp.where(half, k_wide[...], mark_k_ref[...])
        scores = contract(queries, keys, (1, 1)) * (scale * LOG2E)
        top = jnp.max(scores, axis=1, keepdims=True)
        weights = jnp.exp2(scores - top)
        values = jnp.where(half, v_wide[...], one)
        outs.append(contract(weights.astype(jnp.bfloat16), values, (1, 0)))
        tops.append(top)
    mass = pltpu.roll(jnp.where(halves[0], outs[1], outs[0]), width // 2, 1)
    mixture = jnp.where(halves[0], outs[0], outs[1]) / mass
    mixture_ref[...] = mixture.astype(mixture_ref.dtype)
    total_ref[...] = jnp.where(halves[0], tops[0], tops[1]) + jnp.log2(mass)


def space_specs(rows, features):
    pairs = HEADS // 2
    width = features // pairs
    wide = round_up(rows, 128)
    fixed = [pl.BlockSpec((wide, width), lambda i: (0, 0))] * 2
    blocks = [pl.BlockSpec((rows, width), lambda i, o=o: (0, o + i)) for o in (0, pairs, 2 * pairs)]
    out = pl.BlockSpec((rows, width), lambda i: (0, i))
    scratch = [pltpu.VMEM((wide, width), jnp.bfloat16)] * 2
    return pairs, (features // HEADS) ** -0.5, fixed + blocks, out, scratch


def clip_marks(clip, width):
    rows = clip.shape[0]
    clip = jnp.pad(clip, (0, round_up(rows, 128) - rows), constant_values=-2)
    same = (clip[:, None] + 2) == jnp.arange(width, dtype=jnp.int32)[None] % (width // 2)
    return same.astype(jnp.bfloat16), jnp.where(same, 0.0, -1e30).astype(jnp.bfloat16)


def space_forward(order, qkv, clip, features):
    rows = qkv.shape[0]
    pairs, scale, specs, out, scratch = space_specs(rows, features)
    return order.run(
        functools.partial(space_forward_kernel, scale),
        [*clip_marks(clip, features // pairs), qkv, qkv, qkv],
        specs,
        [out, out],
        [struct((rows, features), jnp.bfloat16), struct((rows, features), jnp.float32)],
        grid=(pairs,),
        scratch=scratch,
    )


def space_backward_kernel(
    scale, mark_q_ref, mark_k_ref, q_ref, k_ref, v_ref, mixture_ref, total_ref, grad_ref, dq_ref, dk_ref, dv_ref,
    q_wide, g_wide
):
    rows, width = q_ref.shape
    wide = q_wide.shape[0]
    if wide > rows:

        @pl.when(pl.program_id(0) == 0)
        def _():
            q_wide[rows:] = jnp.zeros((wide - rows, width), q_wide.dtype)
            g_wide[rows:] = jnp.zeros((wide - rows, width), g_wide.dtype)

    q_wide[:rows] = q_ref[...]
    g_wide[:rows] = grad_ref[...]
    halves = head_halves(width)
    zero = jnp.zeros((), q_ref.dtype)
    product = grad_ref[...].astype(jnp.float32) * mixture_ref[...].astype(jnp.float32)
    sums = [jnp.sum(jnp.where(half, product, 0.0), axis=1, keepdims=True) for half in halves]
    delta = widen_rows(jnp.where(halves[0], sums[0], sums[1]), wide).T
    total = widen_rows(total_ref[...], wide).T
    parts = [[], [], [], [], []]
    for index, half in enumerate(halves):
        at = index * (width // 2)
        queries = jnp.where(half, q_wide[...], mark_q_ref[...])
        keys = jnp.where(half, k_ref[...], mark_k_ref[:rows])
        values = jnp.where(half, v_ref[...], zero)
        scores = contract(keys, queries, (1, 1)) * (scale * LOG2E)
        weights = jnp.exp2(scores - total[at : at + 1])
        slopes = contract(values, g_wide[...], (1, 1))
        slopes = (weights * (slopes - delta[at : at + 1])).astype(jnp.bfloat16)
        own = (
            weights.astype(jnp.bfloat16),
            slopes,
            jnp.where(half, g_wide[...], zero),
            jnp.where(half, q_wide[...], zero),
            jnp.where(half, k_ref[...], zero),
        )
        for part, value in zip(parts, own):
            part.append(value)
    weights, slopes, grads, queries, keys = parts
    grads, queries, keys = (jnp.concatenate(part, axis=0) for part in (grads, queries, keys))
    dv_ref[...] = contract(jnp.concatenate(weights, axis=1), grads, (1, 0)).astype(dv_ref.dtype)
    dk = contract(jnp.concatenate(slopes, axis=1), queries, (1, 0))
    dk_ref[...] = (dk * scale).astype(dk_ref.dtype)
    dq = contract(jnp.concatenate(slopes, axis=0), keys, (0, 0))
    dq_ref[...] = (dq[:rows] * scale).astype(dq_ref.dtype)


def space_backward(order, qkv, mixture, total, grad, clip, features):
    rows = qkv.shape[0]
    pairs, scale, specs, out, scratch = space_specs(rows, features)
    return order.run(
        functools.partial(space_backward_kernel, scale),
        [*clip_marks(clip, features // pairs), qkv, qkv, qkv, mixture, total, grad],
        specs + [out] * 3,
        [out] * 3,
        [struct((rows, features), jnp.bfloat16)] * 3,
        grid=(pairs,),
        scratch=scratch,
    )


def norm_parts(values):
    average = jnp.mean(values, axis=1, keepdims=True)
    centered = values - average
    spread = lax.rsqrt(jnp.mean(centered * centered, axis=1, keepdims=True) + 1e-06)
    return centered * spread, spread
def norm_back(grad, normed, spread, gain):
    scaled = grad * gain
    return spread * (scaled - jnp.mean(scaled, axis=1, keepdims=True) - normed * jnp.mean(scaled * normed, axis=1, keepdims=True))
def column_sum(values):
    return jnp.sum(values, axis=0, keepdims=True)

def square_spec(packed, index):
    batch_count, _, features = packed.shape
    return pl.BlockSpec((batch_count, features // batch_count, features), lambda i: (0, index, 0))


def square(ref):
    return ref[...].reshape(-1, ref.shape[-1])


def feed_kernel(chunks, x1_ref, mixture_ref, dz_ref, so_ref, fi_ref, fo_ref, fb_ref, vec_ref,
                out_ref, dx2_ref, dys_ref, dos_ref, grad_ref, gfb_ref, gvec_ref,
                x2_s, a3_s, a3t_s, acc_s, da_s, g_s, dh_s):
    step = pl.program_id(0)
    rows = x1_ref.shape[0]
    @pl.when(step == 0)
    def _():
        x2 = x1_ref[...] + contract(mixture_ref[...], square(so_ref), (1, 0)) + vec_ref[9:10]
        x2_s[...] = x2
        normed, _ = norm_parts(x2)
        a3 = (normed * vec_ref[10:11] + vec_ref[11:12]).astype(jnp.bfloat16)
        a3_s[...] = a3
        a3t_s[...] = a3.T
        acc_s[...] = x2 + vec_ref[12:13]
        da_s[...] = jnp.zeros_like(da_s)
    inner, outer = square(fi_ref), square(fo_ref)
    part = rows // chunks
    for chunk in range(chunks):
        span = slice(chunk * part, (chunk + 1) * part)
        hidden = contract(a3_s[span], inner, (1, 0)) + fb_ref[...]
        cdf = 0.5 + 0.5 * lax.erf(hidden * math.sqrt(0.5))
        slope = cdf + hidden * jnp.exp(hidden * hidden * -0.5) * (1.0 / math.sqrt(2.0 * math.pi))
        active = (hidden * cdf).astype(jnp.bfloat16)
        g_s[span] = active
        dh = (contract(dz_ref[span], outer, (1, 1)) * slope).astype(jnp.bfloat16)
        dh_s[span] = dh
        acc_s[span] += contract(active, outer, (1, 0))
        da_s[span] += contract(dh, inner, (1, 1))
    grad_ref[0] = contract(a3t_s[...], dh_s[...], (1, 0)).astype(grad_ref.dtype)
    grad_ref[1] = contract(g_s[...], dz_ref[...], (0, 0)).astype(grad_ref.dtype)
    gfb_ref[...] = column_sum(dh_s[...].astype(jnp.float32))
    @pl.when(step == pl.num_programs(0) - 1)
    def _():
        out_ref[0] = acc_s[: out_ref.shape[1]].astype(out_ref.dtype)
        normed, spread = norm_parts(x2_s[...])
        grad = da_s[...]
        dz = dz_ref[...].astype(jnp.float32)
        dx2 = dz + norm_back(grad, normed, spread, vec_ref[10:11])
        dx2_ref[...] = dx2
        dys = dx2.astype(jnp.bfloat16)
        dys_ref[...] = dys
        dos_ref[...] = contract(dys, square(so_ref), (1, 1)).astype(dos_ref.dtype)
        gvec_ref[0:1] = column_sum(grad * normed)
        gvec_ref[1:2] = column_sum(grad)
        gvec_ref[2:3] = column_sum(dz)
        gvec_ref[3:4] = column_sum(dys.astype(jnp.float32))
        gvec_ref[4:8] = jnp.zeros((4, gvec_ref.shape[1]), jnp.float32)

def feed_block(order, row_count, x1, mixture, dz, feed_packed, bias, vec, chunks):
    rows, features = x1.shape
    batch_count = feed_packed.shape[0]
    hidden = bias.shape[1]
    whole = pl.BlockSpec((rows, features), lambda j: (0, 0))
    line = pl.BlockSpec((1, features), lambda j: (0, j))
    shard = hidden // batch_count
    low, full = jnp.bfloat16, jnp.float32
    return order.run(
        functools.partial(feed_kernel, chunks),
        [x1, mixture, dz, feed_packed, feed_packed, feed_packed, bias, vec],
        [
            whole,
            whole,
            whole,
            square_spec(feed_packed, 2 * hidden // features),
            pl.BlockSpec((batch_count, features // batch_count, features), lambda j: (0, j, 0)),
            pl.BlockSpec((features // shard, shard, features), lambda j: (j, 1, 0)),
            line,
            pl.BlockSpec(vec.shape, lambda j: (0, 0)),
        ],
        [
            pl.BlockSpec((1, row_count, features), lambda j: (0, 0, 0)),
            whole,
            whole,
            whole,
            pl.BlockSpec((2, features, features), lambda j: (0, j, 0)),
            line,
            pl.BlockSpec((8, features), lambda j: (0, 0)),
        ],
        [
            struct((1, row_count, features), low),
            struct((rows, features), full),
            struct((rows, features), low),
            struct((rows, features), low),
            struct((2, hidden, features), low),
            struct((1, hidden), full),
            struct((8, features), full),
        ],
        grid=(hidden // features,),
        scratch=[
            pltpu.VMEM((rows, features), full),
            pltpu.VMEM((rows, features), low),
            pltpu.VMEM((features, rows), low),
            pltpu.VMEM((rows, features), full),
            pltpu.VMEM((rows, features), full),
            pltpu.VMEM((rows, features), low),
            pltpu.VMEM((rows, features), low),
        ],
    )


def gather_rows(count, frame, slots, rows_s):
    part = slots[0].shape[0]
    for shift in range(count):
        owner = lax.rem(frame + shift, count)
        rows_s[pl.ds(pl.multiple_of(owner * part, ROW_TILE), part)] = slots[shift][...]


def middle_kernel(count, frame_flag, flags_ref, token_ref, *refs):
    slots, (to_ref, *sp_refs, vec_ref) = refs[:count], refs[count : count + 5]
    mixture_ref, x1_ref, a2_ref, qkv_ref = refs[count + 5 :]
    rows, features = token_ref.shape
    gather_rows(count, flags_ref[frame_flag], slots, mixture_ref)
    number = lax.broadcasted_iota(jnp.int32, (rows, 1), 0)
    branch = contract(mixture_ref[...], square(to_ref), (1, 0)) + vec_ref[4:5]
    x1 = token_ref[...].astype(jnp.float32) + jnp.where(number < PATCHES, branch, 0.0)
    x1_ref[...] = x1
    normed, _ = norm_parts(x1)
    a2 = (normed * vec_ref[5:6] + vec_ref[6:7]).astype(jnp.bfloat16)
    a2_ref[...] = a2
    for third in range(3):
        span = slice(third * features, (third + 1) * features)
        joined = contract(a2, square(sp_refs[third]), (1, 0))
        if third != 1:
            joined = joined + vec_ref[7 + third // 2 : 8 + third // 2]
        qkv_ref[:, span] = joined.astype(jnp.bfloat16)


def project_specs(packed, vec):
    return [square_spec(packed, index) for index in range(4)] + [
        pl.BlockSpec(vec.shape, lambda i: (0, 0))
    ]


def middle_forward(order, tokens, slots, packed, vec):
    rows, features = tokens.shape
    low = jnp.bfloat16
    return order.run(
        functools.partial(middle_kernel, len(slots), order.flags.shape[0] - 1),
        [order.flags, tokens, *slots, *[packed] * 4, vec],
        [SMEM] + [VMEM] * (len(slots) + 1) + project_specs(packed, vec),
        [VMEM] * 4,
        [
            struct((rows, features), low),
            struct((rows, features), jnp.float32),
            struct((rows, features), low),
            struct((rows, 3 * features), low),
        ],
        grid=(1,),
    )


def middle_back_kernel(
    sizes, part, flags_ref, dq_ref, dk_ref, dv_ref, x1_ref, dx2_ref, to_ref, *refs
):
    *sp_refs, vec_ref, time_ref, feed_ref, bias_ref = refs[:7]
    dx1_ref, sums_ref, kept_ref, sent_ref = refs[7:11]
    count = sizes[1]
    slots, rows_s = refs[11 : 11 + count], refs[11 + count]
    rows, features = x1_ref.shape
    grad = 0.0
    for third, piece in enumerate((dq_ref, dk_ref, dv_ref)):
        grad = grad + contract(piece[...], square(sp_refs[third]), (1, 1))
    normed, spread = norm_parts(x1_ref[...])
    dx1 = dx2_ref[...] + norm_back(grad, normed, spread, vec_ref[5:6])
    dx1_ref[...] = dx1
    number = lax.broadcasted_iota(jnp.int32, (rows, 1), 0)
    dyt = jnp.where(number < PATCHES, dx1, 0.0).astype(jnp.bfloat16)
    rows_s[...] = contract(dyt, square(to_ref), (1, 1)).astype(rows_s.dtype)
    block = rows // count
    for shift in range(count):
        owner = lax.rem(flags_ref[flags_ref.shape[0] - 1] + shift, count)
        slots[shift][...] = rows_s[pl.ds(pl.multiple_of(owner * block, ROW_TILE), block)]
    sums_ref[0:1] = column_sum(grad * normed)
    sums_ref[1:2] = column_sum(grad)
    sums_ref[2:3] = column_sum(dq_ref[...].astype(jnp.float32))
    sums_ref[3:4] = column_sum(dv_ref[...].astype(jnp.float32))
    sums_ref[4:5] = column_sum(dyt.astype(jnp.float32))
    sums_ref[5:8] = jnp.zeros((3, features), jnp.float32)
    first = 4 * features
    put = functools.partial(put_parts, flags_ref, kept_ref, sent_ref, sizes, part, first)
    put(first, contract(time_ref[...], dyt, (0, 0)))
    bias = bias_ref[...]
    lines = [bias[:, at : at + features] for at in range(0, bias.shape[1], features)]
    pieces = [sums_ref[0:4], feed_ref[3:4], feed_ref[0:3], *lines]
    put(first + features, fill_rows(pieces, 2 * kept_ref.shape[0] - features, features))


def middle_backward(order, sizes, dq, dk, dv, x1, dx2, packed, vec, mixture, feed_sums, bias):
    rows, features = x1.shape
    count = sizes[1]
    low, full = jnp.bfloat16, jnp.float32
    total, part = space_rows(sizes, features)
    half = struct(((total - 4 * features) // 2, features), low)
    results = order.run(
        functools.partial(middle_back_kernel, sizes, part),
        [order.flags, dq, dk, dv, x1, dx2, *[packed] * 4, vec, mixture, feed_sums, bias],
        [SMEM] + [VMEM] * 5 + project_specs(packed, vec) + [VMEM] * 3,
        [VMEM] * (4 + count),
        [struct((rows, features), full), struct((8, features), full), half, half]
        + [struct((rows // count, features), low)] * count,
        grid=(1,),
        scratch=[pltpu.VMEM((rows, features), low)],
        room=14,
    )
    return results[0], results[1], results[2:4], results[4:]


def put_half(core_ref, kept_ref, sent_ref, at, value):
    half = kept_ref.shape[0]
    low = value.astype(kept_ref.dtype)
    part = math.gcd(half, low.shape[0])
    for offset in range(0, low.shape[0], part):
        owner, first = divmod(at + offset, half)
        piece = low[offset : offset + part]

        @pl.when(core_ref[0] == owner)
        def _():
            kept_ref[first : first + part] = piece

        @pl.when(core_ref[0] != owner)
        def _():
            sent_ref[first : first + part] = piece


def fill_rows(pieces, rows, features):
    used = sum(piece.shape[0] for piece in pieces)
    return jnp.concatenate([*pieces, jnp.zeros((rows - used, features), jnp.float32)])


def put_parts(core_ref, kept_ref, sent_ref, sizes, part, first, at, value):
    low = value.astype(kept_ref.dtype)
    for offset in range(0, low.shape[0], part):
        batch, frame = divmod((at + offset) // part, sizes[1])
        start = ((batch >> 1) * sizes[1] + frame) * part - first // 2
        piece = low[offset : offset + part]

        @pl.when(core_ref[0] == batch & 1)
        def _():
            kept_ref[start : start + part] = piece

        @pl.when(core_ref[0] != batch & 1)
        def _():
            sent_ref[start : start + part] = piece


def space_rows(sizes, features):
    rows = round_up(5 * features + ROW_TILE, sizes[0] * sizes[1] * ROW_TILE)
    return rows, rows // (sizes[0] * sizes[1])


def space_weights_kernel(
    sizes, part, flags_ref, a2_ref, dq_ref, dk_ref, dv_ref, mixture_ref, dys_ref, kept_ref, sent_ref
):
    features = a2_ref.shape[1]
    put = functools.partial(put_parts, flags_ref, kept_ref, sent_ref, sizes, part, 0)
    turned = a2_ref[...].T
    for third, piece in enumerate((dq_ref, dk_ref, dv_ref)):
        put(third * features, contract(turned, piece[...], (1, 0)))
    put(3 * features, contract(mixture_ref[...], dys_ref[...], (0, 0)))


def space_weights(order, sizes, *operands):
    features = operands[0].shape[1]
    part = space_rows(sizes, features)[1]
    half = struct((2 * features, features), jnp.bfloat16)
    return order.run(
        functools.partial(space_weights_kernel, sizes, part),
        [order.flags, *operands],
        [SMEM] + [VMEM] * len(operands),
        [VMEM] * 2,
        [half, half],
    )


CHUNK = 16
def head_map(features, lanes=128):
    head = jnp.arange(features, dtype=jnp.int32) // (features // HEADS)
    return (head[:, None] == jnp.arange(lanes, dtype=jnp.int32)[None]).astype(jnp.bfloat16)

def pair_sums(left, right, gather_ref, pair_s):
    count = len(left)
    for f in range(count):
        for g in range(count):
            at = (f * count + g) * CHUNK
            pair_s[at:at + CHUNK] = (left[f] * right[g]).astype(jnp.bfloat16)
    return contract(pair_s[...], gather_ref[...], (1, 0))

def time_forward_kernel(count, scale, *refs):
    slots, (tp_ref, vec_ref, gather_ref, spread_ref) = refs[:count], refs[count:count + 4]
    outs, (qkv_ref, prob_ref, a1_ref) = refs[count + 4:2 * count + 4], refs[2 * count + 4:2 * count + 7]
    pair_s, weight_s = refs[2 * count + 7:]
    part, features = slots[0].shape
    for s in range(count):
        normed, _ = norm_parts(slots[s][...].astype(jnp.float32))
        a1_ref[s * part:(s + 1) * part] = (normed * vec_ref[0:1] + vec_ref[1:2]).astype(jnp.bfloat16)
    for third in range(3):
        span = slice(third * features, (third + 1) * features)
        joined = contract(a1_ref[...], tp_ref[:, span], (1, 0))
        if third != 1:
            joined = joined + vec_ref[2 + third // 2:3 + third // 2]
        qkv_ref[:, span] = joined.astype(jnp.bfloat16)

    def chunk_step(index, carry):
        def rows_of(s, third):
            start = pl.multiple_of(s * part + index * CHUNK, CHUNK)
            return qkv_ref[pl.ds(start, CHUNK), third * features:(third + 1) * features].astype(jnp.float32)
        queries, keys, values = ([rows_of(s, third) for s in range(count)] for third in range(3))
        scores = pair_sums(queries, keys, gather_ref, pair_s) * (scale * LOG2E)
        place = pl.ds(pl.multiple_of(index * CHUNK, CHUNK), CHUNK)
        for f in range(count):
            row = [scores[(f * count + g) * CHUNK:(f * count + g + 1) * CHUNK] for g in range(count)]
            top = functools.reduce(jnp.maximum, row)
            raised = [jnp.exp2(item - top) for item in row]
            mass = functools.reduce(jnp.add, raised)
            for g in range(count):
                weight = raised[g] / mass
                prob_ref[f * count + g, place] = weight
                at = (f * count + g) * CHUNK
                weight_s[at:at + CHUNK] = weight.astype(jnp.bfloat16)
        wide = contract(weight_s[...], spread_ref[...], (1, 0))
        for f in range(count):
            total = 0.0
            for g in range(count):
                at = (f * count + g) * CHUNK
                total = total + wide[at:at + CHUNK] * values[g]
            outs[f][place] = total.astype(jnp.bfloat16)
        return carry
    lax.fori_loop(0, part // CHUNK, chunk_step, 0, unroll=True)

def time_forward(order, slots, time_weight, vec):
    count = len(slots)
    part, features = slots[0].shape
    gather = head_map(features)
    low, full = jnp.bfloat16, jnp.float32
    results = order.run(
        functools.partial(time_forward_kernel, count, (features // HEADS) ** -0.5),
        [*slots, time_weight, vec, gather, gather.T],
        [VMEM] * count + [pl.BlockSpec((features, 3 * features), lambda i: (0, 0)), VMEM, VMEM, VMEM],
        [VMEM] * (count + 3),
        [struct((part, features), low)] * count
        + [
            struct((count * part, 3 * features), low),
            struct((count * count, part, 128), full),
            struct((count * part, features), low),
        ],
        grid=(1,),
        scratch=[
            pltpu.VMEM((count * count * CHUNK, features), low),
            pltpu.VMEM((count * count * CHUNK, 128), low),
        ],
    )
    return results[:count], results[count], results[count + 1], results[count + 2]


def time_backward_kernel(count, scale, flags_ref, *refs):
    grads, slots = refs[:count], refs[count : 2 * count]
    qkv_ref, prob_ref, a1_ref, gather_ref, spread_ref, tp_ref, vec_ref, other_ref = refs[2 * count : 2 * count + 8]
    refs = refs[2 * count + 8 :]
    outs, (kept_ref, sent_ref, dqkv_ref, pair_s, weight_s) = refs[:count], refs[count:]
    part, features = grads[0].shape
    def chunk_step(index, carry):
        place = pl.ds(pl.multiple_of(index * CHUNK, CHUNK), CHUNK)
        def rows_of(s, third):
            start = pl.multiple_of(s * part + index * CHUNK, CHUNK)
            return qkv_ref[pl.ds(start, CHUNK), third * features:(third + 1) * features].astype(jnp.float32)
        queries, keys, values = ([rows_of(s, third) for s in range(count)] for third in range(3))
        outer = [grads[s][place].astype(jnp.float32) for s in range(count)]
        slopes = pair_sums(outer, values, gather_ref, pair_s)
        size = count * count * CHUNK
        for f in range(count):
            row = [slopes[(f * count + g) * CHUNK:(f * count + g + 1) * CHUNK] for g in range(count)]
            weights = [prob_ref[f * count + g, place] for g in range(count)]
            delta = functools.reduce(jnp.add, [w * s for w, s in zip(weights, row)])
            for g in range(count):
                at = (f * count + g) * CHUNK
                weight_s[at:at + CHUNK] = weights[g].astype(jnp.bfloat16)
                weight_s[size + at:size + at + CHUNK] = (weights[g] * (row[g] - delta)).astype(jnp.bfloat16)
        wide = contract(weight_s[...], spread_ref[...], (1, 0))
        for s in range(count):
            dq, dk, dv = 0.0, 0.0, 0.0
            for t in range(count):
                forth, back = (s * count + t) * CHUNK, (t * count + s) * CHUNK
                dq = dq + wide[size + forth:size + forth + CHUNK] * keys[t]
                dk = dk + wide[size + back:size + back + CHUNK] * queries[t]
                dv = dv + wide[back:back + CHUNK] * outer[t]
            start = pl.ds(pl.multiple_of(s * part + index * CHUNK, CHUNK), CHUNK)
            for third, value in enumerate((dq * scale, dk * scale, dv)):
                dqkv_ref[start, third * features:(third + 1) * features] = value.astype(jnp.bfloat16)
        return carry
    lax.fori_loop(0, part // CHUNK, chunk_step, 0, unroll=True)
    a1t = a1_ref[...].T
    put = functools.partial(put_half, flags_ref, kept_ref, sent_ref)
    for third in range(3):
        span = slice(third * features, (third + 1) * features)
        put(third * features, contract(a1t, dqkv_ref[:, span], (1, 0)))
    grad = contract(dqkv_ref[...], tp_ref[...], (1, 1))
    gain, shift = 0.0, 0.0
    for s in range(count):
        piece = grad[s * part : (s + 1) * part]
        normed, spread = norm_parts(slots[s][...].astype(jnp.float32))
        outs[s][...] = norm_back(piece, normed, spread, vec_ref[0:1]).astype(jnp.bfloat16)
        gain = gain + column_sum(piece * normed)
        shift = shift + column_sum(piece)
    sums = [
        gain,
        shift,
        column_sum(dqkv_ref[:, :features].astype(jnp.float32)),
        column_sum(dqkv_ref[:, 2 * features :].astype(jnp.float32)),
        other_ref[4:5],
    ]
    put(3 * features, fill_rows(sums, 2 * kept_ref.shape[0] - 3 * features, features))


def time_backward(order, grads, slots, qkv, prob, a1, time_weight, vec, other):
    count = len(grads)
    part, features = grads[0].shape
    gather = head_map(features)
    low = jnp.bfloat16
    half = struct((round_up(3 * features + 16, 512) // 2, features), low)
    results = order.run(
        functools.partial(time_backward_kernel, count, (features // HEADS) ** -0.5),
        [order.flags, *grads, *slots, qkv, prob, a1, gather, gather.T, time_weight, vec, other],
        [SMEM] + [VMEM] * (2 * count + 5)
        + [pl.BlockSpec((features, 3 * features), lambda i: (0, 0)), VMEM, VMEM],
        [VMEM] * (count + 2),
        [struct((part, features), low)] * count + [half, half],
        grid=(1,),
        scratch=[
            pltpu.VMEM(qkv.shape, low),
            pltpu.VMEM((count * count * CHUNK, features), low),
            pltpu.VMEM((2 * count * count * CHUNK, 128), low),
        ],
    )
    return results[:count], results[count], results[count + 1]


def place_kernel(flags_ref, first_ref, *refs):
    slots, out_ref, rows_s = refs[:-2], refs[-2], refs[-1]
    gather_rows(len(slots), flags_ref[flags_ref.shape[0] - 1], slots, rows_s)
    lanes = out_ref.shape[1]
    parts = first_ref.shape[1] // lanes
    rows = out_ref.shape[0] // parts
    for index in range(parts):
        span = slice(index * lanes, (index + 1) * lanes)
        total = first_ref[:rows, span] + rows_s[:rows, span].astype(jnp.float32)
        out_ref[pl.ds(index, rows, stride=parts)] = total


def add_slots(order, first, slots, row_count):
    features = first.shape[1]
    return order.run(
        place_kernel,
        [order.flags, first, *slots],
        [SMEM] + [VMEM] * (len(slots) + 1),
        [VMEM],
        [struct((row_count * features // 128, 128), jnp.float32)],
        scratch=[pltpu.VMEM(first.shape, slots[0].dtype)],
    )[0]


def body(
    tokens,
    size_tag,
    cotangent,
    time_project,
    time_output,
    time_vector,
    space_project,
    space_output,
    space_vector,
    feed_inner,
    feed_bias,
    feed_outer,
    feed_vector,
):
    frame_count = lax.axis_size("frame")
    batch_count = lax.axis_size("batch")
    sizes = (batch_count, frame_count)
    frame_index = lax.axis_index("frame")
    batch_index = lax.axis_index("batch")
    flags = [(batch_index >> bit) & 1 for bit in range(batch_count.bit_length() - 1)]
    frame_flag = len(flags)
    order = Order(jnp.stack([*flags, frame_index]).astype(jnp.int32))
    features = tokens.shape[2]
    row_count = tokens.shape[1]
    part = round_up(-(-PATCHES // frame_count), ROW_TILE)
    padded = part * frame_count

    time_weight = lax.all_gather(time_project, "batch", axis=0, tiled=True)
    token_rows = jnp.pad(tokens[0], ((0, padded - row_count), (0, 0)))
    grad_result = jnp.pad(cotangent[0], ((0, padded - row_count), (0, 0)))
    slots = rows_to_frames(token_rows, frame_count, frame_index)
    vectors = jnp.concatenate(
        [time_vector, space_vector, feed_vector, feed_bias.reshape(-1, time_vector.shape[1])], axis=0
    )
    vectors = lax.all_gather(vectors, "batch", axis=0)
    vec = vectors[:, :13].transpose(1, 0, 2).reshape(13, features).astype(jnp.float32)
    vec = jnp.pad(vec, ((0, 3), (0, 0)))
    feed_bias_row = vectors[:, 13:].reshape(1, -1).astype(jnp.float32)

    def stack_columns(weight):
        return [weight[:, at : at + features] for at in range(0, weight.shape[1], features)]

    feed_packed = jnp.concatenate([*stack_columns(feed_inner), feed_outer, space_output], axis=0)
    feed_packed = lax.all_gather(feed_packed, "batch", axis=0)
    clip = jnp.concatenate(
        [
            jnp.arange(PATCHES, dtype=jnp.int32) // size_tag[0],
            jnp.arange(UNITS, dtype=jnp.int32),
            jnp.full((padded - PATCHES - UNITS,), -1, jnp.int32),
        ]
    )

    packed = jnp.concatenate([time_output, *stack_columns(space_project)], axis=0)
    weight_flight = Flight(gather_steps(packed, batch_count))
    advance(order, weight_flight)
    mixture_slots, qkv_time, prob_time, first_input = time_forward(order, slots, time_weight, vec)
    mixture_slots = send_back(mixture_slots)
    while weight_flight.result is None:
        advance(order, weight_flight)
    packed = weight_flight.result.reshape(batch_count, -1, features)
    mixture_time, after_time, second_input, qkv_space = middle_forward(
        order, token_rows, mixture_slots, packed, vec
    )
    mixture_space, total_space = space_forward(order, qkv_space, clip, features)
    (
        block_out,
        grad_second,
        grad_branch,
        grad_mixture,
        feed_grads,
        grad_feed_bias,
        feed_sums,
    ) = feed_block(
        order,
        row_count,
        after_time,
        mixture_space,
        grad_result,
        feed_packed,
        feed_bias_row,
        vec,
        chunks=2,
    )

    def sum_batch(block):
        return lax.psum_scatter(block, "batch", scatter_dimension=0, tiled=True)

    feed_part = sum_batch(feed_grads.reshape(-1, features))
    grad_query, grad_keys, grad_values = space_backward(
        order, qkv_space, mixture_space, total_space, grad_mixture, clip, features
    )
    space_pair = space_weights(
        order,
        sizes,
        second_input,
        grad_query,
        grad_keys,
        grad_values,
        mixture_space,
        grad_branch,
    )
    grad_first, space_sums, other_pair, grad_slots = middle_backward(
        order,
        sizes,
        grad_query,
        grad_keys,
        grad_values,
        after_time,
        grad_second,
        packed,
        vec,
        mixture_time,
        feed_sums,
        grad_feed_bias,
    )
    grad_slots = send_parts(grad_slots)
    core_flight = Flight(core_steps([space_pair, other_pair], batch_count))
    advance(order, core_flight, room=4)
    space_part = sum_chips(core_flight.result[0], batch_count)
    feed_flight = Flight(frame_steps(feed_part, frame_count, frame_flag))
    advance(order, feed_flight, after=grad_slots[1:], room=4)
    input_slots, time_kept, time_sent = time_backward(
        order,
        grad_slots,
        slots,
        qkv_time,
        prob_time,
        first_input,
        time_weight,
        vec,
        space_sums,
    )
    time_flight = Flight(sum_steps(time_kept, time_sent, sizes, frame_flag))
    input_slots = send_back(input_slots)
    space_flight = Flight(frame_steps(space_part, frame_count, frame_flag))
    advance(order, feed_flight, space_flight, room=4)
    whole = finish_together(order, space_flight, feed_flight)
    whole = lax.all_gather(whole, ("batch", "frame"), axis=0)
    while time_flight.result is None:
        advance(order, time_flight)
    space_part_rows = space_part.shape[0] // frame_count
    (
        grad_feed_inner,
        grad_feed_outer,
        grad_space_project,
        grad_space_output,
        grad_time_output,
    ) = deliver_parts(order, whole, space_part_rows)
    grad_time_project, time_vectors = deliver_halves(order, *time_flight.result)
    some_vectors = whole[5 * features // space_part_rows, :ROW_TILE].astype(jnp.float32)
    grad_tokens = add_slots(order, grad_first, input_slots, row_count)
    grad_tokens = grad_tokens.reshape(1, row_count, features)
    return (
        block_out,
        grad_tokens,
        grad_time_project,
        grad_time_output,
        time_vectors[0:5],
        grad_space_project,
        grad_space_output,
        some_vectors[0:5],
        grad_feed_inner,
        some_vectors[8:12].reshape(-1),
        grad_feed_outer,
        some_vectors[5:8],
    )


def solution(mesh):
    placed = (
        P("frame", "batch", None),
        P("batch"),
        P("frame", "batch", None),
        P("batch", None),
        P("batch", None),
        P(None, "batch"),
        P("batch", None),
        P("batch", None),
        P(None, "batch"),
        P("batch", None),
        P("batch"),
        P("batch", None),
        P(None, "batch"),
    )
    return jax.shard_map(
        body,
        mesh=mesh,
        in_specs=placed,
        out_specs=(
            P("frame", "batch", None),
            P("frame", "batch", None),
            P(),
            P(),
            P(),
            P(),
            P(),
            P(),
            P(),
            P(),
            P(),
            P(),
        ),
        check_vma=False,
    )
```

```python
import functools
import math

import jax
import jax.numpy as jnp
from jax import lax
from jax.experimental import pallas as pl
from jax.experimental.pallas import tpu as pltpu
from jax.sharding import PartitionSpec as P

HEADS = 12
UNITS = 4
PATCHES = 784
LOG2E = 1.4426950408889634
ROW_TILE = 16
FEED_BLOCKS = 8
LIMIT = 56
ROOM = 64


def round_up(count, step):
    return -(-count // step) * step


def struct(shape, dtype):
    return jax.ShapeDtypeStruct(shape, dtype)


def block_bytes(array, spec):
    shape = spec.block_shape or array.shape
    return math.prod(shape) * jnp.dtype(array.dtype).itemsize


VMEM = pl.BlockSpec(memory_space=pltpu.VMEM)
SMEM = pl.BlockSpec(memory_space=pltpu.SMEM)


class Order:
    def __init__(self, flags):
        self.flags = flags
        self.token = None

    def run(
        self,
        kernel,
        operands,
        in_specs,
        out_specs,
        out_shape,
        grid=(),
        scratch=(),
        prefetch=0,
        after=(),
        room=ROOM,
    ):
        token = [*after] if self.token is None else [self.token, *after]
        inputs, outputs, ordered = len(operands), len(out_shape), len(token)

        def body(*refs):
            refs = refs[:prefetch] + refs[prefetch + ordered :]
            token_ref = refs[inputs + outputs]
            token_ref[...] = jnp.zeros(token_ref.shape, token_ref.dtype)
            kernel(*refs[: inputs + outputs], *refs[inputs + outputs + 1 :])

        pairs = [*zip(operands[prefetch:], in_specs), *zip(out_shape, out_specs)]
        limit = sum(block_bytes(*pair) for pair in pairs) * (2 if math.prod(grid) > 1 else 1)
        limit += sum(math.prod(item.shape) * item.dtype.itemsize for item in scratch)
        limit = min(limit + (room << 20), LIMIT << 20)
        token_spec = pl.BlockSpec((8, 128), lambda *index: (0, 0))
        results = pl.pallas_call(
            body,
            grid_spec=pltpu.PrefetchScalarGridSpec(
                num_scalar_prefetch=prefetch,
                grid=grid,
                in_specs=[pl.BlockSpec(memory_space=pl.ANY)] * ordered + list(in_specs),
                out_specs=list(out_specs) + [token_spec],
                scratch_shapes=list(scratch),
            ),
            out_shape=list(out_shape) + [struct((8, 128), jnp.float32)],
            compiler_params=pltpu.CompilerParams(vmem_limit_bytes=limit),
        )(*operands[:prefetch], *token, *operands[prefetch:])
        self.token = results[-1]
        return results[:-1]


def shift_frames(block, frame_count, shift):
    if shift % frame_count == 0:
        return block
    pairs = [(index, (index + shift) % frame_count) for index in range(frame_count)]
    return lax.ppermute(block, "frame", pairs)


def rows_to_frames(rows, frame_count, frame_index):
    part = rows.shape[0] // frame_count
    slots = []
    for shift in range(frame_count):
        owner = (frame_index + shift) % frame_count
        block = lax.dynamic_slice_in_dim(rows, owner * part, part, 0)
        slots.append(shift_frames(block, frame_count, shift))
    return slots


def send_back(slots):
    return [shift_frames(slot, len(slots), -shift) for shift, slot in enumerate(slots)]


def swap_bit(block, axis, size, bit):
    pairs = [(index, index ^ (1 << bit)) for index in range(size)]
    return lax.ppermute(block, axis, pairs)


def shuffle_kernel(plan, source_count, flags_ref, *refs):
    sources, outputs = refs[:source_count], refs[source_count:]

    def emit(output, at, rows, terms):
        steps = [step for step in range(ROW_TILE, 65, ROW_TILE) if rows % step == 0]
        step = max(steps, default=rows)

        def some(index, carry):
            def load(term):
                source, start = term
                if steps:
                    return sources[source][pl.ds(pl.multiple_of(start + index * step, ROW_TILE), step)]
                return sources[source][start : start + step]

            value = load(terms[0])
            if len(terms) > 1:
                total = value.astype(jnp.float32)
                for term in terms[1:]:
                    total = total + load(term).astype(jnp.float32)
                value = total.astype(output.dtype)
            if steps:
                output[pl.ds(pl.multiple_of(at + index * step, ROW_TILE), step)] = value
            else:
                output[at : at + step] = value
            return carry

        if rows // step == 1:
            some(0, 0)
        else:
            lax.fori_loop(0, rows // step, some, 0)

    for output, segments in zip(outputs, plan):
        at = 0
        for rows, flag, *choices in segments:
            for value, terms in enumerate(choices):

                @pl.when(flags_ref[flag] == value)
                def _():
                    emit(output, at, rows, terms)

            at += rows


def shuffle(order, requests, after, room):
    sources, plan, counts = [], [], []
    for own_sources, own_plan in requests:
        base = len(sources)

        def lift(terms):
            return tuple((source + base, start) for source, start in terms)

        plan += [
            [(rows, flag, *map(lift, choices)) for rows, flag, *choices in out] for out in own_plan
        ]
        sources += own_sources
        counts.append(len(own_plan))
    features = sources[0].shape[1]
    shapes = [struct((sum(segment[0] for segment in out), features), jnp.bfloat16) for out in plan]
    results = order.run(
        functools.partial(shuffle_kernel, plan, len(sources)),
        [order.flags, *sources],
        [SMEM] + [VMEM] * len(sources),
        [VMEM] * len(plan),
        shapes,
        after=after,
        room=room,
    )
    outputs = []
    for count in counts:
        outputs.append(results[:count])
        results = results[count:]
    return outputs


def split_plan(rows, flag, left, right):
    half = rows // 2
    low = ((left[0], left[1]), (right[0], right[1]))
    high = ((left[0], left[1] + half), (right[0], right[1] + half))
    return [[(half, flag, high, low)], [(half, flag, low, high)]]


def join_plan(rows, flag, own, arrived):
    return [(rows, flag, (own,), (arrived,)), (rows, flag, (arrived,), (own,))]


def frame_parts(rows, frame_count, flag, terms_at):
    part = rows // frame_count
    return [
        [
            (part, flag)
            + tuple(terms_at((frame + shift) % frame_count * part) for frame in range(frame_count))
        ]
        for shift in range(frame_count)
    ]


def send_parts(parts):
    return [shift_frames(part, len(parts), shift) for shift, part in enumerate(parts)]


def add_parts(rows, flag, frame_count):
    terms = tuple((source, 0) for source in range(frame_count))
    return [[(rows // frame_count, flag, *[terms] * frame_count)]]


def frame_steps(block, frame_count, flag):
    (block,) = yield [block]
    rows = block.shape[0]
    parts = yield [block], frame_parts(rows, frame_count, flag, lambda at: ((0, at),))
    parts = yield send_parts(parts)
    return list(parts), add_parts(rows, flag, frame_count)


def core_steps(pairs, batch_size):
    moved = yield [swap_bit(sent, "batch", batch_size, 0) for _, sent in pairs]
    sources, segments = [], []
    for (kept, _), arrived in zip(pairs, moved):
        terms = ((len(sources), 0), (len(sources) + 1, 0))
        segments.append((kept.shape[0], 0, terms, terms))
        sources += [kept, arrived]
    return sources, [segments]


def sum_chips(block, batch_size):
    groups = [list(range(core, batch_size, 2)) for core in range(2)]
    return lax.psum_scatter(
        block, "batch", scatter_dimension=0, axis_index_groups=groups, tiled=True
    )


def sum_steps(kept, sent, sizes, flag):
    wide = list(range(1, sizes[0].bit_length() - 1))
    ways = (wide, wide[::-1])
    frame_count = sizes[1]

    def over_batch(block, bit):
        return swap_bit(block, "batch", sizes[0], bit)

    (arrived,) = yield [over_batch(sent, 0)]
    rows = kept.shape[0] // 2
    sources = [kept, arrived]
    pairs = [((0, 0), (1, 0)), ((0, rows), (1, rows))]
    for level in range(len(wide)):
        plan = []
        for (left, right), way in zip(pairs, ways):
            plan += split_plan(rows, way[level], left, right)
        first_out, first_kept, second_out, second_kept = yield sources, plan
        moved = yield [over_batch(first_out, ways[0][level]), over_batch(second_out, ways[1][level])]
        sources = [first_kept, moved[0], second_kept, moved[1]]
        pairs = [((0, 0), (1, 0)), ((2, 0), (3, 0))]
        rows //= 2

    def terms_at(start):
        (left, right), at = pairs[start // rows], start % rows
        return (left[0], left[1] + at), (right[0], right[1] + at)

    parts = yield sources, frame_parts(2 * rows, frame_count, flag, terms_at)
    parts = yield send_parts(parts)
    (part,) = yield parts, add_parts(2 * rows, flag, frame_count)
    parts = yield [shift_frames(part, frame_count, shift) for shift in range(frame_count)]
    size = 2 * rows // frame_count
    segments = [
        (size, flag) + tuple((((frame - owner) % frame_count, 0),) for frame in range(frame_count))
        for owner in range(frame_count)
    ]
    blocks = yield parts, [segments[: frame_count // 2], segments[frame_count // 2 :]]
    for level in range(len(wide))[::-1]:
        moved = yield [over_batch(block, way[level]) for block, way in zip(blocks, ways)]
        sources = [blocks[0], moved[0], blocks[1], moved[1]]
        plan = [join_plan(rows, ways[0][level], (0, 0), (1, 0))]
        plan += [join_plan(rows, ways[1][level], (2, 0), (3, 0))]
        if level == 0:
            plan = [plan[0] + plan[1]]
        blocks = yield sources, plan
        rows *= 2
    (arrived,) = yield [over_batch(blocks[0], 0)]
    return blocks[0], arrived


def gather_steps(shard, batch_size):
    wide = list(range(1, batch_size.bit_length() - 1))
    ways = (wide, wide[::-1])
    half = shard.shape[0] // 2

    def over_batch(block, bit):
        return swap_bit(block, "batch", batch_size, bit)

    blocks = [shard[:half], shard[half:]]
    done = [[], []]
    for level in range(len(wide)):
        moved = yield [over_batch(block, way[level]) for block, way in zip(blocks, ways)]
        plan = []
        for index, way in enumerate(ways):
            bit, before = way[level], done[index]
            done[index] = sorted([*before, bit])
            segments = []
            for place in range(2 ** len(done[index])):
                value = {one: (place >> at) & 1 for at, one in enumerate(done[index])}
                row = half * sum(value[one] << at for at, one in enumerate(before))
                own, other = ((2 * index, row),), ((2 * index + 1, row),)
                segments.append((half, bit, *((other, own) if value[bit] else (own, other))))
            plan.append(segments)
        if level == len(wide) - 1:
            plan = [plan[0] + plan[1]]
        blocks = yield [blocks[0], moved[0], blocks[1], moved[1]], plan
    (block,) = blocks
    (arrived,) = yield [over_batch(block, 0)]
    segments = []
    for place in range(batch_size):
        for index in range(2):
            row = (index * batch_size // 2 + (place >> 1)) * half
            own, other = ((0, row),), ((1, row),)
            segments.append((half, 0, *((other, own) if place & 1 else (own, other))))
    (whole,) = yield [block, arrived], [segments]
    return whole


class Flight:
    def __init__(self, steps):
        self.steps, self.result = steps, None
        self.moved = next(steps)

    def send(self, value):
        try:
            return self.steps.send(value)
        except StopIteration as stop:
            self.result = stop.value
            return None


def advance(order, *flights, after=(), room=ROOM):
    active, requests = [], []
    for flight in flights:
        if flight.result is not None:
            continue
        request = flight.send(flight.moved)
        if request is None and isinstance(flight.result[0], list):
            request = flight.result
        if request is not None:
            active.append(flight)
            requests.append(request)
    if requests:
        for flight, outputs in zip(active, shuffle(order, requests, after, room)):
            if flight.result is None:
                flight.moved = flight.send(outputs)
            else:
                flight.result = outputs


def finish_together(order, *flights):
    sources, segments = [], []
    for flight in flights:
        if flight.result is None:
            flight.send(flight.moved)
            parts, ((segment,),) = flight.result
        else:
            parts = flight.result
            segment = (parts[0].shape[0], 0, ((0, 0),), ((0, 0),))
        rows, flag, *choices = segment
        base = len(sources)
        segments.append(
            (rows, flag, *[tuple((source + base, at) for source, at in terms) for terms in choices])
        )
        sources += parts
    ((whole,),) = shuffle(order, [(sources, [segments])], (), 4)
    return whole


def deliver_kernel(flags_ref, own_ref, arrived_ref, out_ref, rest_ref):
    half, features = own_ref.shape
    columns = out_ref.shape[1] // features
    for core in range(2):

        @pl.when(flags_ref[0] == core)
        def _():
            for index in range(columns + 1):
                first = index * features
                height = features if index < columns else rest_ref.shape[0]
                while height:
                    owner, at = divmod(first, half)
                    size = min(height, half - at)
                    piece = (own_ref if owner == core else arrived_ref)[at : at + size]
                    piece = piece.astype(jnp.float32)
                    row = first % features
                    if index < columns:
                        span = slice(index * features, (index + 1) * features)
                        out_ref[row : row + size, span] = piece
                    else:
                        rest_ref[row : row + size] = piece
                    first, height = first + size, height - size


def deliver_halves(order, own, arrived):
    half, features = own.shape
    columns = 2 * half // features
    return order.run(
        deliver_kernel,
        [order.flags, own, arrived],
        [SMEM, VMEM, VMEM],
        [VMEM, VMEM],
        [struct((features, columns * features), jnp.float32), struct((8, features), jnp.float32)],
    )


def deliver_parts_kernel(outputs, counts, *refs):
    step = pl.program_id(0)
    feed_refs, space_refs = refs[: counts[0]], refs[counts[0] : sum(counts)]
    for number, (output, (first, last, _)) in enumerate(zip(refs[sum(counts) :], outputs)):
        sources = feed_refs if number < 2 else space_refs

        @pl.when((step >= first) & (step < last))
        def _():
            rows = sources[0].shape[1]
            for piece in range(sources[0].shape[0]):
                for index, source in enumerate(sources):
                    at = (piece * len(sources) + index) * rows
                    output[at : at + rows] = source[piece].astype(output.dtype)


def deliver_parts(order, gathered, space_part):
    _, part, features = gathered.shape
    feed_part = part - space_part
    unit = math.gcd(space_part, feed_part)

    def source(rows, first, step_of, index):
        def place(step):
            return step_of(step), first // unit + index, 0

        return pl.BlockSpec((features // rows, unit, features), place)

    counts = (feed_part // unit, space_part // unit)
    feed_specs = [
        source(feed_part, space_part, lambda step: jnp.minimum(step, FEED_BLOCKS - 1), index)
        for index in range(counts[0])
    ]
    space_specs_ = [
        source(space_part, 0, lambda step: jnp.minimum(step, 4), index)
        for index in range(counts[1])
    ]
    half = FEED_BLOCKS // 2
    outputs = [(0, half, True), (half, FEED_BLOCKS, False)]
    for first, last, wide in ((0, 3, True), (3, 4, False), (4, 5, False)):
        outputs.append((first, last, wide))

    def spot(first, last, wide):
        def index(step):
            at = jnp.clip(step - first, 0, last - first - 1)
            return (0, at) if wide else (at, 0)

        return pl.BlockSpec((features, features), index)

    def shape(first, last, wide):
        rows = (last - first) * features
        return struct((features, rows) if wide else (rows, features), jnp.float32)

    return order.run(
        functools.partial(deliver_parts_kernel, outputs, counts),
        [gathered] * sum(counts),
        feed_specs + space_specs_,
        [spot(*item) for item in outputs],
        [shape(*item) for item in outputs],
        grid=(FEED_BLOCKS,),
    )


def contract(x,y,dims):
    return lax.dot_general(x,y,((dims[0:1],dims[1:2]),((),())),preferred_element_type=jnp.float32)

def widen_rows(values, wide):
    rows, width = values.shape
    if wide == rows:
        return values
    return jnp.concatenate([values, jnp.zeros((wide - rows, width), values.dtype)])


def head_halves(width):
    lane = lax.broadcasted_iota(jnp.int32, (1, width), 1)
    return [lane < width // 2, lane >= width // 2]

def space_forward_kernel(
    scale, mark_q_ref, mark_k_ref, q_ref, k_ref, v_ref, mixture_ref, total_ref, k_wide, v_wide
):
    rows, width = q_ref.shape
    wide = k_wide.shape[0]
    if wide > rows:

        @pl.when(pl.program_id(0) == 0)
        def _():
            k_wide[rows:] = jnp.zeros((wide - rows, width), k_wide.dtype)
            v_wide[rows:] = jnp.zeros((wide - rows, width), v_wide.dtype)

    k_wide[:rows] = k_ref[...]
    v_wide[:rows] = v_ref[...]
    halves = head_halves(width)
    one = jnp.ones((), q_ref.dtype)
    outs, tops = [], []
    for half in halves:
        queries = jnp.where(half, q_ref[...], mark_q_ref[:rows])
        keys = jnp.where(half, k_wide[...], mark_k_ref[...])
        scores = contract(queries, keys, (1, 1)) * (scale * LOG2E)
        top = jnp.max(scores, axis=1, keepdims=True)
        weights = jnp.exp2(scores - top)
        values = jnp.where(half, v_wide[...], one)
        outs.append(contract(weights.astype(jnp.bfloat16), values, (1, 0)))
        tops.append(top)
    mass = pltpu.roll(jnp.where(halves[0], outs[1], outs[0]), width // 2, 1)
    mixture = jnp.where(halves[0], outs[0], outs[1]) / mass
    mixture_ref[...] = mixture.astype(mixture_ref.dtype)
    total_ref[...] = jnp.where(halves[0], tops[0], tops[1]) + jnp.log2(mass)


def space_specs(rows, features):
    pairs = HEADS // 2
    width = features // pairs
    wide = round_up(rows, 128)
    fixed = [pl.BlockSpec((wide, width), lambda i: (0, 0))] * 2
    blocks = [pl.BlockSpec((rows, width), lambda i, o=o: (0, o + i)) for o in (0, pairs, 2 * pairs)]
    out = pl.BlockSpec((rows, width), lambda i: (0, i))
    scratch = [pltpu.VMEM((wide, width), jnp.bfloat16)] * 2
    return pairs, (features // HEADS) ** -0.5, fixed + blocks, out, scratch


def clip_marks(clip, width):
    rows = clip.shape[0]
    clip = jnp.pad(clip, (0, round_up(rows, 128) - rows), constant_values=-2)
    same = (clip[:, None] + 2) == jnp.arange(width, dtype=jnp.int32)[None] % (width // 2)
    return same.astype(jnp.bfloat16), jnp.where(same, 0.0, -1e30).astype(jnp.bfloat16)


def space_forward(order, qkv, clip, features):
    rows = qkv.shape[0]
    pairs, scale, specs, out, scratch = space_specs(rows, features)
    return order.run(
        functools.partial(space_forward_kernel, scale),
        [*clip_marks(clip, features // pairs), qkv, qkv, qkv],
        specs,
        [out, out],
        [struct((rows, features), jnp.bfloat16), struct((rows, features), jnp.float32)],
        grid=(pairs,),
        scratch=scratch,
    )


def space_backward_kernel(
    scale, mark_q_ref, mark_k_ref, q_ref, k_ref, v_ref, mixture_ref, total_ref, grad_ref, dq_ref, dk_ref, dv_ref,
    q_wide, g_wide
):
    rows, width = q_ref.shape
    wide = q_wide.shape[0]
    if wide > rows:

        @pl.when(pl.program_id(0) == 0)
        def _():
            q_wide[rows:] = jnp.zeros((wide - rows, width), q_wide.dtype)
            g_wide[rows:] = jnp.zeros((wide - rows, width), g_wide.dtype)

    q_wide[:rows] = q_ref[...]
    g_wide[:rows] = grad_ref[...]
    halves = head_halves(width)
    zero = jnp.zeros((), q_ref.dtype)
    product = grad_ref[...].astype(jnp.float32) * mixture_ref[...].astype(jnp.float32)
    sums = [jnp.sum(jnp.where(half, product, 0.0), axis=1, keepdims=True) for half in halves]
    delta = widen_rows(jnp.where(halves[0], sums[0], sums[1]), wide).T
    total = widen_rows(total_ref[...], wide).T
    parts = [[], [], [], [], []]
    for index, half in enumerate(halves):
        at = index * (width // 2)
        queries = jnp.where(half, q_wide[...], mark_q_ref[...])
        keys = jnp.where(half, k_ref[...], mark_k_ref[:rows])
        values = jnp.where(half, v_ref[...], zero)
        scores = contract(keys, queries, (1, 1)) * (scale * LOG2E)
        weights = jnp.exp2(scores - total[at : at + 1])
        slopes = contract(values, g_wide[...], (1, 1))
        slopes = (weights * (slopes - delta[at : at + 1])).astype(jnp.bfloat16)
        own = (
            weights.astype(jnp.bfloat16),
            slopes,
            jnp.where(half, g_wide[...], zero),
            jnp.where(half, q_wide[...], zero),
            jnp.where(half, k_ref[...], zero),
        )
        for part, value in zip(parts, own):
            part.append(value)
    weights, slopes, grads, queries, keys = parts
    grads, queries, keys = (jnp.concatenate(part, axis=0) for part in (grads, queries, keys))
    dv_ref[...] = contract(jnp.concatenate(weights, axis=1), grads, (1, 0)).astype(dv_ref.dtype)
    dk = contract(jnp.concatenate(slopes, axis=1), queries, (1, 0))
    dk_ref[...] = (dk * scale).astype(dk_ref.dtype)
    dq = contract(jnp.concatenate(slopes, axis=0), keys, (0, 0))
    dq_ref[...] = (dq[:rows] * scale).astype(dq_ref.dtype)


def space_backward(order, qkv, mixture, total, grad, clip, features):
    rows = qkv.shape[0]
    pairs, scale, specs, out, scratch = space_specs(rows, features)
    return order.run(
        functools.partial(space_backward_kernel, scale),
        [*clip_marks(clip, features // pairs), qkv, qkv, qkv, mixture, total, grad],
        specs + [out] * 3,
        [out] * 3,
        [struct((rows, features), jnp.bfloat16)] * 3,
        grid=(pairs,),
        scratch=scratch,
    )


def norm_parts(values):
    average = jnp.mean(values, axis=1, keepdims=True)
    centered = values - average
    spread = lax.rsqrt(jnp.mean(centered * centered, axis=1, keepdims=True) + 1e-06)
    return centered * spread, spread
def norm_back(grad, normed, spread, gain):
    scaled = grad * gain
    return spread * (scaled - jnp.mean(scaled, axis=1, keepdims=True) - normed * jnp.mean(scaled * normed, axis=1, keepdims=True))
def column_sum(values):
    return jnp.sum(values, axis=0, keepdims=True)

def square_spec(packed, index):
    batch_count, _, features = packed.shape
    return pl.BlockSpec((batch_count, features // batch_count, features), lambda i: (0, index, 0))


def square(ref):
    return ref[...].reshape(-1, ref.shape[-1])


def feed_kernel(chunks, x1_ref, mixture_ref, dz_ref, so_ref, fi_ref, fo_ref, fb_ref, vec_ref,
                out_ref, dx2_ref, dys_ref, dos_ref, grad_ref, gfb_ref, gvec_ref,
                x2_s, a3_s, a3t_s, acc_s, da_s, g_s, dh_s):
    step = pl.program_id(0)
    rows = x1_ref.shape[0]
    @pl.when(step == 0)
    def _():
        x2 = x1_ref[...] + contract(mixture_ref[...], square(so_ref), (1, 0)) + vec_ref[9:10]
        x2_s[...] = x2
        normed, _ = norm_parts(x2)
        a3 = (normed * vec_ref[10:11] + vec_ref[11:12]).astype(jnp.bfloat16)
        a3_s[...] = a3
        a3t_s[...] = a3.T
        acc_s[...] = x2 + vec_ref[12:13]
        da_s[...] = jnp.zeros_like(da_s)
    inner, outer = square(fi_ref), square(fo_ref)
    part = rows // chunks
    for chunk in range(chunks):
        span = slice(chunk * part, (chunk + 1) * part)
        hidden = contract(a3_s[span], inner, (1, 0)) + fb_ref[...]
        cdf = 0.5 + 0.5 * lax.erf(hidden * math.sqrt(0.5))
        slope = cdf + hidden * jnp.exp(hidden * hidden * -0.5) * (1.0 / math.sqrt(2.0 * math.pi))
        active = (hidden * cdf).astype(jnp.bfloat16)
        g_s[span] = active
        dh = (contract(dz_ref[span], outer, (1, 1)) * slope).astype(jnp.bfloat16)
        dh_s[span] = dh
        acc_s[span] += contract(active, outer, (1, 0))
        da_s[span] += contract(dh, inner, (1, 1))
    grad_ref[0] = contract(a3t_s[...], dh_s[...], (1, 0)).astype(grad_ref.dtype)
    grad_ref[1] = contract(g_s[...], dz_ref[...], (0, 0)).astype(grad_ref.dtype)
    gfb_ref[...] = column_sum(dh_s[...].astype(jnp.float32))
    @pl.when(step == pl.num_programs(0) - 1)
    def _():
        out_ref[0] = acc_s[: out_ref.shape[1]].astype(out_ref.dtype)
        normed, spread = norm_parts(x2_s[...])
        grad = da_s[...]
        dz = dz_ref[...].astype(jnp.float32)
        dx2 = dz + norm_back(grad, normed, spread, vec_ref[10:11])
        dx2_ref[...] = dx2
        dys = dx2.astype(jnp.bfloat16)
        dys_ref[...] = dys
        dos_ref[...] = contract(dys, square(so_ref), (1, 1)).astype(dos_ref.dtype)
        gvec_ref[0:1] = column_sum(grad * normed)
        gvec_ref[1:2] = column_sum(grad)
        gvec_ref[2:3] = column_sum(dz)
        gvec_ref[3:4] = column_sum(dys.astype(jnp.float32))
        gvec_ref[4:8] = jnp.zeros((4, gvec_ref.shape[1]), jnp.float32)

def feed_block(order, row_count, x1, mixture, dz, feed_packed, bias, vec, chunks):
    rows, features = x1.shape
    batch_count = feed_packed.shape[0]
    hidden = bias.shape[1]
    whole = pl.BlockSpec((rows, features), lambda j: (0, 0))
    line = pl.BlockSpec((1, features), lambda j: (0, j))
    shard = hidden // batch_count
    low, full = jnp.bfloat16, jnp.float32
    return order.run(
        functools.partial(feed_kernel, chunks),
        [x1, mixture, dz, feed_packed, feed_packed, feed_packed, bias, vec],
        [
            whole,
            whole,
            whole,
            square_spec(feed_packed, 2 * hidden // features),
            pl.BlockSpec((batch_count, features // batch_count, features), lambda j: (0, j, 0)),
            pl.BlockSpec((features // shard, shard, features), lambda j: (j, 1, 0)),
            line,
            pl.BlockSpec(vec.shape, lambda j: (0, 0)),
        ],
        [
            pl.BlockSpec((1, row_count, features), lambda j: (0, 0, 0)),
            whole,
            whole,
            whole,
            pl.BlockSpec((2, features, features), lambda j: (0, j, 0)),
            line,
            pl.BlockSpec((8, features), lambda j: (0, 0)),
        ],
        [
            struct((1, row_count, features), low),
            struct((rows, features), full),
            struct((rows, features), low),
            struct((rows, features), low),
            struct((2, hidden, features), low),
            struct((1, hidden), full),
            struct((8, features), full),
        ],
        grid=(hidden // features,),
        scratch=[
            pltpu.VMEM((rows, features), full),
            pltpu.VMEM((rows, features), low),
            pltpu.VMEM((features, rows), low),
            pltpu.VMEM((rows, features), full),
            pltpu.VMEM((rows, features), full),
            pltpu.VMEM((rows, features), low),
            pltpu.VMEM((rows, features), low),
        ],
    )


def gather_rows(count, frame, slots, rows_s):
    part = slots[0].shape[0]
    for shift in range(count):
        owner = lax.rem(frame + shift, count)
        rows_s[pl.ds(pl.multiple_of(owner * part, ROW_TILE), part)] = slots[shift][...]


def middle_kernel(count, frame_flag, flags_ref, token_ref, *refs):
    slots, (to_ref, *sp_refs, vec_ref) = refs[:count], refs[count : count + 5]
    mixture_ref, x1_ref, a2_ref, qkv_ref = refs[count + 5 :]
    rows, features = token_ref.shape
    gather_rows(count, flags_ref[frame_flag], slots, mixture_ref)
    number = lax.broadcasted_iota(jnp.int32, (rows, 1), 0)
    branch = contract(mixture_ref[...], square(to_ref), (1, 0)) + vec_ref[4:5]
    x1 = token_ref[...].astype(jnp.float32) + jnp.where(number < PATCHES, branch, 0.0)
    x1_ref[...] = x1
    normed, _ = norm_parts(x1)
    a2 = (normed * vec_ref[5:6] + vec_ref[6:7]).astype(jnp.bfloat16)
    a2_ref[...] = a2
    for third in range(3):
        span = slice(third * features, (third + 1) * features)
        joined = contract(a2, square(sp_refs[third]), (1, 0))
        if third != 1:
            joined = joined + vec_ref[7 + third // 2 : 8 + third // 2]
        qkv_ref[:, span] = joined.astype(jnp.bfloat16)


def project_specs(packed, vec):
    return [square_spec(packed, index) for index in range(4)] + [
        pl.BlockSpec(vec.shape, lambda i: (0, 0))
    ]


def middle_forward(order, tokens, slots, packed, vec):
    rows, features = tokens.shape
    low = jnp.bfloat16
    return order.run(
        functools.partial(middle_kernel, len(slots), order.flags.shape[0] - 1),
        [order.flags, tokens, *slots, *[packed] * 4, vec],
        [SMEM] + [VMEM] * (len(slots) + 1) + project_specs(packed, vec),
        [VMEM] * 4,
        [
            struct((rows, features), low),
            struct((rows, features), jnp.float32),
            struct((rows, features), low),
            struct((rows, 3 * features), low),
        ],
        grid=(1,),
    )


def middle_back_kernel(
    sizes, part, flags_ref, dq_ref, dk_ref, dv_ref, x1_ref, dx2_ref, to_ref, *refs
):
    *sp_refs, vec_ref, time_ref, feed_ref, bias_ref = refs[:7]
    dx1_ref, sums_ref, kept_ref, sent_ref = refs[7:11]
    count = sizes[1]
    slots, rows_s = refs[11 : 11 + count], refs[11 + count]
    rows, features = x1_ref.shape
    grad = 0.0
    for third, piece in enumerate((dq_ref, dk_ref, dv_ref)):
        grad = grad + contract(piece[...], square(sp_refs[third]), (1, 1))
    normed, spread = norm_parts(x1_ref[...])
    dx1 = dx2_ref[...] + norm_back(grad, normed, spread, vec_ref[5:6])
    dx1_ref[...] = dx1
    number = lax.broadcasted_iota(jnp.int32, (rows, 1), 0)
    dyt = jnp.where(number < PATCHES, dx1, 0.0).astype(jnp.bfloat16)
    rows_s[...] = contract(dyt, square(to_ref), (1, 1)).astype(rows_s.dtype)
    block = rows // count
    for shift in range(count):
        owner = lax.rem(flags_ref[flags_ref.shape[0] - 1] + shift, count)
        slots[shift][...] = rows_s[pl.ds(pl.multiple_of(owner * block, ROW_TILE), block)]
    sums_ref[0:1] = column_sum(grad * normed)
    sums_ref[1:2] = column_sum(grad)
    sums_ref[2:3] = column_sum(dq_ref[...].astype(jnp.float32))
    sums_ref[3:4] = column_sum(dv_ref[...].astype(jnp.float32))
    sums_ref[4:5] = column_sum(dyt.astype(jnp.float32))
    sums_ref[5:8] = jnp.zeros((3, features), jnp.float32)
    first = 4 * features
    put = functools.partial(put_parts, flags_ref, kept_ref, sent_ref, sizes, part, first)
    put(first, contract(time_ref[...], dyt, (0, 0)))
    bias = bias_ref[...]
    lines = [bias[:, at : at + features] for at in range(0, bias.shape[1], features)]
    pieces = [sums_ref[0:4], feed_ref[3:4], feed_ref[0:3], *lines]
    put(first + features, fill_rows(pieces, 2 * kept_ref.shape[0] - features, features))


def middle_backward(order, sizes, dq, dk, dv, x1, dx2, packed, vec, mixture, feed_sums, bias):
    rows, features = x1.shape
    count = sizes[1]
    low, full = jnp.bfloat16, jnp.float32
    total, part = space_rows(sizes, features)
    half = struct(((total - 4 * features) // 2, features), low)
    results = order.run(
        functools.partial(middle_back_kernel, sizes, part),
        [order.flags, dq, dk, dv, x1, dx2, *[packed] * 4, vec, mixture, feed_sums, bias],
        [SMEM] + [VMEM] * 5 + project_specs(packed, vec) + [VMEM] * 3,
        [VMEM] * (4 + count),
        [struct((rows, features), full), struct((8, features), full), half, half]
        + [struct((rows // count, features), low)] * count,
        grid=(1,),
        scratch=[pltpu.VMEM((rows, features), low)],
        room=14,
    )
    return results[0], results[1], results[2:4], results[4:]


def put_half(core_ref, kept_ref, sent_ref, at, value):
    half = kept_ref.shape[0]
    low = value.astype(kept_ref.dtype)
    part = math.gcd(half, low.shape[0])
    for offset in range(0, low.shape[0], part):
        owner, first = divmod(at + offset, half)
        piece = low[offset : offset + part]

        @pl.when(core_ref[0] == owner)
        def _():
            kept_ref[first : first + part] = piece

        @pl.when(core_ref[0] != owner)
        def _():
            sent_ref[first : first + part] = piece


def fill_rows(pieces, rows, features):
    used = sum(piece.shape[0] for piece in pieces)
    return jnp.concatenate([*pieces, jnp.zeros((rows - used, features), jnp.float32)])


def put_parts(core_ref, kept_ref, sent_ref, sizes, part, first, at, value):
    low = value.astype(kept_ref.dtype)
    for offset in range(0, low.shape[0], part):
        batch, frame = divmod((at + offset) // part, sizes[1])
        start = ((batch >> 1) * sizes[1] + frame) * part - first // 2
        piece = low[offset : offset + part]

        @pl.when(core_ref[0] == batch & 1)
        def _():
            kept_ref[start : start + part] = piece

        @pl.when(core_ref[0] != batch & 1)
        def _():
            sent_ref[start : start + part] = piece


def space_rows(sizes, features):
    rows = round_up(5 * features + ROW_TILE, sizes[0] * sizes[1] * ROW_TILE)
    return rows, rows // (sizes[0] * sizes[1])


def space_weights_kernel(
    sizes, part, flags_ref, a2_ref, dq_ref, dk_ref, dv_ref, mixture_ref, dys_ref, kept_ref, sent_ref
):
    features = a2_ref.shape[1]
    put = functools.partial(put_parts, flags_ref, kept_ref, sent_ref, sizes, part, 0)
    turned = a2_ref[...].T
    for third, piece in enumerate((dq_ref, dk_ref, dv_ref)):
        put(third * features, contract(turned, piece[...], (1, 0)))
    put(3 * features, contract(mixture_ref[...], dys_ref[...], (0, 0)))


def space_weights(order, sizes, *operands):
    features = operands[0].shape[1]
    part = space_rows(sizes, features)[1]
    half = struct((2 * features, features), jnp.bfloat16)
    return order.run(
        functools.partial(space_weights_kernel, sizes, part),
        [order.flags, *operands],
        [SMEM] + [VMEM] * len(operands),
        [VMEM] * 2,
        [half, half],
    )


CHUNK = 16
def head_map(features, lanes=128):
    head = jnp.arange(features, dtype=jnp.int32) // (features // HEADS)
    return (head[:, None] == jnp.arange(lanes, dtype=jnp.int32)[None]).astype(jnp.bfloat16)

def pair_sums(left, right, gather_ref, pair_s):
    count = len(left)
    for f in range(count):
        for g in range(count):
            at = (f * count + g) * CHUNK
            pair_s[at:at + CHUNK] = (left[f] * right[g]).astype(jnp.bfloat16)
    return contract(pair_s[...], gather_ref[...], (1, 0))

def time_forward_kernel(count, scale, *refs):
    slots, (tp_ref, vec_ref, gather_ref, spread_ref) = refs[:count], refs[count:count + 4]
    outs, (qkv_ref, prob_ref, a1_ref) = refs[count + 4:2 * count + 4], refs[2 * count + 4:2 * count + 7]
    pair_s, weight_s = refs[2 * count + 7:]
    part, features = slots[0].shape
    for s in range(count):
        normed, _ = norm_parts(slots[s][...].astype(jnp.float32))
        a1_ref[s * part:(s + 1) * part] = (normed * vec_ref[0:1] + vec_ref[1:2]).astype(jnp.bfloat16)
    for third in range(3):
        span = slice(third * features, (third + 1) * features)
        joined = contract(a1_ref[...], tp_ref[:, span], (1, 0))
        if third != 1:
            joined = joined + vec_ref[2 + third // 2:3 + third // 2]
        qkv_ref[:, span] = joined.astype(jnp.bfloat16)

    def chunk_step(index, carry):
        def rows_of(s, third):
            start = pl.multiple_of(s * part + index * CHUNK, CHUNK)
            return qkv_ref[pl.ds(start, CHUNK), third * features:(third + 1) * features].astype(jnp.float32)
        queries, keys, values = ([rows_of(s, third) for s in range(count)] for third in range(3))
        scores = pair_sums(queries, keys, gather_ref, pair_s) * (scale * LOG2E)
        place = pl.ds(pl.multiple_of(index * CHUNK, CHUNK), CHUNK)
        for f in range(count):
            row = [scores[(f * count + g) * CHUNK:(f * count + g + 1) * CHUNK] for g in range(count)]
            top = functools.reduce(jnp.maximum, row)
            raised = [jnp.exp2(item - top) for item in row]
            mass = functools.reduce(jnp.add, raised)
            for g in range(count):
                weight = raised[g] / mass
                prob_ref[f * count + g, place] = weight
                at = (f * count + g) * CHUNK
                weight_s[at:at + CHUNK] = weight.astype(jnp.bfloat16)
        wide = contract(weight_s[...], spread_ref[...], (1, 0))
        for f in range(count):
            total = 0.0
            for g in range(count):
                at = (f * count + g) * CHUNK
                total = total + wide[at:at + CHUNK] * values[g]
            outs[f][place] = total.astype(jnp.bfloat16)
        return carry
    lax.fori_loop(0, part // CHUNK, chunk_step, 0, unroll=True)

def time_forward(order, slots, time_weight, vec):
    count = len(slots)
    part, features = slots[0].shape
    gather = head_map(features)
    low, full = jnp.bfloat16, jnp.float32
    results = order.run(
        functools.partial(time_forward_kernel, count, (features // HEADS) ** -0.5),
        [*slots, time_weight, vec, gather, gather.T],
        [VMEM] * count + [pl.BlockSpec((features, 3 * features), lambda i: (0, 0)), VMEM, VMEM, VMEM],
        [VMEM] * (count + 3),
        [struct((part, features), low)] * count
        + [
            struct((count * part, 3 * features), low),
            struct((count * count, part, 128), full),
            struct((count * part, features), low),
        ],
        grid=(1,),
        scratch=[
            pltpu.VMEM((count * count * CHUNK, features), low),
            pltpu.VMEM((count * count * CHUNK, 128), low),
        ],
    )
    return results[:count], results[count], results[count + 1], results[count + 2]


def time_backward_kernel(count, scale, flags_ref, *refs):
    grads, slots = refs[:count], refs[count : 2 * count]
    qkv_ref, prob_ref, a1_ref, gather_ref, spread_ref, tp_ref, vec_ref, other_ref = refs[2 * count : 2 * count + 8]
    refs = refs[2 * count + 8 :]
    outs, (kept_ref, sent_ref, dqkv_ref, pair_s, weight_s) = refs[:count], refs[count:]
    part, features = grads[0].shape
    def chunk_step(index, carry):
        place = pl.ds(pl.multiple_of(index * CHUNK, CHUNK), CHUNK)
        def rows_of(s, third):
            start = pl.multiple_of(s * part + index * CHUNK, CHUNK)
            return qkv_ref[pl.ds(start, CHUNK), third * features:(third + 1) * features].astype(jnp.float32)
        queries, keys, values = ([rows_of(s, third) for s in range(count)] for third in range(3))
        outer = [grads[s][place].astype(jnp.float32) for s in range(count)]
        slopes = pair_sums(outer, values, gather_ref, pair_s)
        size = count * count * CHUNK
        for f in range(count):
            row = [slopes[(f * count + g) * CHUNK:(f * count + g + 1) * CHUNK] for g in range(count)]
            weights = [prob_ref[f * count + g, place] for g in range(count)]
            delta = functools.reduce(jnp.add, [w * s for w, s in zip(weights, row)])
            for g in range(count):
                at = (f * count + g) * CHUNK
                weight_s[at:at + CHUNK] = weights[g].astype(jnp.bfloat16)
                weight_s[size + at:size + at + CHUNK] = (weights[g] * (row[g] - delta)).astype(jnp.bfloat16)
        wide = contract(weight_s[...], spread_ref[...], (1, 0))
        for s in range(count):
            dq, dk, dv = 0.0, 0.0, 0.0
            for t in range(count):
                forth, back = (s * count + t) * CHUNK, (t * count + s) * CHUNK
                dq = dq + wide[size + forth:size + forth + CHUNK] * keys[t]
                dk = dk + wide[size + back:size + back + CHUNK] * queries[t]
                dv = dv + wide[back:back + CHUNK] * outer[t]
            start = pl.ds(pl.multiple_of(s * part + index * CHUNK, CHUNK), CHUNK)
            for third, value in enumerate((dq * scale, dk * scale, dv)):
                dqkv_ref[start, third * features:(third + 1) * features] = value.astype(jnp.bfloat16)
        return carry
    lax.fori_loop(0, part // CHUNK, chunk_step, 0, unroll=True)
    a1t = a1_ref[...].T
    put = functools.partial(put_half, flags_ref, kept_ref, sent_ref)
    for third in range(3):
        span = slice(third * features, (third + 1) * features)
        put(third * features, contract(a1t, dqkv_ref[:, span], (1, 0)))
    grad = contract(dqkv_ref[...], tp_ref[...], (1, 1))
    gain, shift = 0.0, 0.0
    for s in range(count):
        piece = grad[s * part : (s + 1) * part]
        normed, spread = norm_parts(slots[s][...].astype(jnp.float32))
        outs[s][...] = norm_back(piece, normed, spread, vec_ref[0:1]).astype(jnp.bfloat16)
        gain = gain + column_sum(piece * normed)
        shift = shift + column_sum(piece)
    sums = [
        gain,
        shift,
        column_sum(dqkv_ref[:, :features].astype(jnp.float32)),
        column_sum(dqkv_ref[:, 2 * features :].astype(jnp.float32)),
        other_ref[4:5],
    ]
    put(3 * features, fill_rows(sums, 2 * kept_ref.shape[0] - 3 * features, features))


def time_backward(order, grads, slots, qkv, prob, a1, time_weight, vec, other):
    count = len(grads)
    part, features = grads[0].shape
    gather = head_map(features)
    low = jnp.bfloat16
    half = struct((round_up(3 * features + 16, 512) // 2, features), low)
    results = order.run(
        functools.partial(time_backward_kernel, count, (features // HEADS) ** -0.5),
        [order.flags, *grads, *slots, qkv, prob, a1, gather, gather.T, time_weight, vec, other],
        [SMEM] + [VMEM] * (2 * count + 5)
        + [pl.BlockSpec((features, 3 * features), lambda i: (0, 0)), VMEM, VMEM],
        [VMEM] * (count + 2),
        [struct((part, features), low)] * count + [half, half],
        grid=(1,),
        scratch=[
            pltpu.VMEM(qkv.shape, low),
            pltpu.VMEM((count * count * CHUNK, features), low),
            pltpu.VMEM((2 * count * count * CHUNK, 128), low),
        ],
    )
    return results[:count], results[count], results[count + 1]


def place_kernel(flags_ref, first_ref, *refs):
    slots, out_ref, rows_s = refs[:-2], refs[-2], refs[-1]
    gather_rows(len(slots), flags_ref[flags_ref.shape[0] - 1], slots, rows_s)
    lanes = out_ref.shape[1]
    parts = first_ref.shape[1] // lanes
    rows = out_ref.shape[0] // parts
    for index in range(parts):
        span = slice(index * lanes, (index + 1) * lanes)
        total = first_ref[:rows, span] + rows_s[:rows, span].astype(jnp.float32)
        out_ref[pl.ds(index, rows, stride=parts)] = total


def add_slots(order, first, slots, row_count):
    features = first.shape[1]
    return order.run(
        place_kernel,
        [order.flags, first, *slots],
        [SMEM] + [VMEM] * (len(slots) + 1),
        [VMEM],
        [struct((row_count * features // 128, 128), jnp.float32)],
        scratch=[pltpu.VMEM(first.shape, slots[0].dtype)],
        room=4,
    )[0]


def body(
    tokens,
    size_tag,
    cotangent,
    time_project,
    time_output,
    time_vector,
    space_project,
    space_output,
    space_vector,
    feed_inner,
    feed_bias,
    feed_outer,
    feed_vector,
):
    frame_count = lax.axis_size("frame")
    batch_count = lax.axis_size("batch")
    sizes = (batch_count, frame_count)
    frame_index = lax.axis_index("frame")
    batch_index = lax.axis_index("batch")
    flags = [(batch_index >> bit) & 1 for bit in range(batch_count.bit_length() - 1)]
    frame_flag = len(flags)
    order = Order(jnp.stack([*flags, frame_index]).astype(jnp.int32))
    features = tokens.shape[2]
    row_count = tokens.shape[1]
    part = round_up(-(-PATCHES // frame_count), ROW_TILE)
    padded = part * frame_count

    time_weight = lax.all_gather(time_project, "batch", axis=0, tiled=True)
    token_rows = jnp.pad(tokens[0], ((0, padded - row_count), (0, 0)))
    grad_result = jnp.pad(cotangent[0], ((0, padded - row_count), (0, 0)))
    slots = rows_to_frames(token_rows, frame_count, frame_index)
    vectors = jnp.concatenate(
        [time_vector, space_vector, feed_vector, feed_bias.reshape(-1, time_vector.shape[1])], axis=0
    )
    vectors = lax.all_gather(vectors, "batch", axis=0)
    vec = vectors[:, :13].transpose(1, 0, 2).reshape(13, features).astype(jnp.float32)
    vec = jnp.pad(vec, ((0, 3), (0, 0)))
    feed_bias_row = vectors[:, 13:].reshape(1, -1).astype(jnp.float32)

    def stack_columns(weight):
        return [weight[:, at : at + features] for at in range(0, weight.shape[1], features)]

    feed_packed = jnp.concatenate([*stack_columns(feed_inner), feed_outer, space_output], axis=0)
    feed_packed = lax.all_gather(feed_packed, "batch", axis=0)
    clip = jnp.concatenate(
        [
            jnp.arange(PATCHES, dtype=jnp.int32) // size_tag[0],
            jnp.arange(UNITS, dtype=jnp.int32),
            jnp.full((padded - PATCHES - UNITS,), -1, jnp.int32),
        ]
    )

    packed = jnp.concatenate([time_output, *stack_columns(space_project)], axis=0)
    weight_flight = Flight(gather_steps(packed, batch_count))
    advance(order, weight_flight)
    mixture_slots, qkv_time, prob_time, first_input = time_forward(order, slots, time_weight, vec)
    mixture_slots = send_back(mixture_slots)
    while weight_flight.result is None:
        advance(order, weight_flight, room=4)
    packed = weight_flight.result.reshape(batch_count, -1, features)
    mixture_time, after_time, second_input, qkv_space = middle_forward(
        order, token_rows, mixture_slots, packed, vec
    )
    mixture_space, total_space = space_forward(order, qkv_space, clip, features)
    (
        block_out,
        grad_second,
        grad_branch,
        grad_mixture,
        feed_grads,
        grad_feed_bias,
        feed_sums,
    ) = feed_block(
        order,
        row_count,
        after_time,
        mixture_space,
        grad_result,
        feed_packed,
        feed_bias_row,
        vec,
        chunks=2,
    )

    def sum_batch(block):
        return lax.psum_scatter(block, "batch", scatter_dimension=0, tiled=True)

    feed_part = sum_batch(feed_grads.reshape(-1, features))
    grad_query, grad_keys, grad_values = space_backward(
        order, qkv_space, mixture_space, total_space, grad_mixture, clip, features
    )
    space_pair = space_weights(
        order,
        sizes,
        second_input,
        grad_query,
        grad_keys,
        grad_values,
        mixture_space,
        grad_branch,
    )
    grad_first, space_sums, other_pair, grad_slots = middle_backward(
        order,
        sizes,
        grad_query,
        grad_keys,
        grad_values,
        after_time,
        grad_second,
        packed,
        vec,
        mixture_time,
        feed_sums,
        grad_feed_bias,
    )
    grad_slots = send_parts(grad_slots)
    core_flight = Flight(core_steps([space_pair, other_pair], batch_count))
    advance(order, core_flight, room=4)
    space_part = sum_chips(core_flight.result[0], batch_count)
    feed_flight = Flight(frame_steps(feed_part, frame_count, frame_flag))
    advance(order, feed_flight, after=grad_slots[1:], room=4)
    input_slots, time_kept, time_sent = time_backward(
        order,
        grad_slots,
        slots,
        qkv_time,
        prob_time,
        first_input,
        time_weight,
        vec,
        space_sums,
    )
    time_flight = Flight(sum_steps(time_kept, time_sent, sizes, frame_flag))
    input_slots = send_back(input_slots)
    space_flight = Flight(frame_steps(space_part, frame_count, frame_flag))
    advance(order, feed_flight, space_flight, room=4)
    whole = finish_together(order, space_flight, feed_flight)
    whole = lax.all_gather(whole, ("batch", "frame"), axis=0)
    while time_flight.result is None:
        advance(order, time_flight)
    space_part_rows = space_part.shape[0] // frame_count
    (
        grad_feed_inner,
        grad_feed_outer,
        grad_space_project,
        grad_space_output,
        grad_time_output,
    ) = deliver_parts(order, whole, space_part_rows)
    grad_time_project, time_vectors = deliver_halves(order, *time_flight.result)
    some_vectors = whole[5 * features // space_part_rows, :ROW_TILE].astype(jnp.float32)
    grad_tokens = add_slots(order, grad_first, input_slots, row_count)
    grad_tokens = grad_tokens.reshape(1, row_count, features)
    return (
        block_out,
        grad_tokens,
        grad_time_project,
        grad_time_output,
        time_vectors[0:5],
        grad_space_project,
        grad_space_output,
        some_vectors[0:5],
        grad_feed_inner,
        some_vectors[8:12].reshape(-1),
        grad_feed_outer,
        some_vectors[5:8],
    )


def solution(mesh):
    placed = (
        P("frame", "batch", None),
        P("batch"),
        P("frame", "batch", None),
        P("batch", None),
        P("batch", None),
        P(None, "batch"),
        P("batch", None),
        P("batch", None),
        P(None, "batch"),
        P("batch", None),
        P("batch"),
        P("batch", None),
        P(None, "batch"),
    )
    return jax.shard_map(
        body,
        mesh=mesh,
        in_specs=placed,
        out_specs=(
            P("frame", "batch", None),
            P("frame", "batch", None),
            P(),
            P(),
            P(),
            P(),
            P(),
            P(),
            P(),
            P(),
            P(),
            P(),
        ),
        check_vma=False,
    )
```
